128 devices in a mesh: outer: 8 (over z, y_hi), inner: 16 (over x, y_lo, core).
Axes of the slice: x: 4, y: 4 (y_hi: 2, y_lo: 2; y = y_hi * 2 + y_lo), z: 4, core: 2. Of those that a mesh axis runs over, the one named last changes fastest.
Arguments:
- queries: bfloat16 [131072, 1024], P(('outer', 'inner')), may hold values from -180 to 180
- keys: bfloat16 [131072, 1024], P(('outer', 'inner')), may hold values from -6 to 6
- values: bfloat16 [131072, 1024], P(('outer', 'inner')), may hold values from -48 to 48
- out_grad: bfloat16 [131072, 1024], P(('outer', 'inner')), may hold values from -192 to 192
- middle_head_offsets: int32 [8], replicated, may hold values from 0 to 31
- distant_head_offsets: int32 [8], replicated, may hold values from 0 to 511
Outputs:
- attended: bfloat16 [131072, 1024], P(('outer', 'inner'))
- grad_q: bfloat16 [131072, 1024], P(('outer', 'inner'))
- grad_k: bfloat16 [131072, 1024], P(('outer', 'inner'))
- grad_v: bfloat16 [131072, 1024], P(('outer', 'inner'))
The draws below stay inside these ranges and needn't reach their ends.
All inputs are finite; a program needn't handle non-finite values.
Results may differ from the reference program's by a relative error of at most 0.0075.
The reference program's roundings to bfloat16 on the way count: a program that leaves them out, or rounds other values in their place, can miss the bound.
Values may be sent and summed in bfloat16 or wider, within the bound.
No kernel may reach another device: no remote copies, remote signals or barrier semaphores. Data moves between devices by JAX's collectives and lax.ppermute only.
A program may use at most 192 MiB of HBM per device.

```python
import jax
import jax.numpy as jnp
from jax import lax

HEAD_TOTAL = 8
D = 1024
SEG1 = 512
DILATION_TWO = 32
DILATION_THREE = 512
SEQUENCE_TOKENS = 131072
SEGMENT_TWO = 16384


def shared_base(key):
    return jnp.clip(jax.random.normal(key, (SEQUENCE_TOKENS, D), jnp.float32), -6.0, 6.0)


def draw_queries(key, part):
    key = jax.random.fold_in(key, 11)
    result = jnp.clip(jax.random.normal(key, (SEQUENCE_TOKENS, D), jnp.float32), -6.0, 6.0)
    return result.astype(jnp.bfloat16)


def draw_keys(key, part):
    base = shared_base(key)
    result = base
    return result.astype(jnp.bfloat16)


def plant(entries, own_key, low, high):
    index_at = [jax.random.randint(jax.random.fold_in(own_key, axis), (), 0, length) for axis, length in enumerate(entries.shape)]
    longest = entries.shape.index(max(entries.shape))
    beside = index_at[:longest] + [(index_at[longest] + 1) % entries.shape[longest]] + index_at[longest + 1:]
    return entries.at[tuple(index_at)].set(low).at[tuple(beside)].set(high)


def levels(own_key, dims, cuts, low, high):
    level = 1.0
    for axis_at, blocks in cuts:
        steps = jax.random.uniform(jax.random.fold_in(jax.random.fold_in(own_key, 6), axis_at), (blocks,), jnp.float32, low / len(cuts), high / len(cuts))
        level = level * jnp.repeat(jnp.exp(steps), dims[axis_at] // blocks).reshape((-1,) + (1,) * (len(dims) - 1 - axis_at))
    return level


def centred(rng, shape, scale, bound, shards=(), kind=jnp.bfloat16):
    values = scale * jax.random.normal(rng, shape, jnp.float32)
    if shards:
        values = values * levels(rng, shape, shards, -0.22, 0.18)
    return jnp.clip(values, -bound, bound).astype(kind)


def setup_inputs(seed: int = 0) -> dict:
    splits = jax.random.split(jax.random.key(seed), 7)
    return {
        "queries": draw_queries(jax.random.fold_in(splits[6], 71), 0),
        "keys": draw_keys(jax.random.fold_in(splits[6], 71), 0),
        "values": centred(splits[2], (SEQUENCE_TOKENS, D), 8.0, 48.0, ((0, 128),)),
        "out_grad": centred(splits[3], (SEQUENCE_TOKENS, D), 32.0, 192.0, ((0, 128),)),
        "middle_head_offsets": plant(jax.random.randint(splits[4], (HEAD_TOTAL,), 0, DILATION_TWO), jax.random.fold_in(splits[4], 1), 0, DILATION_TWO - 1).astype(jnp.int32),
        "distant_head_offsets": plant(jax.random.randint(splits[5], (HEAD_TOTAL,), 0, DILATION_THREE), jax.random.fold_in(splits[5], 1), 0, DILATION_THREE - 1).astype(jnp.int32),
    }


def gather_rows(source, stride, offsets):
    number_of_heads = offsets.shape[0]
    shaped = source.reshape((source.shape[0] // stride, stride) + source.shape[1:])
    chosen = lax.broadcasted_iota(jnp.int32, (stride, number_of_heads), 0) == offsets[None, :]
    chosen = chosen.reshape((1, stride, number_of_heads) + (1,) * (source.ndim - 2))
    return jnp.sum(jnp.where(chosen, shaped, jnp.zeros((), source.dtype)), axis=1).astype(source.dtype)


def insert_rows(source, stride, offsets):
    number_of_heads = offsets.shape[0]
    chosen = lax.broadcasted_iota(jnp.int32, (stride, number_of_heads), 0) == offsets[None, :]
    chosen = chosen.reshape((1, stride, number_of_heads) + (1,) * (source.ndim - 2))
    spread = jnp.where(chosen, source[:, None], jnp.zeros((), source.dtype))
    return spread.reshape((source.shape[0] * stride,) + source.shape[1:])


def coverage_count(number_of_rows, stride, offsets):
    position = lax.broadcasted_iota(jnp.int32, (number_of_rows, offsets.shape[0]), 0)
    return (position % stride) == offsets[None, :]


def attend(q_part, k_part, v_part):
    factor = q_part.shape[-1] ** -0.5
    scores = jnp.einsum("gqhe,gkhe->ghqk", q_part.astype(jnp.float32), k_part.astype(jnp.float32),
                        precision=lax.Precision.HIGHEST) * factor
    highest = jnp.max(scores, axis=-1, keepdims=True)
    exponent = jnp.exp(scores - highest)
    denominator = jnp.sum(exponent, axis=-1)
    weights = exponent.astype(jnp.bfloat16)
    blended = jnp.einsum("ghqk,gkhe->gqhe", weights.astype(jnp.float32), v_part.astype(jnp.float32),
                         precision=lax.Precision.HIGHEST)
    blended = blended / jnp.transpose(denominator, (0, 2, 1))[..., None]
    log_sum = jnp.transpose(highest[..., 0] + jnp.log(denominator), (0, 2, 1))
    return blended, log_sum


def gradients(q_part, k_part, v_part, g_part, combined_logsumexp, delta_per_row):
    factor = q_part.shape[-1] ** -0.5
    q_wide = q_part.astype(jnp.float32)
    k_wide = k_part.astype(jnp.float32)
    g_wide = g_part.astype(jnp.float32)
    scores = jnp.einsum("gqhe,gkhe->ghqk", q_wide, k_wide, precision=lax.Precision.HIGHEST) * factor
    chances = jnp.exp(scores - jnp.transpose(combined_logsumexp, (0, 2, 1))[..., None])
    chance_low = chances.astype(jnp.bfloat16).astype(jnp.float32)
    grad_prob = jnp.einsum("gqhe,gkhe->ghqk", g_wide, v_part.astype(jnp.float32), precision=lax.Precision.HIGHEST)
    dscore = (chances * (grad_prob - jnp.transpose(delta_per_row, (0, 2, 1))[..., None])).astype(jnp.bfloat16)
    dscore = dscore.astype(jnp.float32)
    grad_v = jnp.einsum("ghqk,gqhe->gkhe", chance_low, g_wide, precision=lax.Precision.HIGHEST)
    grad_k = jnp.einsum("ghqk,gqhe->gkhe", dscore, q_wide, precision=lax.Precision.HIGHEST) * factor
    grad_q = jnp.einsum("ghqk,gkhe->gqhe", dscore, k_wide, precision=lax.Precision.HIGHEST) * factor
    return grad_q, grad_k, grad_v


def combine(lse_one, middle_logsumexp, middle_coverage, distant_logsumexp, distant_coverage):
    highest = jnp.maximum(lse_one, jnp.maximum(jnp.where(middle_coverage, middle_logsumexp, lse_one),
                                               jnp.where(distant_coverage, distant_logsumexp, lse_one)))
    summed = jnp.exp(lse_one - highest)
    summed = summed + jnp.where(middle_coverage, jnp.exp(jnp.where(middle_coverage, middle_logsumexp - highest, 0.0)), 0.0)
    summed = summed + jnp.where(distant_coverage, jnp.exp(jnp.where(distant_coverage, distant_logsumexp - highest, 0.0)), 0.0)
    return highest + jnp.log(summed)


def share(log_sum, cover, combined_logsumexp):
    return jnp.where(cover, jnp.exp(jnp.where(cover, log_sum - combined_logsumexp, 0.0)), 0.0)


def forward_group(parts):
    return attend(parts[0], parts[1], parts[2])


def backward_group(parts):
    return gradients(parts[0], parts[1], parts[2], parts[3], parts[4], parts[5])


def reference(queries, keys, values, out_grad, middle_head_offsets, distant_head_offsets):
    number_of_heads = middle_head_offsets.shape[0]
    per_head_width = queries.shape[1] // number_of_heads
    split_shape = (SEQUENCE_TOKENS, number_of_heads, per_head_width)
    query_sections = queries.reshape(split_shape)
    key_sections = keys.reshape(split_shape)
    value_sections = values.reshape(split_shape)
    gradient_sections = out_grad.reshape(split_shape)
    group_count = SEQUENCE_TOKENS // (8 * SEG1)
    group_shape = (group_count, 8, SEG1, number_of_heads, per_head_width)
    stat_shape = (group_count, 8, SEG1, number_of_heads)
    out_one, lse_one = lax.map(forward_group, (query_sections.reshape(group_shape), key_sections.reshape(group_shape),
                                               value_sections.reshape(group_shape)))
    out_one = out_one.reshape(split_shape)
    lse_one = lse_one.reshape(SEQUENCE_TOKENS, number_of_heads)

    middle_layout = (SEQUENCE_TOKENS // SEGMENT_TWO, SEGMENT_TWO // DILATION_TWO, number_of_heads, per_head_width)
    distant_layout = (1, SEQUENCE_TOKENS // DILATION_THREE, number_of_heads, per_head_width)
    middle_query_rows = gather_rows(query_sections, DILATION_TWO, middle_head_offsets).reshape(middle_layout)
    middle_key_rows = gather_rows(key_sections, DILATION_TWO, middle_head_offsets).reshape(middle_layout)
    middle_value_rows = gather_rows(value_sections, DILATION_TWO, middle_head_offsets).reshape(middle_layout)
    distant_query_rows = gather_rows(query_sections, DILATION_THREE, distant_head_offsets).reshape(distant_layout)
    distant_key_rows = gather_rows(key_sections, DILATION_THREE, distant_head_offsets).reshape(distant_layout)
    distant_value_rows = gather_rows(value_sections, DILATION_THREE, distant_head_offsets).reshape(distant_layout)
    middle_output, middle_logsumexp = attend(middle_query_rows, middle_key_rows, middle_value_rows)
    distant_output, distant_logsumexp = attend(distant_query_rows, distant_key_rows, distant_value_rows)
    middle_rows = SEQUENCE_TOKENS // DILATION_TWO
    distant_rows = SEQUENCE_TOKENS // DILATION_THREE
    middle_output_full = insert_rows(middle_output.reshape(middle_rows, number_of_heads, per_head_width), DILATION_TWO, middle_head_offsets)
    middle_logsumexp_full = insert_rows(middle_logsumexp.reshape(middle_rows, number_of_heads), DILATION_TWO, middle_head_offsets)
    distant_output_full = insert_rows(distant_output.reshape(distant_rows, number_of_heads, per_head_width), DILATION_THREE, distant_head_offsets)
    distant_logsumexp_full = insert_rows(distant_logsumexp.reshape(distant_rows, number_of_heads), DILATION_THREE, distant_head_offsets)
    cover_one = coverage_count(SEQUENCE_TOKENS, 1, jnp.zeros((number_of_heads,), jnp.int32))
    middle_coverage = coverage_count(SEQUENCE_TOKENS, DILATION_TWO, middle_head_offsets)
    distant_coverage = coverage_count(SEQUENCE_TOKENS, DILATION_THREE, distant_head_offsets)
    combined_logsumexp = combine(lse_one, middle_logsumexp_full, middle_coverage, distant_logsumexp_full, distant_coverage)
    blended = share(lse_one, cover_one, combined_logsumexp)[..., None] * out_one
    blended = blended + share(middle_logsumexp_full, middle_coverage, combined_logsumexp)[..., None] * middle_output_full
    blended = blended + share(distant_logsumexp_full, distant_coverage, combined_logsumexp)[..., None] * distant_output_full
    attended = blended.astype(jnp.bfloat16)
    delta_per_row = jnp.sum(gradient_sections.astype(jnp.float32) * attended.astype(jnp.float32), axis=-1)

    dq_one, dk_one, dv_one = lax.map(backward_group, (
        query_sections.reshape(group_shape), key_sections.reshape(group_shape), value_sections.reshape(group_shape),
        gradient_sections.reshape(group_shape), combined_logsumexp.reshape(stat_shape), delta_per_row.reshape(stat_shape)))
    middle_output_gradient = gather_rows(gradient_sections, DILATION_TWO, middle_head_offsets).reshape(middle_layout)
    distant_output_gradient = gather_rows(gradient_sections, DILATION_THREE, distant_head_offsets).reshape(distant_layout)
    middle_total = gather_rows(combined_logsumexp, DILATION_TWO, middle_head_offsets).reshape(middle_layout[:3])
    middle_delta = gather_rows(delta_per_row, DILATION_TWO, middle_head_offsets).reshape(middle_layout[:3])
    distant_total = gather_rows(combined_logsumexp, DILATION_THREE, distant_head_offsets).reshape(distant_layout[:3])
    distant_delta = gather_rows(delta_per_row, DILATION_THREE, distant_head_offsets).reshape(distant_layout[:3])
    dq_mid, dk_mid, dv_mid = gradients(middle_query_rows, middle_key_rows, middle_value_rows, middle_output_gradient, middle_total, middle_delta)
    dq_far, dk_far, dv_far = gradients(distant_query_rows, distant_key_rows, distant_value_rows, distant_output_gradient, distant_total, distant_delta)

    def merge_three(one_part, middle_portion, distant_portion):
        complete_sequence = one_part.reshape(split_shape)
        complete_sequence = complete_sequence + insert_rows(middle_portion.reshape(middle_rows, number_of_heads, per_head_width), DILATION_TWO, middle_head_offsets)
        complete_sequence = complete_sequence + insert_rows(distant_portion.reshape(distant_rows, number_of_heads, per_head_width), DILATION_THREE, distant_head_offsets)
        return complete_sequence.astype(jnp.bfloat16).reshape(SEQUENCE_TOKENS, number_of_heads * per_head_width)

    return (attended.reshape(SEQUENCE_TOKENS, number_of_heads * per_head_width), merge_three(dq_one, dq_mid, dq_far),
            merge_three(dk_one, dk_mid, dk_far), merge_three(dv_one, dv_mid, dv_far))
```

```python
import math

import jax
import jax.numpy as jnp
from jax import lax
from jax.experimental import pallas as pl
from jax.experimental.pallas import tpu as pltpu
from jax.sharding import PartitionSpec as P

SEG1 = 512
DILATION_TWO = 32
DILATION_THREE = 512
HEADS = 8
WIDTH = 128
FACTOR = WIDTH ** (-0.5)
MID = SEG1 // DILATION_TWO
COV = 32
PACK = 128
KEPT = 7
EXTRACT_HEADS = 2
FINISH_HEADS = 2
VMEM = 60 * 2**20
NEG = -1e30
F32 = jnp.float32
BF16 = jnp.bfloat16


def dot_nn(a, b):
    return lax.dot_general(a, b, (((1,), (0,)), ((), ())), preferred_element_type=F32)


def dot_nt(a, b):
    return lax.dot_general(a, b, (((1,), (1,)), ((), ())), preferred_element_type=F32)


def dot_tn(a, b):
    return lax.dot_general(a, b, (((0,), (0,)), ((), ())), preferred_element_type=F32)


def iota(shape, dim):
    return lax.broadcasted_iota(jnp.int32, shape, dim)


def split3(x):
    high = x.astype(BF16).astype(F32)
    rest = x - high
    middle = rest.astype(BF16).astype(F32)
    return high, middle, (rest - middle).astype(BF16).astype(F32)


def lanes(columns, rows):
    lane = iota((rows, WIDTH), 1)
    out = jnp.zeros((rows, WIDTH), F32)
    for j, column in enumerate(columns):
        out = jnp.where(lane == j, column, out)
    return out


def join3(x, at):
    return x[:, at : at + 1] + x[:, at + 1 : at + 2] + x[:, at + 2 : at + 3]


def targets(shape, dim, off_two, off_three):
    j = iota(shape, dim)
    return jnp.where(j < MID, DILATION_TWO * j + off_two, jnp.where(j == MID, off_three, -1))


def far_rows_kernel(off3_ref, k_ref, v_ref, out_ref, slab, sems):
    copies = []
    for head in range(HEADS):
        start = pl.multiple_of((off3_ref[head] // 16) * 16, 16)
        for j in range(4):
            source = (k_ref, v_ref)[j // 2]
            copies.append(
                pltpu.make_async_copy(
                    source.at[pl.ds((j % 2) * SEG1 + start, 16), pl.ds(head * WIDTH, WIDTH)],
                    slab.at[4 * head + j],
                    sems.at[4 * head + j],
                )
            )
    for copy in copies:
        copy.start()
    for copy in copies:
        copy.wait()
    picked = []
    for head in range(HEADS):
        inside = iota((16, 1), 0) == off3_ref[head] % 16
        for j in range(4):
            picked.append(
                jnp.sum(jnp.where(inside, slab[4 * head + j].astype(F32), 0.0), axis=0, keepdims=True)
            )
    rows = jnp.concatenate(picked, 0).astype(BF16)
    for o in range(out_ref.shape[0]):
        out_ref[o] = rows


def far_rows(off3, k, v, copies):
    return pl.pallas_call(
        far_rows_kernel,
        in_specs=[pl.BlockSpec(memory_space=pltpu.SMEM)] + [pl.BlockSpec(memory_space=pl.ANY)] * 2,
        out_specs=pl.BlockSpec(memory_space=pltpu.VMEM),
        out_shape=jax.ShapeDtypeStruct((copies, 4 * HEADS, WIDTH), BF16),
        scratch_shapes=[
            pltpu.VMEM((4 * HEADS, 16, WIDTH), BF16),
            pltpu.SemaphoreType.DMA((4 * HEADS,)),
        ],
        compiler_params=pltpu.CompilerParams(vmem_limit_bytes=VMEM),
        cost_estimate=pl.CostEstimate(flops=2**18, bytes_accessed=2**18, transcendentals=0),
        name="far_rows",
    )(off3, k, v)


def extract_kernel(
    off2_ref, off3_ref, q_ref, k_ref, v_ref, g_ref, send_ref, cov_ref, left_ref
):
    cells = [(i, t) for i in range(EXTRACT_HEADS) for t in range(2)]

    def block(ref, cell):
        i, t = cell
        return ref[t * SEG1 : (t + 1) * SEG1, i * WIDTH : (i + 1) * WIDTH]

    selects, valids = [], []
    row = iota((COV, 1), 0)
    for i in range(EXTRACT_HEADS):
        head = pl.program_id(0) * EXTRACT_HEADS + i
        off_two, off_three = off2_ref[head], off3_ref[head]
        position = targets((COV, 1), 0, off_two, off_three)
        selects.append((iota((COV, SEG1), 1) == position).astype(BF16))
        twice = (off_three % DILATION_TWO) == off_two
        valids.append(((row < MID) | ((row == MID) & jnp.logical_not(twice))).astype(F32))
    picked = [
        dot_nn(selects[cell[0]], jnp.concatenate([block(r, cell) for r in (q_ref, k_ref, v_ref, g_ref)], 1))
        for cell in cells
    ]
    low = [x.astype(BF16) for x in picked]
    scores = [dot_nt(x[:, :WIDTH], block(k_ref, cell)) for x, cell in zip(low, cells)]
    grads = [dot_nt(x[:, 3 * WIDTH :], block(v_ref, cell)) for x, cell in zip(low, cells)]
    scores, grads = jnp.concatenate(scores, 0) * FACTOR, jnp.concatenate(grads, 0)
    top = jnp.max(scores, axis=1, keepdims=True)
    weight = jnp.exp(scores - top)
    total = jnp.sum(weight, axis=1, keepdims=True)
    weight_low = weight.astype(BF16)
    out = jnp.concatenate(
        [dot_nn(weight_low[n * COV : (n + 1) * COV], block(v_ref, cell)) for n, cell in enumerate(cells)], 0
    ) / total
    lse = top + jnp.log(total)
    g_cov = jnp.concatenate([x[:, 3 * WIDTH :] for x in picked], 0)
    delta = jnp.sum(g_cov * out, axis=1, keepdims=True)
    stats = lanes(split3(lse) + split3(delta), COV * len(cells))
    prob = weight * (jnp.concatenate([valids[i] for i, _ in cells], 0) / total)
    dscore = (prob * (grads - delta)).astype(BF16)
    prob = prob.astype(BF16)
    first = iota((MID, 1), 0) == 0
    shape = (COV, WIDTH)
    for n, (i, t) in enumerate(cells):
        rows = slice(n * COV, (n + 1) * COV)
        own = stats[rows]
        far_block = (
            picked[n][MID:, :WIDTH] + pltpu.roll(picked[n][MID:, 3 * WIDTH :], 1, 0)
            + pltpu.roll(jnp.where(first, own[MID:], 0.0), 2, 0)
        )
        for c in range(2):
            send_ref[2 * i + c, t * MID : (t + 1) * MID, :] = low[n][:MID, WIDTH : 2 * WIDTH]
            send_ref[2 * i + c, 2 * MID + t * MID : 2 * MID + (t + 1) * MID, :] = low[n][:MID, 2 * WIDTH : 3 * WIDTH]
        send_ref[2 * i + t, 4 * MID : 5 * MID, :] = low[n][:MID, :WIDTH]
        send_ref[2 * i + t, 5 * MID : 6 * MID, :] = low[n][:MID, 3 * WIDTH :]
        send_ref[2 * i + t, 6 * MID : 7 * MID, :] = own[:MID].astype(BF16)
        send_ref[2 * i + t, 7 * MID : 8 * MID, :] = far_block.astype(BF16)
        kept = (
            picked[n][:, :WIDTH], picked[n][:, 3 * WIDTH :], out[rows],
            jnp.broadcast_to(lse[rows], shape), jnp.broadcast_to(delta[rows], shape),
        )
        for at, x in enumerate(kept):
            cov_ref[at, i, t] = x
        keys = block(k_ref, (i, t))
        both = dot_nn(jnp.concatenate([dscore[rows], prob[rows]], 0), keys)
        cov_ref[5, i, t] = both[:COV]
        cov_ref[6, i, t] = both[COV:]
        chosen = selects[i] * valids[i].astype(BF16)
        left_ref[i, t] = jnp.concatenate([dscore[rows], prob[rows], chosen, chosen], 0).T


def extract(offsets, q, k, v, g, pack):
    n = EXTRACT_HEADS
    column = pl.BlockSpec((2 * SEG1, n * WIDTH), lambda h, *_: (0, h))
    return pl.pallas_call(
        extract_kernel,
        grid_spec=pltpu.PrefetchScalarGridSpec(
            num_scalar_prefetch=2,
            grid=(HEADS // n,),
            in_specs=[column] * 4,
            out_specs=[
                pl.BlockSpec((2 * n, PACK, WIDTH), lambda h, *_: (h, 0, 0)),
                pl.BlockSpec((KEPT, n, 2, COV, WIDTH), lambda h, *_: (0, h, 0, 0, 0)),
                pl.BlockSpec((n, 2, SEG1, 4 * COV), lambda h, *_: (h, 0, 0, 0)),
            ],
        ),
        out_shape=[
            jax.ShapeDtypeStruct((2 * HEADS, pack, WIDTH), BF16),
            jax.ShapeDtypeStruct((KEPT, HEADS, 2, COV, WIDTH), F32),
            jax.ShapeDtypeStruct((HEADS, 2, SEG1, 4 * COV), BF16),
        ],
        compiler_params=pltpu.CompilerParams(vmem_limit_bytes=VMEM),
        cost_estimate=pl.CostEstimate(flops=2**32, bytes_accessed=12 * 2**20, transcendentals=2**18),
        name="extract",
    )(*offsets, q, k, v, g)


def local_kernel(first, off2_ref, off3_ref, q_ref, k_ref, v_ref, g_ref, *rest):
    att_ref, dq_ref, dk_ref, dv_ref = rest[-4:]
    head = pl.program_id(0) + first
    position = iota((1, SEG1), 1)
    covered = ((position & (DILATION_TWO - 1)) == off2_ref[head]) | (position == off3_ref[head])
    for t in range(2):
        rows = slice(t * SEG1, (t + 1) * SEG1)
        q, k, v, g = (ref[rows, :] for ref in (q_ref, k_ref, v_ref, g_ref))
        scores = dot_nt(k, q) * (FACTOR * math.log2(math.e))
        grad = dot_nt(v, g)
        weight = jnp.exp2(scores - jnp.max(scores, axis=0, keepdims=True))
        inverse = 1.0 / jnp.sum(weight, axis=0, keepdims=True)
        att = (dot_nn(v.T, weight.astype(BF16)) * inverse).astype(BF16).astype(F32)
        delta = jnp.sum(g.T.astype(F32) * att, axis=0, keepdims=True)
        att_ref[rows, :] = jnp.where(covered, 0.0, att).astype(BF16).T
        prob = weight * jnp.where(covered, 0.0, inverse)
        dscore = (prob * (grad - delta)).astype(BF16)
        dq_ref[rows, :] = (dot_nn(k.T, dscore) * FACTOR).astype(BF16).T
        dk_ref[rows, :] = dot_nn(dscore, q)
        dv_ref[rows, :] = dot_nn(prob.astype(BF16), g)


def local(offsets, q, k, v, g, first, count, earlier):
    block = pl.BlockSpec((2 * SEG1, WIDTH), lambda h, *_: (0, h + first))
    kept = [pl.BlockSpec(memory_space=pl.ANY)] * len(earlier)
    share = count / HEADS
    return pl.pallas_call(
        lambda *refs: local_kernel(first, *refs),
        grid_spec=pltpu.PrefetchScalarGridSpec(
            num_scalar_prefetch=2,
            grid=(count,),
            in_specs=[block] * 4 + kept,
            out_specs=[block] * 4,
        ),
        out_shape=[jax.ShapeDtypeStruct(q.shape, d) for d in (BF16, BF16, F32, F32)],
        input_output_aliases={6 + i: i for i in range(len(earlier))},
        compiler_params=pltpu.CompilerParams(vmem_limit_bytes=VMEM),
        cost_estimate=pl.CostEstimate(
            flops=int(share * 12 * 2**30), bytes_accessed=int(share * 20 * 2**20), transcendentals=int(share * 2**22)
        ),
        name="local",
    )(*offsets, q, k, v, g, *earlier)


def merge_lse(parts):
    top = parts[0]
    for part in parts[1:]:
        top = jnp.maximum(top, part)
    total = jnp.exp(parts[0] - top)
    for part in parts[1:]:
        total = total + jnp.exp(part - top)
    return top + jnp.log(total)


def remote_kernel(off2_ref, off3_ref, in_ref, out_ref, far_out_ref):
    head = lax.axis_index("inner") // 2
    off_two, off_three = off2_ref[head], off3_ref[head]
    double = (off_three % DILATION_TWO) == off_two
    place = off_three // DILATION_TWO
    n = in_ref.shape[0]
    queries = n * MID

    def part(at, rows):
        return in_ref[:, at * MID : at * MID + rows, :].reshape(n * rows, WIDTH)

    k, v = part(0, 2 * MID), part(2, 2 * MID)
    q, g = part(4, MID), part(5, MID)
    stats = part(6, MID).astype(F32)
    packed = part(7, MID)
    row = iota((3 * n, queries), 0)
    pick = (iota((3 * n, queries), 1) == MID * (row % n) + row // n).astype(BF16)
    picked = dot_nn(pick, packed)
    qf, gf = picked[:n].astype(BF16), picked[n : 2 * n].astype(BF16)
    turn = (iota((8, WIDTH), 0) == iota((8, WIDTH), 1)).astype(BF16)
    figures = dot_nt(turn, picked[2 * n :].astype(BF16))
    lse1_far = figures[0:1] + figures[1:2] + figures[2:3]
    delta1_far = figures[3:4] + figures[4:5] + figures[5:6]
    scores = dot_nt(q, k) * FACTOR
    top = jnp.max(scores, axis=1, keepdims=True)
    weight = jnp.exp(scores - top)
    total = jnp.sum(weight, axis=1, keepdims=True)
    out = dot_nn(weight.astype(BF16), v) / total
    lse2 = top + jnp.log(total)
    delta2 = jnp.sum(g.astype(F32) * out, axis=1, keepdims=True)
    far = part(8, in_ref.shape[1] - PACK)
    held = far.shape[0]
    is_key = (iota((held, n), 0) & 3) < 2
    scores_far = jnp.where(is_key, dot_nt(far, qf) * FACTOR, NEG)
    top_far = jnp.max(scores_far, axis=0, keepdims=True)
    weight_far = jnp.where(is_key, jnp.exp(scores_far - top_far), 0.0)
    total_far = jnp.sum(weight_far, axis=0, keepdims=True)
    lse3 = top_far + jnp.log(total_far)
    share_far = weight_far / total_far
    out_far = dot_tn(pltpu.roll(share_far, 2, 0).astype(BF16), far)
    grad_far = pltpu.roll(dot_nt(far, gf), held - 2, 0)
    delta3 = jnp.sum(share_far * grad_far, axis=0, keepdims=True)
    same = (iota((queries, n), 0) == MID * iota((queries, n), 1) + place) & double
    lse3_mid = jnp.max(jnp.where(same, lse3, NEG), axis=1, keepdims=True)
    delta3_mid = jnp.sum(jnp.where(same, delta3, 0.0), axis=1, keepdims=True)
    lse2_far = jnp.max(jnp.where(same, lse2, NEG), axis=0, keepdims=True)
    delta2_far = jnp.sum(jnp.where(same, delta2, 0.0), axis=0, keepdims=True)
    lse1, delta1 = join3(stats, 0), join3(stats, 3)
    lse = merge_lse([lse1, lse2, lse3_mid])
    delta = (
        jnp.exp(lse1 - lse) * delta1 + jnp.exp(lse2 - lse) * delta2 + jnp.exp(lse3_mid - lse) * delta3_mid
    )
    lse_far = merge_lse([lse1_far, lse3, lse2_far])
    delta_far = (
        jnp.exp(lse1_far - lse_far) * delta1_far + jnp.exp(lse3 - lse_far) * delta3
        + jnp.exp(lse2_far - lse_far) * delta2_far
    )
    prob = jnp.exp(scores - lse)
    dscore = (prob * (dot_nt(g, v) - delta)).astype(BF16)
    dq = dot_nn(dscore, k)
    dk = dot_tn(dscore, q)
    dv = dot_tn(prob.astype(BF16), g)
    prob_far = jnp.where(is_key, jnp.exp(scores_far - lse_far), 0.0)
    dscore_far = (prob_far * (grad_far - delta_far)).astype(BF16)
    dq_far = dot_tn(dscore_far, far)
    far_out_ref[...] = (
        dot_nn(pltpu.roll(prob_far, 2, 0).astype(BF16), gf) + dot_nn(dscore_far, qf)
    ).astype(BF16)
    high, middle, low = split3(lse3)
    eight = iota((8, n), 0)
    figures = jnp.where(eight == 0, high, jnp.where(eight == 1, middle, jnp.where(eight == 2, low, 0.0)))
    stats_far = dot_tn(figures.astype(BF16), turn)
    unpick = (iota((queries, 3 * n), 0) == MID * (iota((queries, 3 * n), 1) % n) + iota((queries, 3 * n), 1) // n)
    packed = dot_nn(
        unpick.astype(BF16), jnp.concatenate([dq_far, out_far, stats_far], 0).astype(BF16)
    )

    def give(at, rows, value):
        out_ref[:, at * MID : at * MID + rows, :] = value.astype(BF16).reshape(n, rows, WIDTH)

    give(0, 2 * MID, dk)
    give(2, 2 * MID, dv)
    give(4, MID, dq)
    give(5, MID, out)
    give(6, MID, lanes(split3(lse2), queries))
    give(7, MID, packed)


def remote(offsets, received):
    vmem = pl.BlockSpec(memory_space=pltpu.VMEM)
    smem = pl.BlockSpec(memory_space=pltpu.SMEM)
    n, pack, _ = received.shape
    return pl.pallas_call(
        remote_kernel,
        in_specs=[smem, smem, vmem],
        out_specs=[vmem, vmem],
        out_shape=[
            jax.ShapeDtypeStruct((n, PACK, WIDTH), BF16),
            jax.ShapeDtypeStruct((n * (pack - PACK), WIDTH), BF16),
        ],
        compiler_params=pltpu.CompilerParams(vmem_limit_bytes=VMEM),
        cost_estimate=pl.CostEstimate(flops=2**31, bytes_accessed=2**21, transcendentals=2**19),
        name="remote",
    )(*offsets, received)


def prepare(off2_ref, off3_ref, cov_ref, back_ref, far_ref, right_ref):
    cells, rows = 2 * HEADS, 2 * HEADS * COV
    back = back_ref[...].astype(F32)

    def pad(x):
        return jnp.concatenate([x, jnp.zeros((cells, COV - MID, WIDTH), F32)], 1).reshape(rows, WIDTH)

    def own(at):
        return pad(back[:, at * MID : (at + 1) * MID])

    def both(at):
        x = back[:, at * MID : (at + 2) * MID].reshape(HEADS, 2, COV, WIDTH)
        return pad((x[:, 0] + x[:, 1]).reshape(cells, MID, WIDTH))

    def spread(x):
        return jnp.broadcast_to(x.reshape(cells, 1, WIDTH), (cells, COV, WIDTH)).reshape(rows, WIDTH)

    row = iota((COV, WIDTH), 0)
    is_far = []
    for head in range(HEADS):
        off_three = off3_ref[head]
        twice = (off_three % DILATION_TWO) == off2_ref[head]
        is_far += [(row == jnp.where(twice, off_three // DILATION_TWO, MID)).astype(F32)] * 2
    is_far = jnp.concatenate(is_far, 0) > 0.0
    is_mid = jnp.concatenate([row] * cells, 0) < MID
    ones = (iota((WIDTH, WIDTH), 0) < 3).astype(BF16)

    def joined(x):
        return dot_nn(x.astype(BF16), ones)

    q, g, out, lse1, delta1, dq_one, dq_two = (cov_ref[at].reshape(rows, WIDTH) for at in range(KEPT))
    packed = back[:, 7 * MID : 8 * MID]
    far = far_ref[...].astype(F32)
    far = (far[:, :4] + far[:, 4:]).reshape(HEADS, 2, 2, WIDTH)
    lse2 = jnp.where(is_mid, joined(own(6)), NEG)
    lse3 = jnp.where(is_far, joined(spread(packed[:, 2:3])), NEG)
    lse = merge_lse([lse1, lse2, lse3])
    share = jnp.exp(lse1 - lse)
    att = (
        share * out + jnp.exp(lse2 - lse) * own(5) + jnp.exp(lse3 - lse) * spread(packed[:, 1:2])
    ).astype(BF16)
    delta = jnp.sum(g * att.astype(F32), axis=1, keepdims=True)
    change = share * (delta - delta1)
    dq = share * dq_one - change * dq_two + own(4) + jnp.where(is_far, spread(packed[:, 0:1]), 0.0)
    dk = both(0) + jnp.where(is_far, spread(far[:, 0]), 0.0)
    dv = both(2) + jnp.where(is_far, spread(far[:, 1]), 0.0)

    def put(at, column, x):
        right_ref[:, at * COV : (at + 1) * COV, column * WIDTH : (column + 1) * WIDTH] = x.astype(BF16).reshape(
            cells, COV, WIDTH
        )

    def put_two(column, x):
        high = x.astype(BF16)
        put(2, column, high)
        put(3, column, x - high.astype(F32))

    right_ref[:, : 2 * COV, : 2 * WIDTH] = jnp.zeros((cells, 2 * COV, 2 * WIDTH), BF16)
    right_ref[:, :COV, 3 * WIDTH :] = jnp.zeros((cells, COV, WIDTH), BF16)
    right_ref[:, 3 * COV :, :WIDTH] = jnp.zeros((cells, COV, WIDTH), BF16)
    put(2, 0, att)
    put_two(1, dq)
    put(0, 2, share * q)
    put(1, 2, -change * q)
    put_two(2, dk)
    put(1, 3, share * g)
    put_two(3, dv)


def finish_kernel(
    off2_ref, off3_ref, cov_ref, back_ref, far_ref, left_ref,
    att_ref, dq_ref, dk_ref, dv_ref, att_out, dq_out, dk_out, dv_out, right_ref,
):
    head, t = pl.program_id(0) * FINISH_HEADS, pl.program_id(1)

    @pl.when((pl.program_id(0) == 0) & (t == 0))
    def _():
        prepare(off2_ref, off3_ref, cov_ref, back_ref, far_ref, right_ref)

    for i in range(FINISH_HEADS):
        c = slice(i * WIDTH, (i + 1) * WIDTH)
        x = dot_nn(left_ref[i, 0], right_ref[2 * (head + i) + t])
        att_out[:, c] = (att_ref[:, c].astype(F32) + x[:, :WIDTH]).astype(BF16)
        dq_out[:, c] = (dq_ref[:, c].astype(F32) + FACTOR * x[:, WIDTH : 2 * WIDTH]).astype(BF16)
        dk_out[:, c] = (FACTOR * (dk_ref[:, c] + x[:, 2 * WIDTH : 3 * WIDTH])).astype(BF16)
        dv_out[:, c] = (dv_ref[:, c] + x[:, 3 * WIDTH :]).astype(BF16)


def finish(offsets, cov, left, back, far, local_parts):
    n = FINISH_HEADS
    block = pl.BlockSpec((SEG1, n * WIDTH), lambda h, t, *_: (t, h))
    whole = [pl.BlockSpec(x.shape, lambda *_, r=x.ndim: (0,) * r, pipeline_mode=pl.Buffered(1)) for x in (cov, back, far)]
    return pl.pallas_call(
        finish_kernel,
        grid_spec=pltpu.PrefetchScalarGridSpec(
            num_scalar_prefetch=2,
            grid=(HEADS // n, 2),
            in_specs=whole
            + [pl.BlockSpec((n, 1, SEG1, 4 * COV), lambda h, t, *_: (h, t, 0, 0))]
            + [block] * 4,
            out_specs=[block] * 4,
            scratch_shapes=[pltpu.VMEM((2 * HEADS, 4 * COV, 4 * WIDTH), BF16)],
        ),
        out_shape=[jax.ShapeDtypeStruct(x.shape, BF16) for x in local_parts],
        compiler_params=pltpu.CompilerParams(vmem_limit_bytes=VMEM),
        cost_estimate=pl.CostEstimate(flops=2**30, bytes_accessed=28 * 2**20, transcendentals=2**18),
        name="finish",
    )(*offsets, cov, back, far, left, *local_parts)


def solution(mesh):
    outer, inner = mesh.shape["outer"], mesh.shape["inner"]
    split = P(("outer", "inner"), None)

    def body(queries, keys, values, out_grad, middle_head_offsets, distant_head_offsets):
        offsets = (middle_head_offsets, distant_head_offsets)
        arrays = (queries, keys, values, out_grad)
        far = far_rows(distant_head_offsets, keys, values, outer)
        far, *arrays = lax.optimization_barrier((far, *arrays))
        far = lax.all_to_all(far, "outer", 0, 0)
        send, cov, left = extract(offsets, *arrays, PACK + 4 * outer)
        far, send = lax.optimization_barrier((far, send))
        far = far.reshape(outer, HEADS, 4, WIDTH).transpose(1, 0, 2, 3).reshape(HEADS, 1, 4 * outer, WIDTH)
        far = jnp.broadcast_to(far, (HEADS, 2, 4 * outer, WIDTH)).reshape(inner, 4 * outer, WIDTH)
        send = lax.dynamic_update_slice(send, far, (0, PACK, 0))
        got = lax.all_to_all(send, "inner", 0, 0)
        parts = local(offsets, *arrays, 0, 4, ())
        got, *parts = lax.optimization_barrier((got, *parts))
        back, far = remote(offsets, got)
        back, far, *parts = lax.optimization_barrier((back, far, *parts))
        back = lax.all_to_all(back, "inner", 0, 0)
        far = far.reshape(inner, outer, 4, WIDTH).transpose(1, 0, 2, 3)
        far = lax.all_to_all(far.reshape(outer, inner * 4, WIDTH), "outer", 0, 0)
        parts = local(offsets, *arrays, 4, 2, parts)
        far, *parts = lax.optimization_barrier((far, *parts))
        far = jnp.sum(far.astype(F32), axis=0).astype(BF16).reshape(inner, 4, WIDTH)
        far = lax.all_to_all(far, "inner", 0, 0).reshape(HEADS, 8, WIDTH)
        parts = local(offsets, *arrays, 6, 2, parts)
        back, far, *parts = lax.optimization_barrier((back, far, *parts))
        return finish(offsets, cov, left, back, far, parts)

    return jax.shard_map(
        body, mesh=mesh, in_specs=(split,) * 4 + (P(), P()), out_specs=(split,) * 4, check_vma=False
    )
```

```python
import math

import jax
import jax.numpy as jnp
from jax import lax
from jax.experimental import pallas as pl
from jax.experimental.pallas import tpu as pltpu
from jax.sharding import PartitionSpec as P

SEG1 = 512
DILATION_TWO = 32
DILATION_THREE = 512
HEADS = 8
WIDTH = 128
FACTOR = WIDTH ** (-0.5)
MID = SEG1 // DILATION_TWO
COV = 32
PACK = 128
KEPT = 7
EXTRACT_HEADS = 2
FINISH_HEADS = 4
VMEM = 60 * 2**20
NEG = -1e30
F32 = jnp.float32
BF16 = jnp.bfloat16


def dot_nn(a, b):
    return lax.dot_general(a, b, (((1,), (0,)), ((), ())), preferred_element_type=F32)


def dot_nt(a, b):
    return lax.dot_general(a, b, (((1,), (1,)), ((), ())), preferred_element_type=F32)


def dot_tn(a, b):
    return lax.dot_general(a, b, (((0,), (0,)), ((), ())), preferred_element_type=F32)


def iota(shape, dim):
    return lax.broadcasted_iota(jnp.int32, shape, dim)


def split3(x):
    high = x.astype(BF16).astype(F32)
    rest = x - high
    middle = rest.astype(BF16).astype(F32)
    return high, middle, (rest - middle).astype(BF16).astype(F32)


def lanes(columns, rows):
    lane = iota((rows, WIDTH), 1)
    out = jnp.zeros((rows, WIDTH), F32)
    for j, column in enumerate(columns):
        out = jnp.where(lane == j, column, out)
    return out


def join3(x, at):
    return x[:, at : at + 1] + x[:, at + 1 : at + 2] + x[:, at + 2 : at + 3]


def targets(shape, dim, off_two, off_three):
    j = iota(shape, dim)
    return jnp.where(j < MID, DILATION_TWO * j + off_two, jnp.where(j == MID, off_three, -1))


def extract_kernel(
    off2_ref, off3_ref, q_ref, k_ref, v_ref, g_ref, send_ref, cov_ref, left_ref
):
    cells = [(i, t) for i in range(EXTRACT_HEADS) for t in range(2)]

    def block(ref, cell):
        i, t = cell
        return ref[t * SEG1 : (t + 1) * SEG1, i * WIDTH : (i + 1) * WIDTH]

    selects, valids = [], []
    row = iota((COV, 1), 0)
    for i in range(EXTRACT_HEADS):
        head = pl.program_id(0) * EXTRACT_HEADS + i
        off_two, off_three = off2_ref[head], off3_ref[head]
        position = targets((COV, 1), 0, off_two, off_three)
        selects.append((iota((COV, SEG1), 1) == position).astype(BF16))
        twice = (off_three % DILATION_TWO) == off_two
        valids.append(((row < MID) | ((row == MID) & jnp.logical_not(twice))).astype(F32))
    picked = [
        dot_nn(selects[cell[0]], jnp.concatenate([block(r, cell) for r in (q_ref, k_ref, v_ref, g_ref)], 1))
        for cell in cells
    ]
    low = [x.astype(BF16) for x in picked]
    scores = [dot_nt(x[:, :WIDTH], block(k_ref, cell)) for x, cell in zip(low, cells)]
    grads = [dot_nt(x[:, 3 * WIDTH :], block(v_ref, cell)) for x, cell in zip(low, cells)]
    scores, grads = jnp.concatenate(scores, 0) * FACTOR, jnp.concatenate(grads, 0)
    top = jnp.max(scores, axis=1, keepdims=True)
    weight = jnp.exp(scores - top)
    total = jnp.sum(weight, axis=1, keepdims=True)
    weight_low = weight.astype(BF16)
    out = jnp.concatenate(
        [dot_nn(weight_low[n * COV : (n + 1) * COV], block(v_ref, cell)) for n, cell in enumerate(cells)], 0
    ) / total
    lse = top + jnp.log(total)
    g_cov = jnp.concatenate([x[:, 3 * WIDTH :] for x in picked], 0)
    delta = jnp.sum(g_cov * out, axis=1, keepdims=True)
    stats = lanes(split3(lse) + split3(delta), COV * len(cells))
    prob = weight * (jnp.concatenate([valids[i] for i, _ in cells], 0) / total)
    dscore = (prob * (grads - delta)).astype(BF16)
    prob = prob.astype(BF16)
    first = iota((MID, 1), 0) == 0
    shape = (COV, WIDTH)
    for n, (i, t) in enumerate(cells):
        rows = slice(n * COV, (n + 1) * COV)
        own = stats[rows]
        for c in range(2):
            send_ref[2 * i + c, t * MID : (t + 1) * MID, :] = low[n][:MID, WIDTH : 2 * WIDTH]
            send_ref[2 * i + c, 2 * MID + t * MID : 2 * MID + (t + 1) * MID, :] = low[n][:MID, 2 * WIDTH : 3 * WIDTH]
        send_ref[2 * i + t, 4 * MID : 5 * MID, :] = low[n][:MID, :WIDTH]
        send_ref[2 * i + t, 5 * MID : 6 * MID, :] = low[n][:MID, 3 * WIDTH :]
        send_ref[2 * i + t, 6 * MID : 7 * MID, :] = own[:MID].astype(BF16)
        mine = (picked[n][MID:, :WIDTH], picked[n][MID:, 3 * WIDTH :], jnp.where(first, own[MID:], 0.0))
        pair = [picked[n - t + u][MID:, at * WIDTH : (at + 1) * WIDTH] for at in (1, 2) for u in range(2)]
        far_block = pair[0]
        for at, x in enumerate((*pair[1:], *mine)):
            far_block = far_block + pltpu.roll(x, at + 1, 0)
        send_ref[2 * i + t, 7 * MID :, :] = far_block.astype(BF16)
        kept = (
            picked[n][:, :WIDTH], picked[n][:, 3 * WIDTH :], out[rows],
            jnp.broadcast_to(lse[rows], shape), jnp.broadcast_to(delta[rows], shape),
        )
        for at, x in enumerate(kept):
            cov_ref[at, i, t] = x
        keys = block(k_ref, (i, t))
        both = dot_nn(jnp.concatenate([dscore[rows], prob[rows]], 0), keys)
        cov_ref[5, i, t] = both[:COV]
        cov_ref[6, i, t] = both[COV:]
        chosen = selects[i] * valids[i].astype(BF16)
        left_ref[i, t] = jnp.concatenate([dscore[rows], prob[rows], chosen, chosen], 0).T


def extract(offsets, q, k, v, g):
    n = EXTRACT_HEADS
    column = pl.BlockSpec((2 * SEG1, n * WIDTH), lambda h, *_: (0, h))
    return pl.pallas_call(
        extract_kernel,
        grid_spec=pltpu.PrefetchScalarGridSpec(
            num_scalar_prefetch=2,
            grid=(HEADS // n,),
            in_specs=[column] * 4,
            out_specs=[
                pl.BlockSpec((2 * n, PACK, WIDTH), lambda h, *_: (h, 0, 0)),
                pl.BlockSpec((KEPT, n, 2, COV, WIDTH), lambda h, *_: (0, h, 0, 0, 0)),
                pl.BlockSpec((n, 2, SEG1, 4 * COV), lambda h, *_: (h, 0, 0, 0)),
            ],
        ),
        out_shape=[
            jax.ShapeDtypeStruct((2 * HEADS, PACK, WIDTH), BF16),
            jax.ShapeDtypeStruct((KEPT, HEADS, 2, COV, WIDTH), F32),
            jax.ShapeDtypeStruct((HEADS, 2, SEG1, 4 * COV), BF16),
        ],
        compiler_params=pltpu.CompilerParams(vmem_limit_bytes=VMEM),
        cost_estimate=pl.CostEstimate(flops=2**32, bytes_accessed=12 * 2**20, transcendentals=2**18),
        name="extract",
    )(*offsets, q, k, v, g)


def local_kernel(first, off2_ref, off3_ref, q_ref, k_ref, v_ref, g_ref, *rest):
    att_ref, dq_ref, dk_ref, dv_ref = rest[-4:]
    head = pl.program_id(0) + first
    position = iota((1, SEG1), 1)
    covered = ((position & (DILATION_TWO - 1)) == off2_ref[head]) | (position == off3_ref[head])
    for t in range(2):
        rows = slice(t * SEG1, (t + 1) * SEG1)
        q, k, v, g = (ref[rows, :] for ref in (q_ref, k_ref, v_ref, g_ref))
        scores = dot_nt(k, q) * (FACTOR * math.log2(math.e))
        grad = dot_nt(v, g)
        weight = jnp.exp2(scores - jnp.max(scores, axis=0, keepdims=True))
        inverse = 1.0 / jnp.sum(weight, axis=0, keepdims=True)
        att = (dot_nn(v.T, weight.astype(BF16)) * inverse).astype(BF16).astype(F32)
        delta = jnp.sum(g.T.astype(F32) * att, axis=0, keepdims=True)
        att_ref[rows, :] = jnp.where(covered, 0.0, att).astype(BF16).T
        prob = weight * jnp.where(covered, 0.0, inverse)
        dscore = (prob * (grad - delta)).astype(BF16)
        dq_ref[rows, :] = (dot_nn(k.T, dscore) * FACTOR).astype(BF16).T
        dk_ref[rows, :] = dot_nn(dscore, q)
        dv_ref[rows, :] = dot_nn(prob.astype(BF16), g)


def local(offsets, q, k, v, g, first, count, earlier):
    block = pl.BlockSpec((2 * SEG1, WIDTH), lambda h, *_: (0, h + first))
    kept = [pl.BlockSpec(memory_space=pl.ANY)] * len(earlier)
    share = count / HEADS
    return pl.pallas_call(
        lambda *refs: local_kernel(first, *refs),
        grid_spec=pltpu.PrefetchScalarGridSpec(
            num_scalar_prefetch=2,
            grid=(count,),
            in_specs=[block] * 4 + kept,
            out_specs=[block] * 4,
        ),
        out_shape=[jax.ShapeDtypeStruct(q.shape, d) for d in (BF16, BF16, F32, F32)],
        input_output_aliases={6 + i: i for i in range(len(earlier))},
        compiler_params=pltpu.CompilerParams(vmem_limit_bytes=VMEM),
        cost_estimate=pl.CostEstimate(
            flops=int(share * 12 * 2**30), bytes_accessed=int(share * 20 * 2**20), transcendentals=int(share * 2**22)
        ),
        name="local",
    )(*offsets, q, k, v, g, *earlier)


def merge_lse(parts):
    top = parts[0]
    for part in parts[1:]:
        top = jnp.maximum(top, part)
    total = jnp.exp(parts[0] - top)
    for part in parts[1:]:
        total = total + jnp.exp(part - top)
    return top + jnp.log(total)


def part(ref, at, rows):
    return ref[:, at * MID : at * MID + rows, :].reshape(ref.shape[0] * rows, WIDTH)


def far_places(shape, dim, starts):
    j = iota(shape, dim)
    n = shape[dim] // 7
    place = jnp.zeros(shape, jnp.int32)
    for at, start in enumerate(starts):
        if at < 2:
            u = j - 2 * n * at
            place = jnp.where((u >= 0) & (u < 2 * n), MID * (u // 2) + u % 2 + start, place)
        else:
            u = j - n * (at + 2)
            place = jnp.where((u >= 0) & (u < n), MID * u + start, place)
    return place


def forward_kernel(off2_ref, off3_ref, in_ref, far_ref, out_ref, figures_ref):
    head = lax.axis_index("inner") // 2
    off_three = off3_ref[head]
    n = in_ref.shape[0]
    k, v, q, g = part(in_ref, 0, 2 * MID), part(in_ref, 2, 2 * MID), part(in_ref, 4, MID), part(in_ref, 5, MID)
    queries = n * MID
    scores = dot_nt(q, k) * FACTOR
    top = jnp.max(scores, axis=1, keepdims=True)
    weight = jnp.exp(scores - top)
    total = jnp.sum(weight, axis=1, keepdims=True)
    out = dot_nn(weight.astype(BF16), v) / total
    lse = jnp.broadcast_to(top + jnp.log(total), (queries, WIDTH))
    delta = jnp.broadcast_to(jnp.sum(g.astype(F32) * out, axis=1, keepdims=True), (queries, WIDTH))
    out_ref[...] = out
    figures_ref[0] = lse
    figures_ref[1] = delta
    pick = (iota((7 * n, queries), 1) == far_places((7 * n, 1), 0, (0, 2, 4, 5, 6))).astype(BF16)
    picked = dot_nn(pick, part(in_ref, 7, MID))
    stats = picked[6 * n :]
    same = ((off_three % DILATION_TWO) == off2_ref[head]) & (
        iota((n, MID, WIDTH), 1) == off_three // DILATION_TWO
    )
    lse1, delta1 = join3(stats, 0), join3(stats, 3)
    lse2 = jnp.max(jnp.where(same, lse.reshape(n, MID, WIDTH), NEG), axis=1)
    delta2 = jnp.sum(jnp.where(same, delta.reshape(n, MID, WIDTH), 0.0), axis=1)
    both = merge_lse([lse1, lse2])
    delta = jnp.exp(lse1 - both) * delta1 + jnp.exp(lse2 - both) * delta2
    rows = jnp.concatenate([picked[: 6 * n], lanes(split3(both) + split3(delta), n)], 0).astype(BF16)
    for o in range(far_ref.shape[0]):
        far_ref[o] = rows


def backward_kernel(off2_ref, off3_ref, in_ref, far_ref, out2_ref, figures_ref, out_ref, key_ref, query_ref):
    head, outer = lax.axis_index("inner") // 2, lax.axis_index("outer")
    off_three = off3_ref[head]
    n = in_ref.shape[0]
    queries = n * MID
    turn = (iota((8, WIDTH), 0) == iota((8, WIDTH), 1)).astype(BF16)
    kf, vf = part(far_ref, 0, 2 * MID), part(far_ref, 2, 2 * MID)
    qf, gf = part(far_ref, 4, MID), part(far_ref, 5, MID)
    figures = dot_nt(turn, part(far_ref, 6, MID))
    lse12 = figures[0:1] + figures[1:2] + figures[2:3]
    delta12 = figures[3:4] + figures[4:5] + figures[5:6]
    scores = dot_nt(kf, qf) * FACTOR
    grads = dot_nt(vf, gf)
    top = jnp.max(scores, axis=0, keepdims=True)
    weight = jnp.exp(scores - top)
    total = jnp.sum(weight, axis=0, keepdims=True)
    lse3 = top + jnp.log(total)
    share = weight / total
    delta3 = jnp.sum(share * grads, axis=0, keepdims=True)
    lse = merge_lse([lse12, lse3])
    delta = jnp.exp(lse12 - lse) * delta12 + jnp.exp(lse3 - lse) * delta3
    prob = jnp.exp(scores - lse)
    dscore = (prob * (grads - delta)).astype(BF16)
    key_ref[0] = dot_nn(dscore, qf)
    key_ref[1] = dot_nn(prob.astype(BF16), gf)
    query_ref[0] = dot_tn(dscore, kf)
    query_ref[1] = dot_tn(share.astype(BF16), vf)
    eight = iota((8, lse3.shape[1]), 0)
    figures = jnp.zeros(eight.shape, F32)
    for at, x in enumerate(split3(lse3) + split3(delta3)):
        figures = jnp.where(eight == at, x, figures)
    query_ref[2] = dot_tn(figures.astype(BF16), turn)
    own_keys = pl.ds(pl.multiple_of(outer * 2 * n, 2 * n), 2 * n)
    own_queries = pl.ds(pl.multiple_of(outer * n, n), n)
    own = [key_ref[0, own_keys, :], key_ref[1, own_keys, :]] + [query_ref[at, own_queries, :] for at in range(3)]
    unpick = (iota((queries, 7 * n), 0) == far_places((1, 7 * n), 1, (3, 5, 0, 1, 2))).astype(BF16)
    packed = dot_nn(unpick, jnp.concatenate(own, 0).astype(BF16))
    same = ((off_three % DILATION_TWO) == off2_ref[head]) & (
        iota((n, MID, WIDTH), 1) == off_three // DILATION_TWO
    )

    def expand(column, other):
        wide = jnp.broadcast_to(jnp.broadcast_to(column, (n, WIDTH)).reshape(n, 1, WIDTH), (n, MID, WIDTH))
        return jnp.where(same, wide, other).reshape(queries, WIDTH)

    lse3, delta3 = expand(join3(own[4], 0), NEG), expand(join3(own[4], 3), 0.0)
    stats = part(in_ref, 6, MID).astype(F32)
    lse1, delta1 = join3(stats, 0), join3(stats, 3)
    lse2, delta2 = figures_ref[0], figures_ref[1]
    lse = merge_lse([lse1, lse2, lse3])
    delta = jnp.exp(lse1 - lse) * delta1 + jnp.exp(lse2 - lse) * delta2 + jnp.exp(lse3 - lse) * delta3
    k, v, q, g = part(in_ref, 0, 2 * MID), part(in_ref, 2, 2 * MID), part(in_ref, 4, MID), part(in_ref, 5, MID)
    prob = jnp.exp(dot_nt(q, k) * FACTOR - lse[:, :1])
    dscore = (prob * (dot_nt(g, v) - delta[:, :1])).astype(BF16)

    def give(at, rows, value):
        out_ref[:, at * MID : at * MID + rows, :] = value.astype(BF16).reshape(n, rows, WIDTH)

    give(0, 2 * MID, dot_tn(dscore, q))
    give(2, 2 * MID, dot_tn(prob.astype(BF16), g))
    give(4, MID, dot_nn(dscore, k))
    give(5, MID, out2_ref[...])
    give(6, MID, lanes(split3(lse2), queries))
    give(7, MID, packed)


def remote_call(kernel, offsets, arrays, shapes, scratch, name):
    vmem = pl.BlockSpec(memory_space=pltpu.VMEM)
    smem = pl.BlockSpec(memory_space=pltpu.SMEM)
    return pl.pallas_call(
        kernel,
        in_specs=[smem, smem] + [vmem] * len(arrays),
        out_specs=[vmem] * len(shapes),
        out_shape=[jax.ShapeDtypeStruct(*x) for x in shapes],
        scratch_shapes=[pltpu.VMEM(*x) for x in scratch],
        compiler_params=pltpu.CompilerParams(vmem_limit_bytes=VMEM),
        cost_estimate=pl.CostEstimate(flops=2**31, bytes_accessed=2**21, transcendentals=2**19),
        name=name,
    )(*offsets, *arrays)


def remote_forward(offsets, received, outer):
    n = received.shape[0]
    rows = n * MID
    return remote_call(
        forward_kernel, offsets, (received,),
        [((outer, 7 * n, WIDTH), BF16), ((rows, WIDTH), F32), ((2, rows, WIDTH), F32)], [], "remote_forward",
    )


def remote_backward(offsets, received, far, out, figures):
    n, outer = received.shape[0], far.shape[0]
    return remote_call(
        backward_kernel, offsets, (received, far, out, figures), [(received.shape, BF16)],
        [((2, outer * 2 * n, WIDTH), F32), ((3, outer * n, WIDTH), F32)], "remote_backward",
    )[0]


def prepare(off2_ref, off3_ref, cov_ref, back_ref, right_ref):
    cells, rows = 2 * HEADS, 2 * HEADS * COV
    back = back_ref[...].astype(F32)

    def pad(x):
        return jnp.concatenate([x, jnp.zeros((cells, COV - MID, WIDTH), F32)], 1).reshape(rows, WIDTH)

    def own(at):
        return pad(back[:, at * MID : (at + 1) * MID])

    def both(at):
        x = back[:, at * MID : (at + 2) * MID].reshape(HEADS, 2, COV, WIDTH)
        return pad((x[:, 0] + x[:, 1]).reshape(cells, MID, WIDTH))

    def spread(x):
        return jnp.broadcast_to(x.reshape(cells, 1, WIDTH), (cells, COV, WIDTH)).reshape(rows, WIDTH)

    row = iota((COV, WIDTH), 0)
    is_far = []
    for head in range(HEADS):
        off_three = off3_ref[head]
        twice = (off_three % DILATION_TWO) == off2_ref[head]
        is_far += [(row == jnp.where(twice, off_three // DILATION_TWO, MID)).astype(F32)] * 2
    is_far = jnp.concatenate(is_far, 0) > 0.0
    is_mid = jnp.concatenate([row] * cells, 0) < MID
    ones = (iota((WIDTH, WIDTH), 0) < 3).astype(BF16)

    def joined(x):
        return dot_nn(x.astype(BF16), ones)

    q, g, out, lse1, delta1, dq_one, dq_two = (cov_ref[at].reshape(rows, WIDTH) for at in range(KEPT))
    packed = back[:, 7 * MID : 8 * MID]
    far = packed[:, 3:7].reshape(HEADS, 2, 4, WIDTH)
    far = (far[:, 0] + far[:, 1]).reshape(HEADS, 2, 2, WIDTH)
    lse2 = jnp.where(is_mid, joined(own(6)), NEG)
    lse3 = jnp.where(is_far, joined(spread(packed[:, 2:3])), NEG)
    lse = merge_lse([lse1, lse2, lse3])
    share = jnp.exp(lse1 - lse)
    att = (
        share * out + jnp.exp(lse2 - lse) * own(5) + jnp.exp(lse3 - lse) * spread(packed[:, 1:2])
    ).astype(BF16)
    delta = jnp.sum(g * att.astype(F32), axis=1, keepdims=True)
    change = share * (delta - delta1)
    dq = share * dq_one - change * dq_two + own(4) + jnp.where(is_far, spread(packed[:, 0:1]), 0.0)
    dk = both(0) + jnp.where(is_far, spread(far[:, 0]), 0.0)
    dv = both(2) + jnp.where(is_far, spread(far[:, 1]), 0.0)

    def put(at, column, x):
        right_ref[:, at * COV : (at + 1) * COV, column * WIDTH : (column + 1) * WIDTH] = x.astype(BF16).reshape(
            cells, COV, WIDTH
        )

    def put_two(column, x):
        high = x.astype(BF16)
        put(2, column, high)
        put(3, column, x - high.astype(F32))

    right_ref[:, : 2 * COV, : 2 * WIDTH] = jnp.zeros((cells, 2 * COV, 2 * WIDTH), BF16)
    right_ref[:, :COV, 3 * WIDTH :] = jnp.zeros((cells, COV, WIDTH), BF16)
    right_ref[:, 3 * COV :, :WIDTH] = jnp.zeros((cells, COV, WIDTH), BF16)
    put(2, 0, att)
    put_two(1, dq)
    put(0, 2, share * q)
    put(1, 2, -change * q)
    put_two(2, dk)
    put(1, 3, share * g)
    put_two(3, dv)


def finish_kernel(
    off2_ref, off3_ref, cov_ref, back_ref, left_ref,
    att_ref, dq_ref, dk_ref, dv_ref, att_out, dq_out, dk_out, dv_out, right_ref,
):
    head, t = pl.program_id(0) * FINISH_HEADS, pl.program_id(1)

    @pl.when((pl.program_id(0) == 0) & (t == 0))
    def _():
        prepare(off2_ref, off3_ref, cov_ref, back_ref, right_ref)

    for i in range(FINISH_HEADS):
        c = slice(i * WIDTH, (i + 1) * WIDTH)
        x = dot_nn(left_ref[i, 0], right_ref[2 * (head + i) + t])
        att_out[:, c] = (att_ref[:, c].astype(F32) + x[:, :WIDTH]).astype(BF16)
        dq_out[:, c] = (dq_ref[:, c].astype(F32) + FACTOR * x[:, WIDTH : 2 * WIDTH]).astype(BF16)
        dk_out[:, c] = (FACTOR * (dk_ref[:, c] + x[:, 2 * WIDTH : 3 * WIDTH])).astype(BF16)
        dv_out[:, c] = (dv_ref[:, c] + x[:, 3 * WIDTH :]).astype(BF16)


def finish(offsets, cov, left, back, local_parts):
    n = FINISH_HEADS
    block = pl.BlockSpec((SEG1, n * WIDTH), lambda h, t, *_: (t, h))
    whole = [pl.BlockSpec(x.shape, lambda *_, r=x.ndim: (0,) * r, pipeline_mode=pl.Buffered(1)) for x in (cov, back)]
    return pl.pallas_call(
        finish_kernel,
        grid_spec=pltpu.PrefetchScalarGridSpec(
            num_scalar_prefetch=2,
            grid=(HEADS // n, 2),
            in_specs=whole
            + [pl.BlockSpec((n, 1, SEG1, 4 * COV), lambda h, t, *_: (h, t, 0, 0))]
            + [block] * 4,
            out_specs=[block] * 4,
            scratch_shapes=[pltpu.VMEM((2 * HEADS, 4 * COV, 4 * WIDTH), BF16)],
        ),
        out_shape=[jax.ShapeDtypeStruct(x.shape, BF16) for x in local_parts],
        compiler_params=pltpu.CompilerParams(vmem_limit_bytes=VMEM),
        cost_estimate=pl.CostEstimate(flops=2**30, bytes_accessed=28 * 2**20, transcendentals=2**18),
        name="finish",
    )(*offsets, cov, back, left, *local_parts)


def solution(mesh):
    outer = mesh.shape["outer"]
    split = P(("outer", "inner"), None)

    def body(queries, keys, values, out_grad, middle_head_offsets, distant_head_offsets):
        offsets = (middle_head_offsets, distant_head_offsets)
        arrays = (queries, keys, values, out_grad)
        send, cov, left = extract(offsets, *arrays)
        got = lax.all_to_all(send, "inner", 0, 0)
        parts = local(offsets, *arrays, 0, 4, ())
        got, *parts = lax.optimization_barrier((got, *parts))
        far, out, figures = remote_forward(offsets, got, outer)
        far, *parts = lax.optimization_barrier((far, *parts))
        far = lax.all_to_all(far, "outer", 0, 0)
        parts = local(offsets, *arrays, 4, 2, parts)
        far, *parts = lax.optimization_barrier((far, *parts))
        back = remote_backward(offsets, got, far, out, figures)
        back, *parts = lax.optimization_barrier((back, *parts))
        back = lax.all_to_all(back, "inner", 0, 0)
        parts = local(offsets, *arrays, 6, 2, parts)
        back, *parts = lax.optimization_barrier((back, *parts))
        return finish(offsets, cov, left, back, parts)

    return jax.shard_map(
        body, mesh=mesh, in_specs=(split,) * 4 + (P(), P()), out_specs=(split,) * 4, check_vma=False
    )
```

```python
import math

import jax
import jax.numpy as jnp
from jax import lax
from jax.experimental import pallas as pl
from jax.experimental.pallas import tpu as pltpu
from jax.sharding import PartitionSpec as P

SEG1 = 512
DILATION_TWO = 32
DILATION_THREE = 512
HEADS = 8
WIDTH = 128
FACTOR = WIDTH ** (-0.5)
MID = SEG1 // DILATION_TWO
COV = 32
PACK = 128
KEPT = 7
EXTRACT_HEADS = 2
SHARES = (3, 2, 3)
VMEM = 63 * 2**20
HALF = DILATION_TWO // 2
NEG = -1e30
F32 = jnp.float32
BF16 = jnp.bfloat16


def dot_nn(a, b):
    return lax.dot_general(a, b, (((1,), (0,)), ((), ())), preferred_element_type=F32)


def dot_nt(a, b):
    return lax.dot_general(a, b, (((1,), (1,)), ((), ())), preferred_element_type=F32)


def dot_tn(a, b):
    return lax.dot_general(a, b, (((0,), (0,)), ((), ())), preferred_element_type=F32)


def iota(shape, dim):
    return lax.broadcasted_iota(jnp.int32, shape, dim)


def split3(x):
    high = x.astype(BF16).astype(F32)
    rest = x - high
    middle = rest.astype(BF16).astype(F32)
    return high, middle, (rest - middle).astype(BF16).astype(F32)


def lanes(columns, rows):
    lane = iota((rows, WIDTH), 1)
    out = jnp.zeros((rows, WIDTH), F32)
    for j, column in enumerate(columns):
        out = jnp.where(lane == j, column, out)
    return out


def join3(x, at):
    return x[:, at : at + 1] + x[:, at + 1 : at + 2] + x[:, at + 2 : at + 3]


def targets(shape, dim, off_two, off_three):
    j = iota(shape, dim)
    return jnp.where(j < MID, DILATION_TWO * j + off_two, jnp.where(j == MID, off_three, -1))


def columns(ref, head):
    return ref.at[:, pl.ds(pl.multiple_of(head * WIDTH, WIDTH), WIDTH)]


def extract_kernel(
    off2_ref, off3_ref, q_hbm, k_hbm, v_hbm, g_hbm, send_hbm, cov_hbm, left_hbm,
    q_all, k_all, v_all, g_all, send_ref, cov_ref, left_ref, sems, out_sems,
):
    def load(at, head):
        source, target = ((q_hbm, q_all), (k_hbm, k_all), (v_hbm, v_all), (g_hbm, g_all))[at]
        return pltpu.make_async_copy(columns(source, head), target.at[head], sems.at[head, at])

    def places(step):
        heads = pl.ds(step * EXTRACT_HEADS, EXTRACT_HEADS)
        return (pl.ds(step * 2 * EXTRACT_HEADS, 2 * EXTRACT_HEADS),), (slice(None), heads), (heads,)

    def give(step):
        pairs = zip((send_ref, cov_ref, left_ref), (send_hbm, cov_hbm, left_hbm), places(step))
        return [
            pltpu.make_async_copy(source.at[place], target.at[place], out_sems.at[step, at])
            for at, (source, target, place) in enumerate(pairs)
        ]

    for head in range(HEADS):
        for at in range(4):
            load(at, head).start()

    @pl.loop(0, HEADS // EXTRACT_HEADS)
    def _(step):
        first = step * EXTRACT_HEADS
        for i in range(EXTRACT_HEADS):
            for at in range(4):
                load(at, first + i).wait()
        here = [ref.at[pl.ds(first, EXTRACT_HEADS)] for ref in (q_all, k_all, v_all, g_all)]
        out = [ref.at[place] for ref, place in zip((send_ref, cov_ref, left_ref), places(step))]
        extract_heads(first, off2_ref, off3_ref, *here, *out)
        for copy in give(step):
            copy.start()

    for step in range(HEADS // EXTRACT_HEADS):
        for copy in give(step):
            copy.wait()


def extract_heads(first_head, off2_ref, off3_ref, q_ref, k_ref, v_ref, g_ref, send_ref, cov_ref, left_ref):
    cells = [(i, t) for i in range(EXTRACT_HEADS) for t in range(2)]

    def block(ref, cell):
        i, t = cell
        return ref[i, t * SEG1 : (t + 1) * SEG1, :]

    selects, valids = [], []
    row = iota((COV, 1), 0)
    for i in range(EXTRACT_HEADS):
        head = first_head + i
        off_two, off_three = off2_ref[head], off3_ref[head]
        position = targets((COV, 1), 0, off_two, off_three)
        selects.append((iota((COV, SEG1), 1) == position).astype(BF16))
        twice = (off_three % DILATION_TWO) == off_two
        valids.append(((row < MID) | ((row == MID) & jnp.logical_not(twice))).astype(F32))
    picked = [
        dot_nn(selects[cell[0]], jnp.concatenate([block(r, cell) for r in (q_ref, k_ref, v_ref, g_ref)], 1))
        for cell in cells
    ]
    low = [x.astype(BF16) for x in picked]
    scores = [dot_nt(x[:, :WIDTH], block(k_ref, cell)) for x, cell in zip(low, cells)]
    grads = [dot_nt(x[:, 3 * WIDTH :], block(v_ref, cell)) for x, cell in zip(low, cells)]
    scores, grads = jnp.concatenate(scores, 0) * FACTOR, jnp.concatenate(grads, 0)
    top = jnp.max(scores, axis=1, keepdims=True)
    weight = jnp.exp(scores - top)
    total = jnp.sum(weight, axis=1, keepdims=True)
    weight_low = weight.astype(BF16)
    out = jnp.concatenate(
        [dot_nn(weight_low[n * COV : (n + 1) * COV], block(v_ref, cell)) for n, cell in enumerate(cells)], 0
    ) / total
    lse = top + jnp.log(total)
    g_cov = jnp.concatenate([x[:, 3 * WIDTH :] for x in picked], 0)
    delta = jnp.sum(g_cov * out, axis=1, keepdims=True)
    stats = lanes(split3(lse) + split3(delta), COV * len(cells))
    prob = weight * (jnp.concatenate([valids[i] for i, _ in cells], 0) / total)
    dscore = (prob * (grads - delta)).astype(BF16)
    prob = prob.astype(BF16)
    first = iota((MID, 1), 0) == 0
    shape = (COV, WIDTH)
    for n, (i, t) in enumerate(cells):
        rows = slice(n * COV, (n + 1) * COV)
        own = stats[rows]
        for c in range(2):
            send_ref[2 * i + c, t * MID : (t + 1) * MID, :] = low[n][:MID, WIDTH : 2 * WIDTH]
            send_ref[2 * i + c, 2 * MID + t * MID : 2 * MID + (t + 1) * MID, :] = low[n][:MID, 2 * WIDTH : 3 * WIDTH]
        send_ref[2 * i + t, 4 * MID : 5 * MID, :] = low[n][:MID, :WIDTH]
        send_ref[2 * i + t, 5 * MID : 6 * MID, :] = low[n][:MID, 3 * WIDTH :]
        send_ref[2 * i + t, 6 * MID : 7 * MID, :] = own[:MID].astype(BF16)
        mine = (picked[n][MID:, :WIDTH], picked[n][MID:, 3 * WIDTH :], jnp.where(first, own[MID:], 0.0))
        pair = [picked[n - t + u][MID:, at * WIDTH : (at + 1) * WIDTH] for at in (1, 2) for u in range(2)]
        far_block = pair[0]
        for at, x in enumerate((*pair[1:], *mine)):
            far_block = far_block + pltpu.roll(x, at + 1, 0)
        send_ref[2 * i + t, 7 * MID :, :] = far_block.astype(BF16)
        kept = (
            picked[n][:, :WIDTH], picked[n][:, 3 * WIDTH :], out[rows],
            jnp.broadcast_to(lse[rows], shape), jnp.broadcast_to(delta[rows], shape),
        )
        for at, x in enumerate(kept):
            cov_ref[at, i, t] = x
        keys = block(k_ref, (i, t))
        both = dot_nn(jnp.concatenate([dscore[rows], prob[rows]], 0), keys)
        cov_ref[5, i, t] = both[:COV]
        cov_ref[6, i, t] = both[COV:]
        chosen = selects[i] * valids[i].astype(BF16)
        left_ref[i, t] = jnp.concatenate([dscore[rows], prob[rows], chosen, chosen], 0).T


def extract(offsets, q, k, v, g):
    smem, hbm = pl.BlockSpec(memory_space=pltpu.SMEM), pl.BlockSpec(memory_space=pl.ANY)
    shapes = [
        ((2 * HEADS, PACK, WIDTH), BF16),
        ((KEPT, HEADS, 2, COV, WIDTH), F32),
        ((HEADS, 2, SEG1, 4 * COV), BF16),
    ]
    return pl.pallas_call(
        extract_kernel,
        in_specs=[smem, smem] + [hbm] * 4,
        out_specs=[hbm] * 3,
        out_shape=[jax.ShapeDtypeStruct(*x) for x in shapes],
        scratch_shapes=[pltpu.VMEM((HEADS, 2 * SEG1, WIDTH), BF16)] * 4
        + [pltpu.VMEM(*x) for x in shapes]
        + [pltpu.SemaphoreType.DMA((HEADS, 4)), pltpu.SemaphoreType.DMA((HEADS // EXTRACT_HEADS, 3))],
        compiler_params=pltpu.CompilerParams(vmem_limit_bytes=VMEM),
        cost_estimate=pl.CostEstimate(flops=2**32, bytes_accessed=12 * 2**20, transcendentals=2**18),
        name="extract",
    )(*offsets, q, k, v, g)


def local_kernel(first, count, kept, off2_ref, off3_ref, *refs):
    sources, outs = refs[:4], refs[4 + kept : 8 + kept]
    held, done, (in_sems, out_sems) = refs[8 + kept : 12 + kept], refs[12 + kept : 16 + kept], refs[16 + kept :]
    position = iota((1, SEG1), 1)

    def loads(i, t):
        rows = pl.ds(t * SEG1, SEG1)
        lane = pl.ds(pl.multiple_of((first + i) * WIDTH, WIDTH), WIDTH)
        return [
            pltpu.make_async_copy(sources[at].at[rows, lane], held[at].at[i, rows], in_sems.at[i, t, at])
            for at in range(4)
        ]

    def stores(i, t):
        lane = pl.ds(pl.multiple_of((first + i) * WIDTH, WIDTH), WIDTH)
        rows = pl.ds(t * SEG1, SEG1)
        return [
            pltpu.make_async_copy(
                done[at].at[i, t], outs[at].at[t, :, :, :, lane] if at < 2 else outs[at].at[first + i, rows],
                out_sems.at[i, t, at],
            )
            for at in range(4)
        ]

    def start(i):
        for t in range(2):
            for copy in loads(i, t):
                copy.start()

    start(0)

    @pl.loop(0, count)
    def _(i):
        @pl.when(i + 1 < count)
        def _():
            start(i + 1)

        head = first + i
        covered = ((position & (DILATION_TWO - 1)) == off2_ref[head]) | (position == off3_ref[head])
        for t in range(2):
            for copy in loads(i, t):
                copy.wait()
            rows = slice(t * SEG1, (t + 1) * SEG1)
            q, k, v, g = (ref[i, rows, :] for ref in held)
            scores = dot_nt(k, q) * (FACTOR * math.log2(math.e))
            grad = dot_nt(v, g)
            weight = jnp.exp2(scores - jnp.max(scores, axis=0, keepdims=True))
            inverse = 1.0 / jnp.sum(weight, axis=0, keepdims=True)
            att = (dot_nn(v.T, weight.astype(BF16)) * inverse).astype(BF16)
            delta = jnp.sum(g.T.astype(F32) * att.astype(F32), axis=0, keepdims=True)
            done[0][i, t] = att.T.reshape(MID, 2, HALF, WIDTH)
            prob = weight * jnp.where(covered, 0.0, inverse)
            dscore = (prob * (grad - delta)).astype(BF16)
            done[1][i, t] = (dot_nn(k.T, dscore) * FACTOR).astype(BF16).T.reshape(MID, 2, HALF, WIDTH)
            done[2][i, t] = dot_nn(dscore, q).astype(BF16)
            done[3][i, t] = dot_nn(prob.astype(BF16), g).astype(BF16)
            for copy in stores(i, t):
                copy.start()

    @pl.loop(0, count)
    def _(i):
        for t in range(2):
            for copy in stores(i, t):
                copy.wait()


def local(offsets, arrays, first, count, earlier):
    smem, hbm = pl.BlockSpec(memory_space=pltpu.SMEM), pl.BlockSpec(memory_space=pl.ANY)
    share = count / HEADS
    period = (MID, 2, HALF)
    return pl.pallas_call(
        lambda *refs: local_kernel(first, count, len(earlier), *refs),
        in_specs=[smem, smem] + [hbm] * (4 + len(earlier)),
        out_specs=[hbm] * 4,
        out_shape=[jax.ShapeDtypeStruct((2, *period, HEADS * WIDTH), BF16)] * 2
        + [jax.ShapeDtypeStruct((HEADS, 2 * SEG1, WIDTH), BF16)] * 2,
        input_output_aliases={6 + at: at for at in range(len(earlier))},
        scratch_shapes=[pltpu.VMEM((count, 2 * SEG1, WIDTH), BF16)] * 4
        + [pltpu.VMEM((count, 2, *period, WIDTH), BF16)] * 2
        + [pltpu.VMEM((count, 2, SEG1, WIDTH), BF16)] * 2
        + [pltpu.SemaphoreType.DMA((count, 2, 4))] * 2,
        compiler_params=pltpu.CompilerParams(vmem_limit_bytes=VMEM),
        cost_estimate=pl.CostEstimate(
            flops=int(share * 12 * 2**30), bytes_accessed=int(share * 16 * 2**20), transcendentals=int(share * 2**22)
        ),
        name="local",
    )(*offsets, *arrays, *earlier)


def merge_lse(parts):
    top = parts[0]
    for part in parts[1:]:
        top = jnp.maximum(top, part)
    total = jnp.exp(parts[0] - top)
    for part in parts[1:]:
        total = total + jnp.exp(part - top)
    return top + jnp.log(total)


def part(ref, at, rows):
    return ref[:, at * MID : at * MID + rows, :].reshape(ref.shape[0] * rows, WIDTH)


def far_places(shape, dim, starts):
    j = iota(shape, dim)
    n = shape[dim] // 7
    place = jnp.zeros(shape, jnp.int32)
    for at, start in enumerate(starts):
        if at < 2:
            u = j - 2 * n * at
            place = jnp.where((u >= 0) & (u < 2 * n), MID * (u // 2) + u % 2 + start, place)
        else:
            u = j - n * (at + 2)
            place = jnp.where((u >= 0) & (u < n), MID * u + start, place)
    return place


def forward_kernel(off2_ref, off3_ref, in_ref, far_ref, out_ref, figures_ref):
    head = lax.axis_index("inner") // 2
    off_three = off3_ref[head]
    n = in_ref.shape[0]
    k, v, q, g = part(in_ref, 0, 2 * MID), part(in_ref, 2, 2 * MID), part(in_ref, 4, MID), part(in_ref, 5, MID)
    queries = n * MID
    scores = dot_nt(q, k) * FACTOR
    top = jnp.max(scores, axis=1, keepdims=True)
    weight = jnp.exp(scores - top)
    total = jnp.sum(weight, axis=1, keepdims=True)
    out = dot_nn(weight.astype(BF16), v) / total
    lse = jnp.broadcast_to(top + jnp.log(total), (queries, WIDTH))
    delta = jnp.broadcast_to(jnp.sum(g.astype(F32) * out, axis=1, keepdims=True), (queries, WIDTH))
    out_ref[...] = out.astype(BF16)
    figures_ref[...] = lanes([lse, delta], queries)
    pick = (iota((7 * n, queries), 1) == far_places((7 * n, 1), 0, (0, 2, 4, 5, 6))).astype(BF16)
    picked = dot_nn(pick, part(in_ref, 7, MID))
    stats = picked[6 * n :]
    same = ((off_three % DILATION_TWO) == off2_ref[head]) & (
        iota((n, MID, WIDTH), 1) == off_three // DILATION_TWO
    )
    lse1, delta1 = join3(stats, 0), join3(stats, 3)
    lse2 = jnp.max(jnp.where(same, lse.reshape(n, MID, WIDTH), NEG), axis=1)
    delta2 = jnp.sum(jnp.where(same, delta.reshape(n, MID, WIDTH), 0.0), axis=1)
    both = merge_lse([lse1, lse2])
    delta = jnp.exp(lse1 - both) * delta1 + jnp.exp(lse2 - both) * delta2
    rows = jnp.concatenate([picked[: 6 * n], lanes(split3(both) + split3(delta), n)], 0).astype(BF16)
    for o in range(far_ref.shape[0]):
        far_ref[o] = rows


def backward_kernel(off2_ref, off3_ref, in_ref, far_ref, out2_ref, figures_ref, out_ref, key_ref, query_ref):
    head, outer = lax.axis_index("inner") // 2, lax.axis_index("outer")
    off_three = off3_ref[head]
    n = in_ref.shape[0]
    queries = n * MID
    turn = (iota((8, WIDTH), 0) == iota((8, WIDTH), 1)).astype(BF16)
    kf, vf = part(far_ref, 0, 2 * MID), part(far_ref, 2, 2 * MID)
    qf, gf = part(far_ref, 4, MID), part(far_ref, 5, MID)
    figures = dot_nt(turn, part(far_ref, 6, MID))
    lse12 = figures[0:1] + figures[1:2] + figures[2:3]
    delta12 = figures[3:4] + figures[4:5] + figures[5:6]
    scores = dot_nt(kf, qf) * FACTOR
    grads = dot_nt(vf, gf)
    top = jnp.max(scores, axis=0, keepdims=True)
    weight = jnp.exp(scores - top)
    total = jnp.sum(weight, axis=0, keepdims=True)
    lse3 = top + jnp.log(total)
    share = weight / total
    delta3 = jnp.sum(share * grads, axis=0, keepdims=True)
    lse = merge_lse([lse12, lse3])
    delta = jnp.exp(lse12 - lse) * delta12 + jnp.exp(lse3 - lse) * delta3
    prob = jnp.exp(scores - lse)
    dscore = (prob * (grads - delta)).astype(BF16)
    key_ref[0] = dot_nn(dscore, qf)
    key_ref[1] = dot_nn(prob.astype(BF16), gf)
    query_ref[0] = dot_tn(dscore, kf)
    query_ref[1] = dot_tn(share.astype(BF16), vf)
    eight = iota((8, lse3.shape[1]), 0)
    figures = jnp.zeros(eight.shape, F32)
    for at, x in enumerate(split3(lse3) + split3(delta3)):
        figures = jnp.where(eight == at, x, figures)
    query_ref[2] = dot_tn(figures.astype(BF16), turn)
    own_keys = pl.ds(pl.multiple_of(outer * 2 * n, 2 * n), 2 * n)
    own_queries = pl.ds(pl.multiple_of(outer * n, n), n)
    own = [key_ref[0, own_keys, :], key_ref[1, own_keys, :]] + [query_ref[at, own_queries, :] for at in range(3)]
    unpick = (iota((queries, 7 * n), 0) == far_places((1, 7 * n), 1, (3, 5, 0, 1, 2))).astype(BF16)
    packed = dot_nn(unpick, jnp.concatenate(own, 0).astype(BF16))
    same = ((off_three % DILATION_TWO) == off2_ref[head]) & (
        iota((n, MID, WIDTH), 1) == off_three // DILATION_TWO
    )

    def expand(column, other):
        wide = jnp.broadcast_to(jnp.broadcast_to(column, (n, WIDTH)).reshape(n, 1, WIDTH), (n, MID, WIDTH))
        return jnp.where(same, wide, other).reshape(queries, WIDTH)[:, 0:1]

    lse3, delta3 = expand(join3(own[4], 0), NEG), expand(join3(own[4], 3), 0.0)
    stats = part(in_ref, 6, MID).astype(F32)
    lse1, delta1 = join3(stats, 0), join3(stats, 3)
    lse2, delta2 = figures_ref[:, 0:1], figures_ref[:, 1:2]
    lse = merge_lse([lse1, lse2, lse3])
    delta = jnp.exp(lse1 - lse) * delta1 + jnp.exp(lse2 - lse) * delta2 + jnp.exp(lse3 - lse) * delta3
    k, v, q, g = part(in_ref, 0, 2 * MID), part(in_ref, 2, 2 * MID), part(in_ref, 4, MID), part(in_ref, 5, MID)
    prob = jnp.exp(dot_nt(q, k) * FACTOR - lse)
    dscore = (prob * (dot_nt(g, v) - delta)).astype(BF16)

    def give(at, rows, value):
        out_ref[:, at * MID : at * MID + rows, :] = value.astype(BF16).reshape(n, rows, WIDTH)

    give(0, 2 * MID, dot_tn(dscore, q))
    give(2, 2 * MID, dot_tn(prob.astype(BF16), g))
    give(4, MID, dot_nn(dscore, k))
    give(5, MID, out2_ref[...])
    give(6, MID, lanes(split3(lse2), queries))
    give(7, MID, packed)


def remote_call(kernel, offsets, arrays, shapes, scratch, name):
    vmem, smem = pl.BlockSpec(memory_space=pltpu.VMEM), pl.BlockSpec(memory_space=pltpu.SMEM)
    return pl.pallas_call(
        kernel,
        in_specs=[smem, smem] + [vmem] * len(arrays),
        out_specs=[vmem] * len(shapes),
        out_shape=shapes,
        scratch_shapes=[pltpu.VMEM(*x) for x in scratch],
        compiler_params=pltpu.CompilerParams(vmem_limit_bytes=VMEM),
        cost_estimate=pl.CostEstimate(flops=2**31, bytes_accessed=2**21, transcendentals=2**19),
        name=name,
    )(*offsets, *arrays)


def remote_forward(offsets, received, outer):
    n = received.shape[0]
    rows = n * MID
    return remote_call(
        forward_kernel, offsets, (received,),
        [jax.ShapeDtypeStruct((outer, 7 * n, WIDTH), BF16), jax.ShapeDtypeStruct((rows, WIDTH), BF16),
         jax.ShapeDtypeStruct((rows, WIDTH), F32)],
        [], "remote_forward",
    )


def remote_backward(offsets, received, far, out, figures):
    n, outer = received.shape[0], far.shape[0]
    return remote_call(
        backward_kernel, offsets, (received, far, out, figures), [jax.ShapeDtypeStruct(received.shape, BF16)],
        [((2, outer * 2 * n, WIDTH), F32), ((3, outer * n, WIDTH), F32)], "remote_backward",
    )[0]


def prepare(off2_ref, off3_ref, cov_ref, back_ref, right_ref, rows_ref):
    cells, rows = 2 * HEADS, 2 * HEADS * COV
    back = back_ref[...].astype(F32)

    def pad(x):
        return jnp.concatenate([x, jnp.zeros((cells, COV - MID, WIDTH), F32)], 1).reshape(rows, WIDTH)

    def own(at):
        return pad(back[:, at * MID : (at + 1) * MID])

    def both(at):
        x = back[:, at * MID : (at + 2) * MID].reshape(HEADS, 2, COV, WIDTH)
        return pad((x[:, 0] + x[:, 1]).reshape(cells, MID, WIDTH))

    def spread(x):
        return jnp.broadcast_to(x.reshape(cells, 1, WIDTH), (cells, COV, WIDTH)).reshape(rows, WIDTH)

    row = iota((COV, WIDTH), 0)
    is_far = []
    for head in range(HEADS):
        off_three = off3_ref[head]
        twice = (off_three % DILATION_TWO) == off2_ref[head]
        is_far += [(row == jnp.where(twice, off_three // DILATION_TWO, MID)).astype(F32)] * 2
    is_far = jnp.concatenate(is_far, 0) > 0.0
    is_mid = jnp.concatenate([row] * cells, 0) < MID
    ones = (iota((WIDTH, WIDTH), 0) < 3).astype(BF16)

    def joined(x):
        return dot_nn(x.astype(BF16), ones)

    q, g, out, lse1, delta1, dq_one, dq_two = (cov_ref[at].reshape(rows, WIDTH) for at in range(KEPT))
    packed = back[:, 7 * MID : 8 * MID]
    far = packed[:, 3:7].reshape(HEADS, 2, 4, WIDTH)
    far = (far[:, 0] + far[:, 1]).reshape(HEADS, 2, 2, WIDTH)
    lse2 = jnp.where(is_mid, joined(own(6)), NEG)
    lse3 = jnp.where(is_far, joined(spread(packed[:, 2:3])), NEG)
    lse = merge_lse([lse1, lse2, lse3])
    share = jnp.exp(lse1 - lse)
    att = (
        share * out + jnp.exp(lse2 - lse) * own(5) + jnp.exp(lse3 - lse) * spread(packed[:, 1:2])
    ).astype(BF16)
    delta = jnp.sum(g * att.astype(F32), axis=1, keepdims=True)
    change = share * (delta - delta1)
    dq = share * dq_one - change * dq_two + own(4) + jnp.where(is_far, spread(packed[:, 0:1]), 0.0)
    dk = both(0) + jnp.where(is_far, spread(far[:, 0]), 0.0)
    dv = both(2) + jnp.where(is_far, spread(far[:, 1]), 0.0)

    def put(at, column, x):
        right_ref[:, at * COV : (at + 1) * COV, column * WIDTH : (column + 1) * WIDTH] = x.astype(BF16).reshape(
            cells, COV, WIDTH
        )

    def put_two(column, x):
        high = x.astype(BF16)
        put(2, column, high)
        put(3, column, x - high.astype(F32))

    rows_ref[0] = att.astype(F32).reshape(HEADS, 2, COV, WIDTH)
    rows_ref[1] = (FACTOR * dq).reshape(HEADS, 2, COV, WIDTH)
    put(0, 0, share * q)
    put(1, 0, -change * q)
    put_two(0, dk)
    put(0, 1, jnp.zeros((rows, WIDTH), F32))
    put(1, 1, share * g)
    put_two(1, dv)


def patch(off_two, off_three, rows_ref, head, at, slab_ref, other_ref):
    half = off_two // HALF
    twice = (off_three % DILATION_TWO) == off_two
    beside = ((off_three % DILATION_TWO) // HALF) == half
    mid = rows_ref[at, head, :, :MID].reshape(2 * MID, 1, WIDTH)
    far = rows_ref[at, head, :, MID : MID + 1]
    shape = (2 * MID, HALF, WIDTH)
    row = iota(shape, 1)
    old = slab_ref[at, head].astype(F32).reshape(shape)
    here = (row == off_three % HALF) & ((iota(shape, 0) & (MID - 1)) == off_three // DILATION_TWO)
    here = here & beside & jnp.logical_not(twice)
    wide = jnp.broadcast_to(far, (2, MID, WIDTH)).reshape(2 * MID, 1, WIDTH)
    slab = jnp.where(here, wide, jnp.where(row == off_two % HALF, mid, old))
    slab_ref[at, head] = slab.astype(BF16).reshape(2, MID, HALF, WIDTH)
    there = (iota((2, HALF, WIDTH), 1) == off_three % HALF) & jnp.logical_not(beside)
    other_ref[at, head] = jnp.where(there, far, other_ref[at, head].astype(F32)).astype(BF16)


def finish_kernel(
    off2_ref, off3_ref, cov_hbm, back_hbm, left_hbm, att_hbm, dq_hbm, dk_hbm, dv_hbm,
    att_out, dq_out, dk_out, dv_out,
    cov_ref, back_ref, left_ref, right_ref, rows_ref, held, done_ref, slab_ref, other_ref,
    first_sems, in_sems, out_sems, slab_in, slab_out,
):
    first = [
        pltpu.make_async_copy(source, target, first_sems.at[at])
        for at, (source, target) in enumerate(((back_hbm, back_ref), (cov_hbm, cov_ref)))
    ]

    def slabs(head, arrays):
        half, period = off2_ref[head] // HALF, off3_ref[head] // DILATION_TWO
        lane = pl.ds(pl.multiple_of(head * WIDTH, WIDTH), WIDTH)
        pairs = []
        for at, array in enumerate(arrays):
            pairs.append((array.at[:, :, half, :, lane], slab_ref.at[at, head]))
            pairs.append((array.at[:, period, 1 - half, :, lane], other_ref.at[at, head]))
        return pairs

    def loads(head):
        pairs = slabs(head, (att_hbm, dq_hbm))
        copies = [pltpu.make_async_copy(*pair, slab_in.at[head, at]) for at, pair in enumerate(pairs)]
        pairs = [(dk_hbm.at[head], held.at[0, head]), (dv_hbm.at[head], held.at[1, head])]
        pairs.append((left_hbm.at[head], left_ref.at[head]))
        return copies + [pltpu.make_async_copy(*pair, in_sems.at[head, at]) for at, pair in enumerate(pairs)]

    def slab_stores(head):
        pairs = slabs(head, (att_out, dq_out))
        return [
            pltpu.make_async_copy(source, target, slab_out.at[head, at]) for at, (target, source) in enumerate(pairs)
        ]

    def stores(head):
        lane = pl.ds(pl.multiple_of(head * WIDTH, WIDTH), WIDTH)
        return [
            pltpu.make_async_copy(done_ref.at[at, head], out.at[:, lane], out_sems.at[head, at])
            for at, out in enumerate((dk_out, dv_out))
        ]

    for copy in first:
        copy.start()

    @pl.loop(0, HEADS)
    def _(head):
        for copy in loads(head):
            copy.start()

    for copy in first:
        copy.wait()
    prepare(off2_ref, off3_ref, cov_ref, back_ref, right_ref, rows_ref)

    @pl.loop(0, HEADS)
    def _(head):
        for copy in loads(head):
            copy.wait()
        for at in range(2):
            patch(off2_ref[head], off3_ref[head], rows_ref, head, at, slab_ref, other_ref)
        for copy in slab_stores(head):
            copy.start()
        for t in range(2):
            rows = slice(t * SEG1, (t + 1) * SEG1)
            x = dot_nn(left_ref[head, t], right_ref[2 * head + t])
            done_ref[0, head, rows, :] = (FACTOR * (held[0, head, rows, :].astype(F32) + x[:, :WIDTH])).astype(BF16)
            done_ref[1, head, rows, :] = (held[1, head, rows, :].astype(F32) + x[:, WIDTH:]).astype(BF16)
        for copy in stores(head):
            copy.start()

    @pl.loop(0, HEADS)
    def _(head):
        for copy in slab_stores(head) + stores(head):
            copy.wait()


def finish(offsets, cov, left, back, att, dq, dk, dv):
    smem, hbm = pl.BlockSpec(memory_space=pltpu.SMEM), pl.BlockSpec(memory_space=pl.ANY)
    kind = (2, HEADS, 2 * SEG1, WIDTH)
    whole = (2 * SEG1, HEADS * WIDTH)
    att, dq, dk, dv = pl.pallas_call(
        finish_kernel,
        in_specs=[smem, smem] + [hbm] * 7,
        out_specs=[hbm] * 4,
        out_shape=[jax.ShapeDtypeStruct(att.shape, BF16)] * 2 + [jax.ShapeDtypeStruct(whole, BF16)] * 2,
        input_output_aliases={5: 0, 6: 1},
        scratch_shapes=[pltpu.VMEM(x.shape, x.dtype) for x in (cov, back, left)]
        + [
            pltpu.VMEM((2 * HEADS, 4 * COV, 2 * WIDTH), BF16),
            pltpu.VMEM((2, HEADS, 2, COV, WIDTH), F32),
            pltpu.VMEM(kind, BF16),
            pltpu.VMEM(kind, BF16),
            pltpu.VMEM((2, HEADS, 2, MID, HALF, WIDTH), BF16),
            pltpu.VMEM((2, HEADS, 2, HALF, WIDTH), BF16),
            pltpu.SemaphoreType.DMA((2,)),
            pltpu.SemaphoreType.DMA((HEADS, 3)),
            pltpu.SemaphoreType.DMA((HEADS, 2)),
            pltpu.SemaphoreType.DMA((HEADS, 4)),
            pltpu.SemaphoreType.DMA((HEADS, 4)),
        ],
        compiler_params=pltpu.CompilerParams(vmem_limit_bytes=VMEM),
        cost_estimate=pl.CostEstimate(flops=2**30, bytes_accessed=17 * 2**20, transcendentals=2**18),
        name="finish",
    )(*offsets, cov, back, left, att, dq, dk, dv)
    return att.reshape(whole), dq.reshape(whole), dk, dv


def solution(mesh):
    outer = mesh.shape["outer"]
    split = P(("outer", "inner"), None)

    def body(queries, keys, values, out_grad, middle_head_offsets, distant_head_offsets):
        offsets = (middle_head_offsets, distant_head_offsets)
        arrays = (queries, keys, values, out_grad)
        send, cov, left = extract(offsets, *arrays)
        got = lax.all_to_all(send, "inner", 0, 0)
        parts = local(offsets, arrays, 0, SHARES[0], ())
        got, *parts = lax.optimization_barrier((got, *parts))
        far, out, figures = remote_forward(offsets, got, outer)
        far, *parts = lax.optimization_barrier((far, *parts))
        far = lax.all_to_all(far, "outer", 0, 0)
        parts = local(offsets, arrays, SHARES[0], SHARES[1], parts)
        far, *parts = lax.optimization_barrier((far, *parts))
        back = remote_backward(offsets, got, far, out, figures)
        back, *parts = lax.optimization_barrier((back, *parts))
        back = lax.all_to_all(back, "inner", 0, 0)
        parts = local(offsets, arrays, SHARES[0] + SHARES[1], SHARES[2], parts)
        back, *parts = lax.optimization_barrier((back, *parts))
        return finish(offsets, cov, left, back, *parts)

    return jax.shard_map(
        body, mesh=mesh, in_specs=(split,) * 4 + (P(), P()), out_specs=(split,) * 4, check_vma=False
    )
```

```python
import math

import jax
import jax.numpy as jnp
from jax import lax
from jax.experimental import pallas as pl
from jax.experimental.pallas import tpu as pltpu
from jax.sharding import PartitionSpec as P

SEG1 = 512
DILATION_TWO = 32
DILATION_THREE = 512
HEADS = 8
WIDTH = 128
FACTOR = WIDTH ** (-0.5)
MID = SEG1 // DILATION_TWO
COV = 32
PACK = 128
EXTRACT_HEADS = 2
SHARES = (3, 2, 3)
VMEM = 44 * 2**20
HALF = DILATION_TWO // 2
NEG = -1e30
F32 = jnp.float32
BF16 = jnp.bfloat16


def dot_nn(a, b):
    return lax.dot_general(a, b, (((1,), (0,)), ((), ())), preferred_element_type=F32)


def dot_nt(a, b):
    return lax.dot_general(a, b, (((1,), (1,)), ((), ())), preferred_element_type=F32)


def dot_tn(a, b):
    return lax.dot_general(a, b, (((0,), (0,)), ((), ())), preferred_element_type=F32)


def iota(shape, dim):
    return lax.broadcasted_iota(jnp.int32, shape, dim)


def split3(x):
    high = x.astype(BF16).astype(F32)
    rest = x - high
    middle = rest.astype(BF16).astype(F32)
    return high, middle, (rest - middle).astype(BF16).astype(F32)


def lanes(columns, rows):
    lane = iota((rows, WIDTH), 1)
    out = jnp.zeros((rows, WIDTH), F32)
    for j, column in enumerate(columns):
        out = jnp.where(lane == j, column, out)
    return out


def join3(x, at):
    return x[:, at : at + 1] + x[:, at + 1 : at + 2] + x[:, at + 2 : at + 3]


def targets(shape, dim, off_two, off_three):
    j = iota(shape, dim) % COV
    return jnp.where(j < MID, DILATION_TWO * j + off_two, jnp.where(j == MID, off_three, -1))


def in_hbm(arrays):
    return [pltpu.with_memory_space_constraint(x, pltpu.HBM) for x in arrays]


def extract_kernel(
    off2_ref, off3_ref, q_hbm, k_hbm, v_hbm, g_hbm, send_hbm, cov_hbm, low_hbm, left_hbm,
    q_all, k_all, v_all, g_all, send_ref, cov_ref, low_ref, left_ref, sems, out_sems,
):
    n = EXTRACT_HEADS

    def loads(step):
        lane = pl.ds(pl.multiple_of(step * n * WIDTH, n * WIDTH), n * WIDTH)
        pairs = ((q_hbm, q_all), (k_hbm, k_all), (v_hbm, v_all), (g_hbm, g_all))
        return [
            pltpu.make_async_copy(source.at[:, :, :, lane], target.at[step], sems.at[step, at])
            for at, (source, target) in enumerate(pairs)
        ]

    def places(step):
        heads = pl.ds(step * n, n)
        return (pl.ds(step * 2 * n, 2 * n),), (slice(None), heads), (slice(None), heads), (heads,)

    scratch = (send_ref, cov_ref, low_ref, left_ref)

    def stores(step):
        pairs = zip(scratch, (send_hbm, cov_hbm, low_hbm, left_hbm), places(step))
        return [
            pltpu.make_async_copy(source.at[place], target.at[place], out_sems.at[step, at])
            for at, (source, target, place) in enumerate(pairs)
        ]

    @pl.loop(0, HEADS // n)
    def _(step):
        for copy in loads(step):
            copy.start()

    @pl.loop(0, HEADS // n)
    def _(step):
        for copy in loads(step):
            copy.wait()
        here = [ref.at[step] for ref in (q_all, k_all, v_all, g_all)]
        out = [ref.at[place] for ref, place in zip(scratch, places(step))]
        extract_heads(step * n, off2_ref, off3_ref, *here, *out)
        for copy in stores(step):
            copy.start()

    @pl.loop(0, HEADS // n)
    def _(step):
        for copy in stores(step):
            copy.wait()


def extract_heads(first_head, off2_ref, off3_ref, q_ref, k_ref, v_ref, g_ref, send_ref, cov_ref, low_ref, left_ref):
    cells = [(i, t) for i in range(EXTRACT_HEADS) for t in range(2)]

    def block(ref, cell):
        i, t = cell
        return ref[t * MID : (t + 1) * MID, :, :, i * WIDTH : (i + 1) * WIDTH].reshape(SEG1, WIDTH)

    def pick(cell):
        i, t = cell
        off_two, off_three = off2_ref[first_head + i], off3_ref[first_head + i]
        lane = slice(i * WIDTH, (i + 1) * WIDTH)
        refs = (q_ref, k_ref, v_ref, g_ref)
        slabs = [ref[t * MID : (t + 1) * MID, off_two // HALF, :, lane].reshape(MID * HALF, WIDTH) for ref in refs]
        place = t * MID + off_three // DILATION_TWO
        others = [ref[place, (off_three % DILATION_TWO) // HALF, :, lane] for ref in refs]
        select = iota((MID, MID * HALF), 1) == HALF * iota((MID, 1), 0) + off_two % HALF
        select_far = (iota((MID, HALF), 1) == off_three % HALF) & (iota((MID, HALF), 0) == 0)
        return jnp.concatenate(
            [
                dot_nn(select.astype(BF16), jnp.concatenate(slabs, 1)),
                dot_nn(select_far.astype(BF16), jnp.concatenate(others, 1)),
            ],
            0,
        )

    valids = []
    row = iota((COV, 1), 0)
    for i in range(EXTRACT_HEADS):
        twice = (off3_ref[first_head + i] % DILATION_TWO) == off2_ref[first_head + i]
        valids.append(((row < MID) | ((row == MID) & jnp.logical_not(twice))).astype(F32))
    picked = [pick(cell) for cell in cells]
    low = [x.astype(BF16) for x in picked]
    scores = [dot_nt(x[:, :WIDTH], block(k_ref, cell)) for x, cell in zip(low, cells)]
    grads = [dot_nt(x[:, 3 * WIDTH :], block(v_ref, cell)) for x, cell in zip(low, cells)]
    scores, grads = jnp.concatenate(scores, 0) * FACTOR, jnp.concatenate(grads, 0)
    top = jnp.max(scores, axis=1, keepdims=True)
    weight = jnp.exp(scores - top)
    total = jnp.sum(weight, axis=1, keepdims=True)
    weight_low = weight.astype(BF16)
    out = jnp.concatenate(
        [dot_nn(weight_low[n * COV : (n + 1) * COV], block(v_ref, cell)) for n, cell in enumerate(cells)], 0
    ) / total
    lse = top + jnp.log(total)
    g_cov = jnp.concatenate([x[:, 3 * WIDTH :] for x in picked], 0)
    delta = jnp.sum(g_cov * out, axis=1, keepdims=True)
    stats = lanes(split3(lse) + split3(delta), COV * len(cells))
    shown = lanes([lse, delta], COV * len(cells))
    prob = weight * (jnp.concatenate([valids[i] for i, _ in cells], 0) / total)
    dscore = (prob * (grads - delta)).astype(BF16)
    prob = prob.astype(BF16)
    first = iota((MID, 1), 0) == 0
    for n, (i, t) in enumerate(cells):
        rows = slice(n * COV, (n + 1) * COV)
        own = stats[rows]
        for c in range(2):
            send_ref[2 * i + c, t * MID : (t + 1) * MID, :] = low[n][:MID, WIDTH : 2 * WIDTH]
            send_ref[2 * i + c, 2 * MID + t * MID : 2 * MID + (t + 1) * MID, :] = low[n][:MID, 2 * WIDTH : 3 * WIDTH]
        send_ref[2 * i + t, 4 * MID : 5 * MID, :] = low[n][:MID, :WIDTH]
        send_ref[2 * i + t, 5 * MID : 6 * MID, :] = low[n][:MID, 3 * WIDTH :]
        send_ref[2 * i + t, 6 * MID : 7 * MID, :] = own[:MID].astype(BF16)
        mine = (picked[n][MID:, :WIDTH], picked[n][MID:, 3 * WIDTH :], jnp.where(first, own[MID:], 0.0))
        pair = [picked[n - t + u][MID:, at * WIDTH : (at + 1) * WIDTH] for at in (1, 2) for u in range(2)]
        far_block = pair[0]
        for at, x in enumerate((*pair[1:], *mine)):
            far_block = far_block + pltpu.roll(x, at + 1, 0)
        send_ref[2 * i + t, 7 * MID :, :] = far_block.astype(BF16)
        both = dot_nn(jnp.concatenate([dscore[rows], prob[rows]], 0), block(k_ref, (i, t)))
        for at, x in enumerate((out[rows], both[:COV], both[COV:], shown[rows])):
            cov_ref[at, i, t] = x
        low_ref[0, i, t] = low[n][:, :WIDTH]
        low_ref[1, i, t] = low[n][:, 3 * WIDTH :]
    for i in range(EXTRACT_HEADS):
        parts = [x[n * COV : (n + 1) * COV] for n in (2 * i, 2 * i + 1) for x in (dscore, prob)]
        left_ref[i] = jnp.concatenate(parts, 0).T


def extract(offsets, q, k, v, g):
    smem, hbm = pl.BlockSpec(memory_space=pltpu.SMEM), pl.BlockSpec(memory_space=pl.ANY)
    steps = HEADS // EXTRACT_HEADS
    period = (2 * MID, 2, HALF)
    shapes = [
        ((2 * HEADS, PACK, WIDTH), BF16),
        ((4, HEADS, 2, COV, WIDTH), F32),
        ((2, HEADS, 2, COV, WIDTH), BF16),
        ((HEADS, SEG1, 4 * COV), BF16),
    ]
    return pl.pallas_call(
        extract_kernel,
        in_specs=[smem, smem] + [hbm] * 4,
        out_specs=[hbm] * 4,
        out_shape=[pltpu.HBM(*x) for x in shapes],
        scratch_shapes=[pltpu.VMEM((steps, *period, EXTRACT_HEADS * WIDTH), BF16)] * 4
        + [pltpu.VMEM(*x) for x in shapes]
        + [pltpu.SemaphoreType.DMA((steps, 4))] * 2,
        compiler_params=pltpu.CompilerParams(vmem_limit_bytes=63 * 2**20),
        cost_estimate=pl.CostEstimate(flops=2**32, bytes_accessed=12 * 2**20, transcendentals=2**18),
        name="extract",
    )(*offsets, *in_hbm([x.reshape(*period, HEADS * WIDTH) for x in (q, k, v, g)]))


def local_kernel(first, count, kept, off2_ref, off3_ref, *refs):
    sources, outs = refs[:4], refs[4 + kept : 8 + kept]
    held, done, (in_sems, out_sems) = refs[8 + kept : 12 + kept], refs[12 + kept : 16 + kept], refs[16 + kept :]
    position = iota((1, SEG1), 1)

    def loads(i, t):
        rows = pl.ds(t * SEG1, SEG1)
        lane = pl.ds(pl.multiple_of((first + i) * WIDTH, WIDTH), WIDTH)
        return [
            pltpu.make_async_copy(sources[at].at[rows, lane], held[at].at[i, rows], in_sems.at[i, t, at])
            for at in range(4)
        ]

    def stores(i, t):
        lane = pl.ds(pl.multiple_of((first + i) * WIDTH, WIDTH), WIDTH)
        rows = pl.ds(t * SEG1, SEG1)
        return [
            pltpu.make_async_copy(
                done[at].at[i, t], outs[at].at[t, :, :, :, lane] if at < 2 else outs[at].at[first + i, rows],
                out_sems.at[i, t, at],
            )
            for at in range(4)
        ]

    def start(i):
        for t in range(2):
            for copy in loads(i, t):
                copy.start()

    start(0)

    @pl.loop(0, count)
    def _(i):
        @pl.when(i + 1 < count)
        def _():
            start(i + 1)

        head = first + i
        covered = ((position & (DILATION_TWO - 1)) == off2_ref[head]) | (position == off3_ref[head])
        for t in range(2):
            for copy in loads(i, t):
                copy.wait()
            rows = slice(t * SEG1, (t + 1) * SEG1)
            q, k, v, g = (ref[i, rows, :] for ref in held)
            scores = dot_nt(k, q) * (FACTOR * math.log2(math.e))
            grad = dot_nt(v, g)
            weight = jnp.exp2(scores - jnp.max(scores, axis=0, keepdims=True))
            inverse = 1.0 / jnp.sum(weight, axis=0, keepdims=True)
            att = (dot_nn(v.T, weight.astype(BF16)) * inverse).astype(BF16)
            delta = jnp.sum(g.T.astype(F32) * att.astype(F32), axis=0, keepdims=True)
            done[0][i, t] = att.T.reshape(MID, 2, HALF, WIDTH)
            prob = weight * jnp.where(covered, 0.0, inverse)
            dscore = (prob * (grad - delta)).astype(BF16)
            done[1][i, t] = (dot_nn(k.T, dscore) * FACTOR).astype(BF16).T.reshape(MID, 2, HALF, WIDTH)
            done[2][i, t] = dot_nn(dscore, q).astype(BF16)
            done[3][i, t] = dot_nn(prob.astype(BF16), g).astype(BF16)
            for copy in stores(i, t):
                copy.start()

    @pl.loop(0, count)
    def _(i):
        for t in range(2):
            for copy in stores(i, t):
                copy.wait()


def local(offsets, arrays, first, count, earlier):
    smem, hbm = pl.BlockSpec(memory_space=pltpu.SMEM), pl.BlockSpec(memory_space=pl.ANY)
    share = count / HEADS
    period = (MID, 2, HALF)
    return pl.pallas_call(
        lambda *refs: local_kernel(first, count, len(earlier), *refs),
        in_specs=[smem, smem] + [hbm] * (4 + len(earlier)),
        out_specs=[hbm] * 4,
        out_shape=[pltpu.HBM((2, *period, HEADS * WIDTH), BF16)] * 2 + [pltpu.HBM((HEADS, 2 * SEG1, WIDTH), BF16)] * 2,
        input_output_aliases={6 + at: at for at in range(len(earlier))},
        scratch_shapes=[pltpu.VMEM((count, 2 * SEG1, WIDTH), BF16)] * 4
        + [pltpu.VMEM((count, 2, *period, WIDTH), BF16)] * 2
        + [pltpu.VMEM((count, 2, SEG1, WIDTH), BF16)] * 2
        + [pltpu.SemaphoreType.DMA((count, 2, 4))] * 2,
        compiler_params=pltpu.CompilerParams(vmem_limit_bytes=VMEM),
        cost_estimate=pl.CostEstimate(
            flops=int(share * 12 * 2**30), bytes_accessed=int(share * 16 * 2**20), transcendentals=int(share * 2**22)
        ),
        name="local",
    )(*offsets, *in_hbm((*arrays, *earlier)))


def merge_lse(parts):
    top = parts[0]
    for part in parts[1:]:
        top = jnp.maximum(top, part)
    total = jnp.exp(parts[0] - top)
    for part in parts[1:]:
        total = total + jnp.exp(part - top)
    return top + jnp.log(total)


def part(ref, at, rows):
    return ref[:, at * MID : at * MID + rows, :].reshape(ref.shape[0] * rows, WIDTH)


def far_places(shape, dim, starts):
    j = iota(shape, dim)
    n = shape[dim] // 7
    place = jnp.zeros(shape, jnp.int32)
    for at, start in enumerate(starts):
        if at < 2:
            u = j - 2 * n * at
            place = jnp.where((u >= 0) & (u < 2 * n), MID * (u // 2) + u % 2 + start, place)
        else:
            u = j - n * (at + 2)
            place = jnp.where((u >= 0) & (u < n), MID * u + start, place)
    return place


def forward_kernel(off2_ref, off3_ref, in_ref, far_ref, out_ref, figures_ref):
    head = lax.axis_index("inner") // 2
    off_three = off3_ref[head]
    n = in_ref.shape[0]
    k, v, q, g = part(in_ref, 0, 2 * MID), part(in_ref, 2, 2 * MID), part(in_ref, 4, MID), part(in_ref, 5, MID)
    queries = n * MID
    scores = dot_nt(q, k) * FACTOR
    top = jnp.max(scores, axis=1, keepdims=True)
    weight = jnp.exp(scores - top)
    total = jnp.sum(weight, axis=1, keepdims=True)
    out = dot_nn(weight.astype(BF16), v) / total
    lse = jnp.broadcast_to(top + jnp.log(total), (queries, WIDTH))
    delta = jnp.broadcast_to(jnp.sum(g.astype(F32) * out, axis=1, keepdims=True), (queries, WIDTH))
    out_ref[...] = out.astype(BF16)
    figures_ref[...] = lanes([lse, delta], queries)
    pick = (iota((7 * n, queries), 1) == far_places((7 * n, 1), 0, (0, 2, 4, 5, 6))).astype(BF16)
    picked = dot_nn(pick, part(in_ref, 7, MID))
    stats = picked[6 * n :]
    same = ((off_three % DILATION_TWO) == off2_ref[head]) & (
        iota((n, MID, WIDTH), 1) == off_three // DILATION_TWO
    )
    lse1, delta1 = join3(stats, 0), join3(stats, 3)
    lse2 = jnp.max(jnp.where(same, lse.reshape(n, MID, WIDTH), NEG), axis=1)
    delta2 = jnp.sum(jnp.where(same, delta.reshape(n, MID, WIDTH), 0.0), axis=1)
    both = merge_lse([lse1, lse2])
    delta = jnp.exp(lse1 - both) * delta1 + jnp.exp(lse2 - both) * delta2
    rows = jnp.concatenate([picked[: 6 * n], lanes(split3(both) + split3(delta), n)], 0).astype(BF16)
    for o in range(far_ref.shape[0]):
        far_ref[o] = rows


def backward_kernel(off2_ref, off3_ref, in_ref, far_ref, out2_ref, figures_ref, out_ref, key_ref, query_ref):
    head, outer = lax.axis_index("inner") // 2, lax.axis_index("outer")
    off_three = off3_ref[head]
    n = in_ref.shape[0]
    queries = n * MID
    turn = (iota((8, WIDTH), 0) == iota((8, WIDTH), 1)).astype(BF16)
    kf, vf = part(far_ref, 0, 2 * MID), part(far_ref, 2, 2 * MID)
    qf, gf = part(far_ref, 4, MID), part(far_ref, 5, MID)
    figures = dot_nt(turn, part(far_ref, 6, MID))
    lse12 = figures[0:1] + figures[1:2] + figures[2:3]
    delta12 = figures[3:4] + figures[4:5] + figures[5:6]
    scores = dot_nt(kf, qf) * FACTOR
    grads = dot_nt(vf, gf)
    top = jnp.max(scores, axis=0, keepdims=True)
    weight = jnp.exp(scores - top)
    total = jnp.sum(weight, axis=0, keepdims=True)
    lse3 = top + jnp.log(total)
    share = weight / total
    delta3 = jnp.sum(share * grads, axis=0, keepdims=True)
    lse = merge_lse([lse12, lse3])
    delta = jnp.exp(lse12 - lse) * delta12 + jnp.exp(lse3 - lse) * delta3
    prob = jnp.exp(scores - lse)
    dscore = (prob * (grads - delta)).astype(BF16)
    key_ref[0] = dot_nn(dscore, qf)
    key_ref[1] = dot_nn(prob.astype(BF16), gf)
    query_ref[0] = dot_tn(dscore, kf)
    query_ref[1] = dot_tn(share.astype(BF16), vf)
    eight = iota((8, lse3.shape[1]), 0)
    figures = jnp.zeros(eight.shape, F32)
    for at, x in enumerate(split3(lse3) + split3(delta3)):
        figures = jnp.where(eight == at, x, figures)
    query_ref[2] = dot_tn(figures.astype(BF16), turn)
    own_keys = pl.ds(pl.multiple_of(outer * 2 * n, 2 * n), 2 * n)
    own_queries = pl.ds(pl.multiple_of(outer * n, n), n)
    own = [key_ref[0, own_keys, :], key_ref[1, own_keys, :]] + [query_ref[at, own_queries, :] for at in range(3)]
    unpick = (iota((queries, 7 * n), 0) == far_places((1, 7 * n), 1, (3, 5, 0, 1, 2))).astype(BF16)
    packed = dot_nn(unpick, jnp.concatenate(own, 0).astype(BF16))
    same = ((off_three % DILATION_TWO) == off2_ref[head]) & (
        iota((n, MID, WIDTH), 1) == off_three // DILATION_TWO
    )

    def expand(column, other):
        wide = jnp.broadcast_to(jnp.broadcast_to(column, (n, WIDTH)).reshape(n, 1, WIDTH), (n, MID, WIDTH))
        return jnp.where(same, wide, other).reshape(queries, WIDTH)[:, 0:1]

    lse3, delta3 = expand(join3(own[4], 0), NEG), expand(join3(own[4], 3), 0.0)
    stats = part(in_ref, 6, MID).astype(F32)
    lse1, delta1 = join3(stats, 0), join3(stats, 3)
    lse2, delta2 = figures_ref[:, 0:1], figures_ref[:, 1:2]
    lse = merge_lse([lse1, lse2, lse3])
    delta = jnp.exp(lse1 - lse) * delta1 + jnp.exp(lse2 - lse) * delta2 + jnp.exp(lse3 - lse) * delta3
    k, v, q, g = part(in_ref, 0, 2 * MID), part(in_ref, 2, 2 * MID), part(in_ref, 4, MID), part(in_ref, 5, MID)
    prob = jnp.exp(dot_nt(q, k) * FACTOR - lse)
    dscore = (prob * (dot_nt(g, v) - delta)).astype(BF16)

    def give(at, rows, value):
        out_ref[:, at * MID : at * MID + rows, :] = value.astype(BF16).reshape(n, rows, WIDTH)

    give(0, 2 * MID, dot_tn(dscore, q))
    give(2, 2 * MID, dot_tn(prob.astype(BF16), g))
    give(4, MID, dot_nn(dscore, k))
    give(5, MID, out2_ref[...])
    give(6, MID, lanes(split3(lse2), queries))
    give(7, MID, packed)


def remote_call(kernel, offsets, arrays, shapes, scratch, name):
    vmem, smem = pl.BlockSpec(memory_space=pltpu.VMEM), pl.BlockSpec(memory_space=pltpu.SMEM)
    return pl.pallas_call(
        kernel,
        in_specs=[smem, smem] + [vmem] * len(arrays),
        out_specs=[vmem] * len(shapes),
        out_shape=shapes,
        scratch_shapes=[pltpu.VMEM(*x) for x in scratch],
        compiler_params=pltpu.CompilerParams(vmem_limit_bytes=VMEM),
        cost_estimate=pl.CostEstimate(flops=2**31, bytes_accessed=2**21, transcendentals=2**19),
        name=name,
    )(*offsets, *arrays)


def remote_forward(offsets, received, outer):
    n = received.shape[0]
    rows = n * MID
    return remote_call(
        forward_kernel, offsets, (received,),
        [jax.ShapeDtypeStruct((outer, 7 * n, WIDTH), BF16), jax.ShapeDtypeStruct((rows, WIDTH), BF16),
         jax.ShapeDtypeStruct((rows, WIDTH), F32)],
        [], "remote_forward",
    )


def remote_backward(offsets, received, far, out, figures):
    n, outer = received.shape[0], far.shape[0]
    return remote_call(
        backward_kernel, offsets, (received, far, out, figures), [jax.ShapeDtypeStruct(received.shape, BF16)],
        [((2, outer * 2 * n, WIDTH), F32), ((3, outer * n, WIDTH), F32)], "remote_backward",
    )[0]


def prepare(off2_ref, off3_ref, cov_ref, low_ref, back_ref, right_ref, rows_ref):
    cells, rows = 2 * HEADS, 2 * HEADS * COV
    back = back_ref[...].astype(F32)

    def pad(x):
        return jnp.concatenate([x, jnp.zeros((cells, COV - MID, WIDTH), F32)], 1).reshape(rows, WIDTH)

    def own(at):
        return pad(back[:, at * MID : (at + 1) * MID])

    def both(at):
        x = back[:, at * MID : (at + 2) * MID].reshape(HEADS, 2, COV, WIDTH)
        return pad((x[:, 0] + x[:, 1]).reshape(cells, MID, WIDTH))

    def spread(x):
        return jnp.broadcast_to(x.reshape(cells, 1, WIDTH), (cells, COV, WIDTH)).reshape(rows, WIDTH)

    row = iota((COV, WIDTH), 0)
    is_far = []
    for head in range(HEADS):
        off_three = off3_ref[head]
        twice = (off_three % DILATION_TWO) == off2_ref[head]
        is_far += [(row == jnp.where(twice, off_three // DILATION_TWO, MID)).astype(F32)] * 2
    is_far = jnp.concatenate(is_far, 0) > 0.0
    is_mid = jnp.concatenate([row] * cells, 0) < MID
    ones = (iota((WIDTH, WIDTH), 0) < 3).astype(BF16)

    def joined(x):
        return dot_nn(x.astype(BF16), ones)

    q, g = (low_ref[at].reshape(rows, WIDTH).astype(F32) for at in range(2))
    out, dq_one, dq_two, figures = (cov_ref[at].reshape(rows, WIDTH) for at in range(4))
    lse1, delta1 = figures[:, 0:1], figures[:, 1:2]
    packed = back[:, 7 * MID : 8 * MID]
    far = packed[:, 3:7].reshape(HEADS, 2, 4, WIDTH)
    far = (far[:, 0] + far[:, 1]).reshape(HEADS, 2, 2, WIDTH)
    lse2 = jnp.where(is_mid, joined(own(6)), NEG)
    lse3 = jnp.where(is_far, joined(spread(packed[:, 2:3])), NEG)
    lse = merge_lse([lse1, lse2, lse3])
    share = jnp.exp(lse1 - lse)
    att = (
        share * out + jnp.exp(lse2 - lse) * own(5) + jnp.exp(lse3 - lse) * spread(packed[:, 1:2])
    ).astype(BF16)
    delta = jnp.sum(g * att.astype(F32), axis=1, keepdims=True)
    change = share * (delta - delta1)
    dq = share * dq_one - change * dq_two + own(4) + jnp.where(is_far, spread(packed[:, 0:1]), 0.0)
    dk = both(0) + jnp.where(is_far, spread(far[:, 0]), 0.0)
    dv = both(2) + jnp.where(is_far, spread(far[:, 1]), 0.0)

    def column(at):
        return slice(at * WIDTH, (at + 1) * WIDTH)

    def put(at, to, x):
        x = x.astype(BF16).reshape(HEADS, 2, COV, WIDTH)
        for t in range(2):
            start = (2 * t + at) * COV
            right_ref[:, t, start : start + COV, column(to)] = x[:, t]

    def put_rows(to, x):
        high = x.astype(BF16)
        for at, part_ in enumerate((high, (x - high.astype(F32)).astype(BF16))):
            start = (4 + at) * COV
            right_ref[:, :, start : start + COV, column(to)] = part_.reshape(HEADS, 2, COV, WIDTH)

    rows_ref[0] = att.astype(F32).reshape(HEADS, 2, COV, WIDTH)
    rows_ref[1] = (FACTOR * dq).reshape(HEADS, 2, COV, WIDTH)
    nothing = jnp.zeros((HEADS, 2 * COV, 2 * WIDTH), BF16)
    right_ref[:, 0, 2 * COV : 4 * COV, :] = nothing
    right_ref[:, 1, : 2 * COV, :] = nothing
    put(0, 0, share * q)
    put(1, 0, -change * q)
    put_rows(0, dk)
    put(0, 1, jnp.zeros((rows, WIDTH), F32))
    put(1, 1, share * g)
    put_rows(1, dv)


def patch(off_two, off_three, rows_ref, head, at, slab_ref, other_ref):
    half = off_two // HALF
    twice = (off_three % DILATION_TWO) == off_two
    beside = ((off_three % DILATION_TWO) // HALF) == half
    mid = rows_ref[at, head, :, :MID].reshape(2 * MID, 1, WIDTH)
    far = rows_ref[at, head, :, MID : MID + 1]
    shape = (2 * MID, HALF, WIDTH)
    row = iota(shape, 1)
    old = slab_ref[at, head].astype(F32).reshape(shape)
    here = (row == off_three % HALF) & ((iota(shape, 0) & (MID - 1)) == off_three // DILATION_TWO)
    here = here & beside & jnp.logical_not(twice)
    wide = jnp.broadcast_to(far, (2, MID, WIDTH)).reshape(2 * MID, 1, WIDTH)
    slab = jnp.where(here, wide, jnp.where(row == off_two % HALF, mid, old))
    slab_ref[at, head] = slab.astype(BF16).reshape(2, MID, HALF, WIDTH)
    there = (iota((2, HALF, WIDTH), 1) == off_three % HALF) & jnp.logical_not(beside)
    other_ref[at, head] = jnp.where(there, far, other_ref[at, head].astype(F32)).astype(BF16)


def finish_kernel(
    off2_ref, off3_ref, cov_hbm, low_hbm, back_hbm, left_hbm, att_hbm, dq_hbm, dk_hbm, dv_hbm,
    att_out, dq_out, dk_out, dv_out,
    cov_ref, low_ref, back_ref, left_ref, right_ref, rows_ref, held, done_ref, slab_ref, other_ref,
    first_sems, in_sems, out_sems, slab_in, slab_out,
):
    first = [
        pltpu.make_async_copy(source, target, first_sems.at[at])
        for at, (source, target) in enumerate(((back_hbm, back_ref), (cov_hbm, cov_ref), (low_hbm, low_ref)))
    ]

    def slabs(head, arrays):
        half, period = off2_ref[head] // HALF, off3_ref[head] // DILATION_TWO
        lane = pl.ds(pl.multiple_of(head * WIDTH, WIDTH), WIDTH)
        pairs = []
        for at, array in enumerate(arrays):
            pairs.append((array.at[:, :, half, :, lane], slab_ref.at[at, head]))
            pairs.append((array.at[:, period, 1 - half, :, lane], other_ref.at[at, head]))
        return pairs

    def loads(head):
        pairs = slabs(head, (att_hbm, dq_hbm))
        copies = [pltpu.make_async_copy(*pair, slab_in.at[head, at]) for at, pair in enumerate(pairs)]
        pairs = [(dk_hbm.at[head], held.at[0, head]), (dv_hbm.at[head], held.at[1, head])]
        pairs.append((left_hbm.at[head], left_ref.at[head]))
        return copies + [pltpu.make_async_copy(*pair, in_sems.at[head, at]) for at, pair in enumerate(pairs)]

    def slab_stores(head):
        pairs = slabs(head, (att_out, dq_out))
        return [
            pltpu.make_async_copy(source, target, slab_out.at[head, at]) for at, (target, source) in enumerate(pairs)
        ]

    def stores(head):
        lane = pl.ds(pl.multiple_of(head * WIDTH, WIDTH), WIDTH)
        return [
            pltpu.make_async_copy(done_ref.at[at, head], out.at[:, lane], out_sems.at[head, at])
            for at, out in enumerate((dk_out, dv_out))
        ]

    for copy in first:
        copy.start()

    @pl.loop(0, HEADS)
    def _(head):
        for copy in loads(head):
            copy.start()

    for copy in first:
        copy.wait()
    prepare(off2_ref, off3_ref, cov_ref, low_ref, back_ref, right_ref, rows_ref)

    @pl.loop(0, HEADS)
    def _(head):
        for copy in loads(head):
            copy.wait()
        for at in range(2):
            patch(off2_ref[head], off3_ref[head], rows_ref, head, at, slab_ref, other_ref)
        for copy in slab_stores(head):
            copy.start()
        off_two, off_three = off2_ref[head], off3_ref[head]
        place = targets((1, 2 * COV), 1, off_two, off_three)
        twice = (off_three % DILATION_TWO) == off_two
        place = jnp.where(((iota((1, 2 * COV), 1) % COV) == MID) & twice, -1, place)
        select = (iota((SEG1, 2 * COV), 0) == place).astype(BF16)
        left = jnp.concatenate([left_ref[head], select], 1)
        for t in range(2):
            rows = slice(t * SEG1, (t + 1) * SEG1)
            x = dot_nn(left, right_ref[head, t])
            done_ref[0, head, rows, :] = (FACTOR * (held[0, head, rows, :].astype(F32) + x[:, :WIDTH])).astype(BF16)
            done_ref[1, head, rows, :] = (held[1, head, rows, :].astype(F32) + x[:, WIDTH:]).astype(BF16)
        for copy in stores(head):
            copy.start()

    @pl.loop(0, HEADS)
    def _(head):
        for copy in slab_stores(head) + stores(head):
            copy.wait()


def finish(offsets, cov, low, left, back, att, dq, dk, dv):
    smem, hbm = pl.BlockSpec(memory_space=pltpu.SMEM), pl.BlockSpec(memory_space=pl.ANY)
    kind = (2, HEADS, 2 * SEG1, WIDTH)
    whole = (2 * SEG1, HEADS * WIDTH)
    att, dq, dk, dv = pl.pallas_call(
        finish_kernel,
        in_specs=[smem, smem] + [hbm] * 8,
        out_specs=[hbm] * 4,
        out_shape=[pltpu.HBM(att.shape, BF16)] * 2 + [pltpu.HBM(whole, BF16)] * 2,
        input_output_aliases={6: 0, 7: 1},
        scratch_shapes=[pltpu.VMEM(x.shape, x.dtype) for x in (cov, low, back, left)]
        + [
            pltpu.VMEM((HEADS, 2, 6 * COV, 2 * WIDTH), BF16),
            pltpu.VMEM((2, HEADS, 2, COV, WIDTH), F32),
            pltpu.VMEM(kind, BF16),
            pltpu.VMEM(kind, BF16),
            pltpu.VMEM((2, HEADS, 2, MID, HALF, WIDTH), BF16),
            pltpu.VMEM((2, HEADS, 2, HALF, WIDTH), BF16),
            pltpu.SemaphoreType.DMA((3,)),
            pltpu.SemaphoreType.DMA((HEADS, 3)),
            pltpu.SemaphoreType.DMA((HEADS, 2)),
            pltpu.SemaphoreType.DMA((HEADS, 4)),
            pltpu.SemaphoreType.DMA((HEADS, 4)),
        ],
        compiler_params=pltpu.CompilerParams(vmem_limit_bytes=VMEM),
        cost_estimate=pl.CostEstimate(flops=2**30, bytes_accessed=17 * 2**20, transcendentals=2**18),
        name="finish",
    )(*offsets, *in_hbm((cov, low)), back, *in_hbm((left, att, dq, dk, dv)))
    return att.reshape(whole), dq.reshape(whole), dk, dv


def solution(mesh):
    outer = mesh.shape["outer"]
    split = P(("outer", "inner"), None)

    def body(queries, keys, values, out_grad, middle_head_offsets, distant_head_offsets):
        offsets = (middle_head_offsets, distant_head_offsets)
        arrays = (queries, keys, values, out_grad)
        send, cov, low, left = extract(offsets, *arrays)
        got = lax.all_to_all(send, "inner", 0, 0)
        parts = local(offsets, arrays, 0, SHARES[0], ())
        got, *parts = lax.optimization_barrier((got, *parts))
        far, out, figures = remote_forward(offsets, got, outer)
        far, *parts = lax.optimization_barrier((far, *parts))
        far = lax.all_to_all(far, "outer", 0, 0)
        parts = local(offsets, arrays, SHARES[0], SHARES[1], parts)
        far, *parts = lax.optimization_barrier((far, *parts))
        back = remote_backward(offsets, got, far, out, figures)
        back, *parts = lax.optimization_barrier((back, *parts))
        back = lax.all_to_all(back, "inner", 0, 0)
        parts = local(offsets, arrays, SHARES[0] + SHARES[1], SHARES[2], parts)
        back, *parts = lax.optimization_barrier((back, *parts))
        return finish(offsets, cov, low, left, back, *parts)

    return jax.shard_map(
        body, mesh=mesh, in_specs=(split,) * 4 + (P(), P()), out_specs=(split,) * 4, check_vma=False
    )
```

```python
import math

import jax
import jax.numpy as jnp
from jax import lax
from jax.experimental import pallas as pl
from jax.experimental.pallas import tpu as pltpu
from jax.sharding import PartitionSpec as P

SEG1 = 512
DILATION_TWO = 32
DILATION_THREE = 512
HEADS = 8
WIDTH = 128
FACTOR = WIDTH ** (-0.5)
MID = SEG1 // DILATION_TWO
COV = 32
PACK = 128
EXTRACT_HEADS = 2
SHARES = (5, 5, 6)
VMEM = 44 * 2**20
HALF = DILATION_TWO // 2
NEG = -1e30
F32 = jnp.float32
BF16 = jnp.bfloat16


def dot_nn(a, b):
    return lax.dot_general(a, b, (((1,), (0,)), ((), ())), preferred_element_type=F32)


def dot_nt(a, b):
    return lax.dot_general(a, b, (((1,), (1,)), ((), ())), preferred_element_type=F32)


def dot_tn(a, b):
    return lax.dot_general(a, b, (((0,), (0,)), ((), ())), preferred_element_type=F32)


def iota(shape, dim):
    return lax.broadcasted_iota(jnp.int32, shape, dim)


def split3(x):
    high = x.astype(BF16).astype(F32)
    rest = x - high
    middle = rest.astype(BF16).astype(F32)
    return high, middle, (rest - middle).astype(BF16).astype(F32)


def lanes(columns, rows):
    lane = iota((rows, WIDTH), 1)
    out = jnp.zeros((rows, WIDTH), F32)
    for j, column in enumerate(columns):
        out = jnp.where(lane == j, column, out)
    return out


def join3(x, at):
    return x[:, at : at + 1] + x[:, at + 1 : at + 2] + x[:, at + 2 : at + 3]


def targets(shape, dim, off_two, off_three):
    j = iota(shape, dim) % COV
    return jnp.where(j < MID, DILATION_TWO * j + off_two, jnp.where(j == MID, off_three, -1))


def in_hbm(arrays):
    return [pltpu.with_memory_space_constraint(x, pltpu.HBM) for x in arrays]


def extract_kernel(
    off2_ref, off3_ref, q_hbm, k_hbm, v_hbm, g_hbm, send_hbm, cov_hbm, low_hbm, left_hbm,
    q_all, k_all, v_all, g_all, send_ref, cov_ref, low_ref, left_ref, sems, out_sems,
):
    n = EXTRACT_HEADS

    def loads(step):
        lane = pl.ds(pl.multiple_of(step * n * WIDTH, n * WIDTH), n * WIDTH)
        pairs = ((q_hbm, q_all), (k_hbm, k_all), (v_hbm, v_all), (g_hbm, g_all))
        return [
            pltpu.make_async_copy(source.at[:, :, :, lane], target.at[step], sems.at[step, at])
            for at, (source, target) in enumerate(pairs)
        ]

    def places(step):
        heads = pl.ds(step * n, n)
        return (pl.ds(step * 2 * n, 2 * n),), (slice(None), heads), (slice(None), heads), (heads,)

    scratch = (send_ref, cov_ref, low_ref, left_ref)

    def stores(step):
        pairs = zip(scratch, (send_hbm, cov_hbm, low_hbm, left_hbm), places(step))
        return [
            pltpu.make_async_copy(source.at[place], target.at[place], out_sems.at[step, at])
            for at, (source, target, place) in enumerate(pairs)
        ]

    @pl.loop(0, HEADS // n)
    def _(step):
        for copy in loads(step):
            copy.start()

    @pl.loop(0, HEADS // n)
    def _(step):
        for copy in loads(step):
            copy.wait()
        here = [ref.at[step] for ref in (q_all, k_all, v_all, g_all)]
        out = [ref.at[place] for ref, place in zip(scratch, places(step))]
        extract_heads(step * n, off2_ref, off3_ref, *here, *out)
        for copy in stores(step):
            copy.start()

    @pl.loop(0, HEADS // n)
    def _(step):
        for copy in stores(step):
            copy.wait()


def extract_heads(first_head, off2_ref, off3_ref, q_ref, k_ref, v_ref, g_ref, send_ref, cov_ref, low_ref, left_ref):
    cells = [(i, t) for i in range(EXTRACT_HEADS) for t in range(2)]

    def block(ref, cell):
        i, t = cell
        return ref[t * MID : (t + 1) * MID, :, :, i * WIDTH : (i + 1) * WIDTH].reshape(SEG1, WIDTH)

    def pick(cell):
        i, t = cell
        off_two, off_three = off2_ref[first_head + i], off3_ref[first_head + i]
        lane = slice(i * WIDTH, (i + 1) * WIDTH)
        refs = (q_ref, k_ref, v_ref, g_ref)
        slabs = [ref[t * MID : (t + 1) * MID, off_two // HALF, :, lane].reshape(MID * HALF, WIDTH) for ref in refs]
        place = t * MID + off_three // DILATION_TWO
        others = [ref[place, (off_three % DILATION_TWO) // HALF, :, lane] for ref in refs]
        select = iota((MID, MID * HALF), 1) == HALF * iota((MID, 1), 0) + off_two % HALF
        select_far = (iota((MID, HALF), 1) == off_three % HALF) & (iota((MID, HALF), 0) == 0)
        return jnp.concatenate(
            [
                dot_nn(select.astype(BF16), jnp.concatenate(slabs, 1)),
                dot_nn(select_far.astype(BF16), jnp.concatenate(others, 1)),
            ],
            0,
        )

    valids = []
    row = iota((COV, 1), 0)
    for i in range(EXTRACT_HEADS):
        twice = (off3_ref[first_head + i] % DILATION_TWO) == off2_ref[first_head + i]
        valids.append(((row < MID) | ((row == MID) & jnp.logical_not(twice))).astype(F32))
    picked = [pick(cell) for cell in cells]
    low = [x.astype(BF16) for x in picked]
    scores = [dot_nt(x[:, :WIDTH], block(k_ref, cell)) for x, cell in zip(low, cells)]
    grads = [dot_nt(x[:, 3 * WIDTH :], block(v_ref, cell)) for x, cell in zip(low, cells)]
    scores, grads = jnp.concatenate(scores, 0) * FACTOR, jnp.concatenate(grads, 0)
    top = jnp.max(scores, axis=1, keepdims=True)
    weight = jnp.exp(scores - top)
    total = jnp.sum(weight, axis=1, keepdims=True)
    weight_low = weight.astype(BF16)
    out = jnp.concatenate(
        [dot_nn(weight_low[n * COV : (n + 1) * COV], block(v_ref, cell)) for n, cell in enumerate(cells)], 0
    ) / total
    lse = top + jnp.log(total)
    g_cov = jnp.concatenate([x[:, 3 * WIDTH :] for x in picked], 0)
    delta = jnp.sum(g_cov * out, axis=1, keepdims=True)
    stats = lanes(split3(lse) + split3(delta), COV * len(cells))
    shown = lanes([lse, delta], COV * len(cells))
    prob = weight * (jnp.concatenate([valids[i] for i, _ in cells], 0) / total)
    dscore = (prob * (grads - delta)).astype(BF16)
    prob = prob.astype(BF16)
    first = iota((MID, 1), 0) == 0
    for n, (i, t) in enumerate(cells):
        rows = slice(n * COV, (n + 1) * COV)
        own = stats[rows]
        for c in range(2):
            send_ref[2 * i + c, t * MID : (t + 1) * MID, :] = low[n][:MID, WIDTH : 2 * WIDTH]
            send_ref[2 * i + c, 2 * MID + t * MID : 2 * MID + (t + 1) * MID, :] = low[n][:MID, 2 * WIDTH : 3 * WIDTH]
        send_ref[2 * i + t, 4 * MID : 5 * MID, :] = low[n][:MID, :WIDTH]
        send_ref[2 * i + t, 5 * MID : 6 * MID, :] = low[n][:MID, 3 * WIDTH :]
        send_ref[2 * i + t, 6 * MID : 7 * MID, :] = own[:MID].astype(BF16)
        mine = (picked[n][MID:, :WIDTH], picked[n][MID:, 3 * WIDTH :], jnp.where(first, own[MID:], 0.0))
        pair = [picked[n - t + u][MID:, at * WIDTH : (at + 1) * WIDTH] for at in (1, 2) for u in range(2)]
        far_block = pair[0]
        for at, x in enumerate((*pair[1:], *mine)):
            far_block = far_block + pltpu.roll(x, at + 1, 0)
        send_ref[2 * i + t, 7 * MID :, :] = far_block.astype(BF16)
        both = dot_nn(jnp.concatenate([dscore[rows], prob[rows]], 0), block(k_ref, (i, t)))
        for at, x in enumerate((out[rows], both[:COV], both[COV:], shown[rows])):
            cov_ref[at, i, t] = x
        low_ref[0, i, t] = low[n][:, :WIDTH]
        low_ref[1, i, t] = low[n][:, 3 * WIDTH :]
    for i in range(EXTRACT_HEADS):
        parts = [x[n * COV : (n + 1) * COV] for n in (2 * i, 2 * i + 1) for x in (dscore, prob)]
        left_ref[i] = jnp.concatenate(parts, 0).T


def extract(offsets, q, k, v, g):
    smem, hbm = pl.BlockSpec(memory_space=pltpu.SMEM), pl.BlockSpec(memory_space=pl.ANY)
    steps = HEADS // EXTRACT_HEADS
    period = (2 * MID, 2, HALF)
    shapes = [
        ((2 * HEADS, PACK, WIDTH), BF16),
        ((4, HEADS, 2, COV, WIDTH), F32),
        ((2, HEADS, 2, COV, WIDTH), BF16),
        ((HEADS, SEG1, 4 * COV), BF16),
    ]
    return pl.pallas_call(
        extract_kernel,
        in_specs=[smem, smem] + [hbm] * 4,
        out_specs=[hbm] * 4,
        out_shape=[pltpu.HBM(*x) for x in shapes],
        scratch_shapes=[pltpu.VMEM((steps, *period, EXTRACT_HEADS * WIDTH), BF16)] * 4
        + [pltpu.VMEM(*x) for x in shapes]
        + [pltpu.SemaphoreType.DMA((steps, 4))] * 2,
        compiler_params=pltpu.CompilerParams(vmem_limit_bytes=63 * 2**20),
        cost_estimate=pl.CostEstimate(flops=2**32, bytes_accessed=12 * 2**20, transcendentals=2**18),
        name="extract",
    )(*offsets, *in_hbm([x.reshape(*period, HEADS * WIDTH) for x in (q, k, v, g)]))


def local_kernel(first, count, kept, off2_ref, off3_ref, *refs):
    sources, outs = refs[:4], refs[4 + kept : 8 + kept]
    held, done, (in_sems, out_sems) = refs[8 + kept : 12 + kept], refs[12 + kept : 16 + kept], refs[16 + kept :]
    position = iota((1, SEG1), 1)

    def place(c):
        head, t = (first + c) // 2, (first + c) % 2
        return head, t, pl.ds(pl.multiple_of(head * WIDTH, WIDTH), WIDTH), pl.ds(pl.multiple_of(t * SEG1, SEG1), SEG1)

    def loads(c):
        _, _, lane, rows = place(c)
        return [
            pltpu.make_async_copy(sources[at].at[rows, lane], held[at].at[c], in_sems.at[c, at]) for at in range(4)
        ]

    def stores(c):
        head, t, lane, rows = place(c)
        return [
            pltpu.make_async_copy(
                done[at].at[c], outs[at].at[t, :, :, :, lane] if at < 2 else outs[at].at[head, rows], out_sems.at[c, at]
            )
            for at in range(4)
        ]

    def start(c):
        for copy in loads(c):
            copy.start()

    start(0)
    start(1)

    @pl.loop(0, count)
    def _(c):
        @pl.when(c + 2 < count)
        def _():
            start(c + 2)

        head = (first + c) // 2
        covered = ((position & (DILATION_TWO - 1)) == off2_ref[head]) | (position == off3_ref[head])
        for copy in loads(c):
            copy.wait()
        q, k, v, g = (ref[c] for ref in held)
        scores = dot_nt(k, q) * (FACTOR * math.log2(math.e))
        grad = dot_nt(v, g)
        weight = jnp.exp2(scores - jnp.max(scores, axis=0, keepdims=True))
        inverse = 1.0 / jnp.sum(weight, axis=0, keepdims=True)
        att = (dot_nn(v.T, weight.astype(BF16)) * inverse).astype(BF16)
        delta = jnp.sum(g.T.astype(F32) * att.astype(F32), axis=0, keepdims=True)
        out = stores(c)
        done[0][c] = att.T.reshape(MID, 2, HALF, WIDTH)
        out[0].start()
        prob = weight * jnp.where(covered, 0.0, inverse)
        dscore = (prob * (grad - delta)).astype(BF16)
        done[1][c] = (dot_nn(k.T, dscore) * FACTOR).astype(BF16).T.reshape(MID, 2, HALF, WIDTH)
        out[1].start()
        done[2][c] = dot_nn(dscore, q).astype(BF16)
        out[2].start()
        done[3][c] = dot_nn(prob.astype(BF16), g).astype(BF16)
        out[3].start()

    @pl.loop(0, count)
    def _(c):
        for copy in stores(c):
            copy.wait()


def local(offsets, arrays, first, count, earlier):
    smem, hbm = pl.BlockSpec(memory_space=pltpu.SMEM), pl.BlockSpec(memory_space=pl.ANY)
    share = count / (2 * HEADS)
    period = (MID, 2, HALF)
    return pl.pallas_call(
        lambda *refs: local_kernel(first, count, len(earlier), *refs),
        in_specs=[smem, smem] + [hbm] * (4 + len(earlier)),
        out_specs=[hbm] * 4,
        out_shape=[pltpu.HBM((2, *period, HEADS * WIDTH), BF16)] * 2 + [pltpu.HBM((HEADS, 2 * SEG1, WIDTH), BF16)] * 2,
        input_output_aliases={6 + at: at for at in range(len(earlier))},
        scratch_shapes=[pltpu.VMEM((count, SEG1, WIDTH), BF16)] * 4
        + [pltpu.VMEM((count, *period, WIDTH), BF16)] * 2
        + [pltpu.VMEM((count, SEG1, WIDTH), BF16)] * 2
        + [pltpu.SemaphoreType.DMA((count, 4))] * 2,
        compiler_params=pltpu.CompilerParams(vmem_limit_bytes=VMEM),
        cost_estimate=pl.CostEstimate(
            flops=int(share * 12 * 2**30), bytes_accessed=int(share * 16 * 2**20), transcendentals=int(share * 2**22)
        ),
        name="local",
    )(*offsets, *in_hbm((*arrays, *earlier)))


def merge_lse(parts):
    top = parts[0]
    for part in parts[1:]:
        top = jnp.maximum(top, part)
    total = jnp.exp(parts[0] - top)
    for part in parts[1:]:
        total = total + jnp.exp(part - top)
    return top + jnp.log(total)


def part(ref, at, rows):
    return ref[:, at * MID : at * MID + rows, :].reshape(ref.shape[0] * rows, WIDTH)


def far_places(shape, dim, starts):
    j = iota(shape, dim)
    n = shape[dim] // 7
    place = jnp.zeros(shape, jnp.int32)
    for at, start in enumerate(starts):
        if at < 2:
            u = j - 2 * n * at
            place = jnp.where((u >= 0) & (u < 2 * n), MID * (u // 2) + u % 2 + start, place)
        else:
            u = j - n * (at + 2)
            place = jnp.where((u >= 0) & (u < n), MID * u + start, place)
    return place


def forward_kernel(off2_ref, off3_ref, in_ref, far_ref, out_ref, figures_ref):
    head = lax.axis_index("inner") // 2
    off_three = off3_ref[head]
    n = in_ref.shape[0]
    k, v, q, g = part(in_ref, 0, 2 * MID), part(in_ref, 2, 2 * MID), part(in_ref, 4, MID), part(in_ref, 5, MID)
    queries = n * MID
    scores = dot_nt(q, k) * FACTOR
    top = jnp.max(scores, axis=1, keepdims=True)
    weight = jnp.exp(scores - top)
    total = jnp.sum(weight, axis=1, keepdims=True)
    out = dot_nn(weight.astype(BF16), v) / total
    lse = jnp.broadcast_to(top + jnp.log(total), (queries, WIDTH))
    delta = jnp.broadcast_to(jnp.sum(g.astype(F32) * out, axis=1, keepdims=True), (queries, WIDTH))
    out_ref[...] = out.astype(BF16)
    figures_ref[...] = lanes([lse, delta], queries)
    pick = (iota((7 * n, queries), 1) == far_places((7 * n, 1), 0, (0, 2, 4, 5, 6))).astype(BF16)
    picked = dot_nn(pick, part(in_ref, 7, MID))
    stats = picked[6 * n :]
    same = ((off_three % DILATION_TWO) == off2_ref[head]) & (
        iota((n, MID, WIDTH), 1) == off_three // DILATION_TWO
    )
    lse1, delta1 = join3(stats, 0), join3(stats, 3)
    lse2 = jnp.max(jnp.where(same, lse.reshape(n, MID, WIDTH), NEG), axis=1)
    delta2 = jnp.sum(jnp.where(same, delta.reshape(n, MID, WIDTH), 0.0), axis=1)
    both = merge_lse([lse1, lse2])
    delta = jnp.exp(lse1 - both) * delta1 + jnp.exp(lse2 - both) * delta2
    rows = jnp.concatenate([picked[: 6 * n], lanes(split3(both) + split3(delta), n)], 0).astype(BF16)
    for o in range(far_ref.shape[0]):
        far_ref[o] = rows


def backward_kernel(off2_ref, off3_ref, in_ref, far_ref, out2_ref, figures_ref, out_ref, key_ref, query_ref):
    head, outer = lax.axis_index("inner") // 2, lax.axis_index("outer")
    off_three = off3_ref[head]
    n = in_ref.shape[0]
    queries = n * MID
    turn = (iota((8, WIDTH), 0) == iota((8, WIDTH), 1)).astype(BF16)
    kf, vf = part(far_ref, 0, 2 * MID), part(far_ref, 2, 2 * MID)
    qf, gf = part(far_ref, 4, MID), part(far_ref, 5, MID)
    figures = dot_nt(turn, part(far_ref, 6, MID))
    lse12 = figures[0:1] + figures[1:2] + figures[2:3]
    delta12 = figures[3:4] + figures[4:5] + figures[5:6]
    scores = dot_nt(kf, qf) * FACTOR
    grads = dot_nt(vf, gf)
    top = jnp.max(scores, axis=0, keepdims=True)
    weight = jnp.exp(scores - top)
    total = jnp.sum(weight, axis=0, keepdims=True)
    lse3 = top + jnp.log(total)
    share = weight / total
    delta3 = jnp.sum(share * grads, axis=0, keepdims=True)
    lse = merge_lse([lse12, lse3])
    delta = jnp.exp(lse12 - lse) * delta12 + jnp.exp(lse3 - lse) * delta3
    prob = jnp.exp(scores - lse)
    dscore = (prob * (grads - delta)).astype(BF16)
    key_ref[0] = dot_nn(dscore, qf)
    key_ref[1] = dot_nn(prob.astype(BF16), gf)
    query_ref[0] = dot_tn(dscore, kf)
    query_ref[1] = dot_tn(share.astype(BF16), vf)
    eight = iota((8, lse3.shape[1]), 0)
    figures = jnp.zeros(eight.shape, F32)
    for at, x in enumerate(split3(lse3) + split3(delta3)):
        figures = jnp.where(eight == at, x, figures)
    query_ref[2] = dot_tn(figures.astype(BF16), turn)
    own_keys = pl.ds(pl.multiple_of(outer * 2 * n, 2 * n), 2 * n)
    own_queries = pl.ds(pl.multiple_of(outer * n, n), n)
    own = [key_ref[0, own_keys, :], key_ref[1, own_keys, :]] + [query_ref[at, own_queries, :] for at in range(3)]
    unpick = (iota((queries, 7 * n), 0) == far_places((1, 7 * n), 1, (3, 5, 0, 1, 2))).astype(BF16)
    packed = dot_nn(unpick, jnp.concatenate(own, 0).astype(BF16))
    same = ((off_three % DILATION_TWO) == off2_ref[head]) & (
        iota((n, MID, WIDTH), 1) == off_three // DILATION_TWO
    )

    def expand(column, other):
        wide = jnp.broadcast_to(jnp.broadcast_to(column, (n, WIDTH)).reshape(n, 1, WIDTH), (n, MID, WIDTH))
        return jnp.where(same, wide, other).reshape(queries, WIDTH)[:, 0:1]

    lse3, delta3 = expand(join3(own[4], 0), NEG), expand(join3(own[4], 3), 0.0)
    stats = part(in_ref, 6, MID).astype(F32)
    lse1, delta1 = join3(stats, 0), join3(stats, 3)
    lse2, delta2 = figures_ref[:, 0:1], figures_ref[:, 1:2]
    lse = merge_lse([lse1, lse2, lse3])
    delta = jnp.exp(lse1 - lse) * delta1 + jnp.exp(lse2 - lse) * delta2 + jnp.exp(lse3 - lse) * delta3
    k, v, q, g = part(in_ref, 0, 2 * MID), part(in_ref, 2, 2 * MID), part(in_ref, 4, MID), part(in_ref, 5, MID)
    prob = jnp.exp(dot_nt(q, k) * FACTOR - lse)
    dscore = (prob * (dot_nt(g, v) - delta)).astype(BF16)

    def give(at, rows, value):
        out_ref[:, at * MID : at * MID + rows, :] = value.astype(BF16).reshape(n, rows, WIDTH)

    give(0, 2 * MID, dot_tn(dscore, q))
    give(2, 2 * MID, dot_tn(prob.astype(BF16), g))
    give(4, MID, dot_nn(dscore, k))
    give(5, MID, out2_ref[...])
    give(6, MID, lanes(split3(lse2), queries))
    give(7, MID, packed)


def remote_call(kernel, offsets, arrays, shapes, scratch, name):
    vmem, smem = pl.BlockSpec(memory_space=pltpu.VMEM), pl.BlockSpec(memory_space=pltpu.SMEM)
    return pl.pallas_call(
        kernel,
        in_specs=[smem, smem] + [vmem] * len(arrays),
        out_specs=[vmem] * len(shapes),
        out_shape=shapes,
        scratch_shapes=[pltpu.VMEM(*x) for x in scratch],
        compiler_params=pltpu.CompilerParams(vmem_limit_bytes=VMEM),
        cost_estimate=pl.CostEstimate(flops=2**31, bytes_accessed=2**21, transcendentals=2**19),
        name=name,
    )(*offsets, *arrays)


def remote_forward(offsets, received, outer):
    n = received.shape[0]
    rows = n * MID
    return remote_call(
        forward_kernel, offsets, (received,),
        [jax.ShapeDtypeStruct((outer, 7 * n, WIDTH), BF16), jax.ShapeDtypeStruct((rows, WIDTH), BF16),
         jax.ShapeDtypeStruct((rows, WIDTH), F32)],
        [], "remote_forward",
    )


def remote_backward(offsets, received, far, out, figures):
    n, outer = received.shape[0], far.shape[0]
    return remote_call(
        backward_kernel, offsets, (received, far, out, figures), [jax.ShapeDtypeStruct(received.shape, BF16)],
        [((2, outer * 2 * n, WIDTH), F32), ((3, outer * n, WIDTH), F32)], "remote_backward",
    )[0]


def prepare(off2_ref, off3_ref, cov_ref, low_ref, back_ref, right_ref, rows_ref):
    cells, rows = 2 * HEADS, 2 * HEADS * COV
    back = back_ref[...].astype(F32)

    def pad(x):
        return jnp.concatenate([x, jnp.zeros((cells, COV - MID, WIDTH), F32)], 1).reshape(rows, WIDTH)

    def own(at):
        return pad(back[:, at * MID : (at + 1) * MID])

    def both(at):
        x = back[:, at * MID : (at + 2) * MID].reshape(HEADS, 2, COV, WIDTH)
        return pad((x[:, 0] + x[:, 1]).reshape(cells, MID, WIDTH))

    def spread(x):
        return jnp.broadcast_to(x.reshape(cells, 1, WIDTH), (cells, COV, WIDTH)).reshape(rows, WIDTH)

    row = iota((COV, WIDTH), 0)
    is_far = []
    for head in range(HEADS):
        off_three = off3_ref[head]
        twice = (off_three % DILATION_TWO) == off2_ref[head]
        is_far += [(row == jnp.where(twice, off_three // DILATION_TWO, MID)).astype(F32)] * 2
    is_far = jnp.concatenate(is_far, 0) > 0.0
    is_mid = jnp.concatenate([row] * cells, 0) < MID
    ones = (iota((WIDTH, WIDTH), 0) < 3).astype(BF16)

    def joined(x):
        return dot_nn(x.astype(BF16), ones)

    q, g = (low_ref[at].reshape(rows, WIDTH).astype(F32) for at in range(2))
    out, dq_one, dq_two, figures = (cov_ref[at].reshape(rows, WIDTH) for at in range(4))
    lse1, delta1 = figures[:, 0:1], figures[:, 1:2]
    packed = back[:, 7 * MID : 8 * MID]
    far = packed[:, 3:7].reshape(HEADS, 2, 4, WIDTH)
    far = (far[:, 0] + far[:, 1]).reshape(HEADS, 2, 2, WIDTH)
    lse2 = jnp.where(is_mid, joined(own(6)), NEG)
    lse3 = jnp.where(is_far, joined(spread(packed[:, 2:3])), NEG)
    lse = merge_lse([lse1, lse2, lse3])
    share = jnp.exp(lse1 - lse)
    att = (
        share * out + jnp.exp(lse2 - lse) * own(5) + jnp.exp(lse3 - lse) * spread(packed[:, 1:2])
    ).astype(BF16)
    delta = jnp.sum(g * att.astype(F32), axis=1, keepdims=True)
    change = share * (delta - delta1)
    dq = share * dq_one - change * dq_two + own(4) + jnp.where(is_far, spread(packed[:, 0:1]), 0.0)
    dk = both(0) + jnp.where(is_far, spread(far[:, 0]), 0.0)
    dv = both(2) + jnp.where(is_far, spread(far[:, 1]), 0.0)

    def column(at):
        return slice(at * WIDTH, (at + 1) * WIDTH)

    def put(at, to, x):
        x = x.astype(BF16).reshape(HEADS, 2, COV, WIDTH)
        for t in range(2):
            start = (2 * t + at) * COV
            right_ref[:, t, start : start + COV, column(to)] = x[:, t]

    def put_rows(to, x):
        high = x.astype(BF16)
        for at, part_ in enumerate((high, (x - high.astype(F32)).astype(BF16))):
            start = (4 + at) * COV
            right_ref[:, :, start : start + COV, column(to)] = part_.reshape(HEADS, 2, COV, WIDTH)

    rows_ref[0] = att.astype(F32).reshape(HEADS, 2, COV, WIDTH)
    rows_ref[1] = (FACTOR * dq).reshape(HEADS, 2, COV, WIDTH)
    nothing = jnp.zeros((HEADS, 2 * COV, 2 * WIDTH), BF16)
    right_ref[:, 0, 2 * COV : 4 * COV, :] = nothing
    right_ref[:, 1, : 2 * COV, :] = nothing
    put(0, 0, share * q)
    put(1, 0, -change * q)
    put_rows(0, dk)
    put(0, 1, jnp.zeros((rows, WIDTH), F32))
    put(1, 1, share * g)
    put_rows(1, dv)


def patch(off_two, off_three, rows_ref, head, at, slab_ref, other_ref, wide_ref):
    size = 2 * MID * HALF
    twice = (off_three % DILATION_TWO) == off_two
    beside = ((off_three % DILATION_TWO) // HALF) == (off_two // HALF)
    far = rows_ref[at, head, :, MID : MID + 1]
    wide_ref[at, :size, :] = slab_ref[at, head].astype(F32).reshape(size, WIDTH)
    wide_ref[at, pl.ds(off_two % HALF, 2 * MID, stride=HALF), :] = rows_ref[at, head, :, :MID].reshape(2 * MID, WIDTH)
    for t in range(2):
        spot = (t * MID + off_three // DILATION_TWO) * HALF + off_three % HALF
        spot = jnp.where(beside & jnp.logical_not(twice), spot, size)
        wide_ref[at, pl.ds(spot, 1), :] = far[t]
    slab_ref[at, head] = wide_ref[at, :size, :].astype(BF16).reshape(2, MID, HALF, WIDTH)
    there = (iota((2, HALF, WIDTH), 1) == off_three % HALF) & jnp.logical_not(beside)
    other_ref[at, head] = jnp.where(there, far, other_ref[at, head].astype(F32)).astype(BF16)


def finish_kernel(
    off2_ref, off3_ref, cov_hbm, low_hbm, back_ref, left_hbm, att_hbm, dq_hbm, dk_hbm, dv_hbm,
    att_out, dq_out, dk_out, dv_out,
    cov_ref, low_ref, left_ref, right_ref, rows_ref, held, done_ref, slab_ref, other_ref, wide_ref,
    first_sems, in_sems, out_sems, slab_in, slab_out,
):
    first = [
        pltpu.make_async_copy(source, target, first_sems.at[at])
        for at, (source, target) in enumerate(((cov_hbm, cov_ref), (low_hbm, low_ref)))
    ]

    def slabs(head, arrays):
        half, period = off2_ref[head] // HALF, off3_ref[head] // DILATION_TWO
        lane = pl.ds(pl.multiple_of(head * WIDTH, WIDTH), WIDTH)
        pairs = []
        for at, array in enumerate(arrays):
            pairs.append((array.at[:, :, half, :, lane], slab_ref.at[at, head]))
            pairs.append((array.at[:, period, 1 - half, :, lane], other_ref.at[at, head]))
        return pairs

    def loads(head):
        pairs = slabs(head, (att_hbm, dq_hbm))
        copies = [pltpu.make_async_copy(*pair, slab_in.at[head, at]) for at, pair in enumerate(pairs)]
        pairs = [(dk_hbm.at[head], held.at[0, head]), (dv_hbm.at[head], held.at[1, head])]
        pairs.append((left_hbm.at[head], left_ref.at[head]))
        return copies + [pltpu.make_async_copy(*pair, in_sems.at[head, at]) for at, pair in enumerate(pairs)]

    def slab_stores(head):
        pairs = slabs(head, (att_out, dq_out))
        return [
            pltpu.make_async_copy(source, target, slab_out.at[head, at]) for at, (target, source) in enumerate(pairs)
        ]

    def stores(head):
        lane = pl.ds(pl.multiple_of(head * WIDTH, WIDTH), WIDTH)
        return [
            pltpu.make_async_copy(done_ref.at[at, head], out.at[:, lane], out_sems.at[head, at])
            for at, out in enumerate((dk_out, dv_out))
        ]

    for copy in first:
        copy.start()

    @pl.loop(0, HEADS)
    def _(head):
        for copy in loads(head):
            copy.start()

    for copy in first:
        copy.wait()
    prepare(off2_ref, off3_ref, cov_ref, low_ref, back_ref, right_ref, rows_ref)

    @pl.loop(0, HEADS)
    def _(head):
        for copy in loads(head):
            copy.wait()
        for at in range(2):
            patch(off2_ref[head], off3_ref[head], rows_ref, head, at, slab_ref, other_ref, wide_ref)
        for copy in slab_stores(head):
            copy.start()
        off_two, off_three = off2_ref[head], off3_ref[head]
        place = targets((1, 2 * COV), 1, off_two, off_three)
        twice = (off_three % DILATION_TWO) == off_two
        place = jnp.where(((iota((1, 2 * COV), 1) % COV) == MID) & twice, -1, place)
        select = (iota((SEG1, 2 * COV), 0) == place).astype(BF16)
        left = jnp.concatenate([left_ref[head], select], 1)
        for t in range(2):
            rows = slice(t * SEG1, (t + 1) * SEG1)
            x = dot_nn(left, right_ref[head, t])
            done_ref[0, head, rows, :] = (FACTOR * (held[0, head, rows, :].astype(F32) + x[:, :WIDTH])).astype(BF16)
            done_ref[1, head, rows, :] = (held[1, head, rows, :].astype(F32) + x[:, WIDTH:]).astype(BF16)
        for copy in stores(head):
            copy.start()

    @pl.loop(0, HEADS)
    def _(head):
        for copy in slab_stores(head) + stores(head):
            copy.wait()


def finish(offsets, cov, low, left, back, att, dq, dk, dv):
    smem, hbm = pl.BlockSpec(memory_space=pltpu.SMEM), pl.BlockSpec(memory_space=pl.ANY)
    kind = (2, HEADS, 2 * SEG1, WIDTH)
    whole = (2 * SEG1, HEADS * WIDTH)
    att, dq, dk, dv = pl.pallas_call(
        finish_kernel,
        in_specs=[smem, smem, hbm, hbm, pl.BlockSpec(memory_space=pltpu.VMEM)] + [hbm] * 5,
        out_specs=[hbm] * 4,
        out_shape=[pltpu.HBM(att.shape, BF16)] * 2 + [pltpu.HBM(whole, BF16)] * 2,
        input_output_aliases={6: 0, 7: 1},
        scratch_shapes=[pltpu.VMEM(x.shape, x.dtype) for x in (cov, low, left)]
        + [
            pltpu.VMEM((HEADS, 2, 6 * COV, 2 * WIDTH), BF16),
            pltpu.VMEM((2, HEADS, 2, COV, WIDTH), F32),
            pltpu.VMEM(kind, BF16),
            pltpu.VMEM(kind, BF16),
            pltpu.VMEM((2, HEADS, 2, MID, HALF, WIDTH), BF16),
            pltpu.VMEM((2, HEADS, 2, HALF, WIDTH), BF16),
            pltpu.VMEM((2, 2 * MID * HALF + 8, WIDTH), F32),
            pltpu.SemaphoreType.DMA((2,)),
            pltpu.SemaphoreType.DMA((HEADS, 3)),
            pltpu.SemaphoreType.DMA((HEADS, 2)),
            pltpu.SemaphoreType.DMA((HEADS, 4)),
            pltpu.SemaphoreType.DMA((HEADS, 4)),
        ],
        compiler_params=pltpu.CompilerParams(vmem_limit_bytes=VMEM),
        cost_estimate=pl.CostEstimate(flops=2**30, bytes_accessed=17 * 2**20, transcendentals=2**18),
        name="finish",
    )(*offsets, *in_hbm((cov, low)), back, *in_hbm((left, att, dq, dk, dv)))
    return att.reshape(whole), dq.reshape(whole), dk, dv


def solution(mesh):
    outer = mesh.shape["outer"]
    split = P(("outer", "inner"), None)

    def body(queries, keys, values, out_grad, middle_head_offsets, distant_head_offsets):
        offsets = (middle_head_offsets, distant_head_offsets)
        arrays = (queries, keys, values, out_grad)
        send, cov, low, left = extract(offsets, *arrays)
        got = lax.all_to_all(send, "inner", 0, 0)
        parts = local(offsets, arrays, 0, SHARES[0], ())
        got, *parts = lax.optimization_barrier((got, *parts))
        far, out, figures = remote_forward(offsets, got, outer)
        far, *parts = lax.optimization_barrier((far, *parts))
        far = lax.all_to_all(far, "outer", 0, 0)
        parts = local(offsets, arrays, SHARES[0], SHARES[1], parts)
        far, *parts = lax.optimization_barrier((far, *parts))
        back = remote_backward(offsets, got, far, out, figures)
        back, *parts = lax.optimization_barrier((back, *parts))
        back = lax.all_to_all(back, "inner", 0, 0)
        parts = local(offsets, arrays, SHARES[0] + SHARES[1], SHARES[2], parts)
        back, *parts = lax.optimization_barrier((back, *parts))
        return finish(offsets, cov, low, left, back, *parts)

    return jax.shard_map(
        body, mesh=mesh, in_specs=(split,) * 4 + (P(), P()), out_specs=(split,) * 4, check_vma=False
    )
```

```python
import math

import jax
import jax.numpy as jnp
from jax import lax
from jax.experimental import pallas as pl
from jax.experimental.pallas import tpu as pltpu
from jax.sharding import PartitionSpec as P

SEG1 = 512
DILATION_TWO = 32
DILATION_THREE = 512
HEADS = 8
WIDTH = 128
FACTOR = WIDTH ** (-0.5)
MID = SEG1 // DILATION_TWO
COV = 32
PACK = 128
EXTRACT_HEADS = 2
SHARES = (5, 5, 6)
VMEM = 44 * 2**20
HALF = DILATION_TWO // 2
NEG = -1e30
F32 = jnp.float32
BF16 = jnp.bfloat16


def dot_nn(a, b):
    return lax.dot_general(a, b, (((1,), (0,)), ((), ())), preferred_element_type=F32)


def dot_nt(a, b):
    return lax.dot_general(a, b, (((1,), (1,)), ((), ())), preferred_element_type=F32)


def dot_tn(a, b):
    return lax.dot_general(a, b, (((0,), (0,)), ((), ())), preferred_element_type=F32)


def iota(shape, dim):
    return lax.broadcasted_iota(jnp.int32, shape, dim)


def split3(x):
    high = x.astype(BF16).astype(F32)
    rest = x - high
    middle = rest.astype(BF16).astype(F32)
    return high, middle, (rest - middle).astype(BF16).astype(F32)


def lanes(columns, rows):
    lane = iota((rows, WIDTH), 1)
    out = jnp.zeros((rows, WIDTH), F32)
    for j, column in enumerate(columns):
        out = jnp.where(lane == j, column, out)
    return out


def join3(x, at):
    return x[:, at : at + 1] + x[:, at + 1 : at + 2] + x[:, at + 2 : at + 3]


def targets(shape, dim, off_two, off_three):
    j = iota(shape, dim) % COV
    return jnp.where(j < MID, DILATION_TWO * j + off_two, jnp.where(j == MID, off_three, -1))


def in_hbm(arrays):
    return [pltpu.with_memory_space_constraint(x, pltpu.HBM) for x in arrays]


def extract_kernel(
    off2_ref, off3_ref, q_hbm, k_hbm, v_hbm, g_hbm, send_hbm, cov_hbm, low_hbm, left_hbm,
    q_all, k_all, v_all, g_all, send_ref, cov_ref, low_ref, left_ref, sems, out_sems,
):
    n = EXTRACT_HEADS

    def loads(step):
        lane = pl.ds(pl.multiple_of(step * n * WIDTH, n * WIDTH), n * WIDTH)
        pairs = ((q_hbm, q_all), (k_hbm, k_all), (v_hbm, v_all), (g_hbm, g_all))
        return [
            pltpu.make_async_copy(source.at[:, :, :, lane], target.at[step], sems.at[step, at])
            for at, (source, target) in enumerate(pairs)
        ]

    def places(step):
        heads = pl.ds(step * n, n)
        return (pl.ds(step * 2 * n, 2 * n),), (slice(None), heads), (slice(None), heads), (heads,)

    scratch = (send_ref, cov_ref, low_ref, left_ref)

    def stores(step):
        pairs = zip(scratch, (send_hbm, cov_hbm, low_hbm, left_hbm), places(step))
        return [
            pltpu.make_async_copy(source.at[place], target.at[place], out_sems.at[step, at])
            for at, (source, target, place) in enumerate(pairs)
        ]

    @pl.loop(0, HEADS // n)
    def _(step):
        for copy in loads(step):
            copy.start()

    @pl.loop(0, HEADS // n)
    def _(step):
        for copy in loads(step):
            copy.wait()
        here = [ref.at[step] for ref in (q_all, k_all, v_all, g_all)]
        out = [ref.at[place] for ref, place in zip(scratch, places(step))]
        extract_heads(step * n, off2_ref, off3_ref, *here, *out)
        for copy in stores(step):
            copy.start()

    @pl.loop(0, HEADS // n)
    def _(step):
        for copy in stores(step):
            copy.wait()


def extract_heads(first_head, off2_ref, off3_ref, q_ref, k_ref, v_ref, g_ref, send_ref, cov_ref, low_ref, left_ref):
    cells = [(i, t) for i in range(EXTRACT_HEADS) for t in range(2)]

    def block(ref, cell):
        i, t = cell
        return ref[t * MID : (t + 1) * MID, :, :, i * WIDTH : (i + 1) * WIDTH].reshape(SEG1, WIDTH)

    def pick(cell):
        i, t = cell
        off_two, off_three = off2_ref[first_head + i], off3_ref[first_head + i]
        lane = slice(i * WIDTH, (i + 1) * WIDTH)
        refs = (q_ref, k_ref, v_ref, g_ref)
        slabs = [ref[t * MID : (t + 1) * MID, off_two // HALF, :, lane].reshape(MID * HALF, WIDTH) for ref in refs]
        place = t * MID + off_three // DILATION_TWO
        others = [ref[place, (off_three % DILATION_TWO) // HALF, :, lane] for ref in refs]
        select = iota((MID, MID * HALF), 1) == HALF * iota((MID, 1), 0) + off_two % HALF
        select_far = (iota((MID, HALF), 1) == off_three % HALF) & (iota((MID, HALF), 0) == 0)
        return jnp.concatenate(
            [
                dot_nn(select.astype(BF16), jnp.concatenate(slabs, 1)),
                dot_nn(select_far.astype(BF16), jnp.concatenate(others, 1)),
            ],
            0,
        )

    valids = []
    row = iota((COV, 1), 0)
    for i in range(EXTRACT_HEADS):
        twice = (off3_ref[first_head + i] % DILATION_TWO) == off2_ref[first_head + i]
        valids.append(((row < MID) | ((row == MID) & jnp.logical_not(twice))).astype(F32))
    picked = [pick(cell) for cell in cells]
    low = [x.astype(BF16) for x in picked]
    scores = [dot_nt(x[:, :WIDTH], block(k_ref, cell)) for x, cell in zip(low, cells)]
    grads = [dot_nt(x[:, 3 * WIDTH :], block(v_ref, cell)) for x, cell in zip(low, cells)]
    scores, grads = jnp.concatenate(scores, 0) * FACTOR, jnp.concatenate(grads, 0)
    top = jnp.max(scores, axis=1, keepdims=True)
    weight = jnp.exp(scores - top)
    total = jnp.sum(weight, axis=1, keepdims=True)
    weight_low = weight.astype(BF16)
    out = jnp.concatenate(
        [dot_nn(weight_low[n * COV : (n + 1) * COV], block(v_ref, cell)) for n, cell in enumerate(cells)], 0
    ) / total
    lse = top + jnp.log(total)
    g_cov = jnp.concatenate([x[:, 3 * WIDTH :] for x in picked], 0)
    delta = jnp.sum(g_cov * out, axis=1, keepdims=True)
    stats = lanes(split3(lse) + split3(delta), COV * len(cells))
    shown = lanes([lse, delta], COV * len(cells))
    prob = weight * (jnp.concatenate([valids[i] for i, _ in cells], 0) / total)
    dscore = (prob * (grads - delta)).astype(BF16)
    prob = prob.astype(BF16)
    first = iota((MID, 1), 0) == 0
    for n, (i, t) in enumerate(cells):
        rows = slice(n * COV, (n + 1) * COV)
        own = stats[rows]
        for c in range(2):
            send_ref[2 * i + c, t * MID : (t + 1) * MID, :] = low[n][:MID, WIDTH : 2 * WIDTH]
            send_ref[2 * i + c, 2 * MID + t * MID : 2 * MID + (t + 1) * MID, :] = low[n][:MID, 2 * WIDTH : 3 * WIDTH]
        send_ref[2 * i + t, 4 * MID : 5 * MID, :] = low[n][:MID, :WIDTH]
        send_ref[2 * i + t, 5 * MID : 6 * MID, :] = low[n][:MID, 3 * WIDTH :]
        send_ref[2 * i + t, 6 * MID : 7 * MID, :] = own[:MID].astype(BF16)
        mine = (picked[n][MID:, :WIDTH], picked[n][MID:, 3 * WIDTH :], jnp.where(first, own[MID:], 0.0))
        pair = [picked[n - t + u][MID:, at * WIDTH : (at + 1) * WIDTH] for at in (1, 2) for u in range(2)]
        far_block = pair[0]
        for at, x in enumerate((*pair[1:], *mine)):
            far_block = far_block + pltpu.roll(x, at + 1, 0)
        send_ref[2 * i + t, 7 * MID :, :] = far_block.astype(BF16)
        both = dot_nn(jnp.concatenate([dscore[rows], prob[rows]], 0), block(k_ref, (i, t)))
        for at, x in enumerate((out[rows], both[:COV], both[COV:], shown[rows])):
            cov_ref[at, i, t] = x
        low_ref[0, i, t] = low[n][:, :WIDTH]
        low_ref[1, i, t] = low[n][:, 3 * WIDTH :]
    for i in range(EXTRACT_HEADS):
        parts = [x[n * COV : (n + 1) * COV] for n in (2 * i, 2 * i + 1) for x in (dscore, prob)]
        left_ref[i] = jnp.concatenate(parts, 0).T


def extract(offsets, q, k, v, g):
    smem, hbm = pl.BlockSpec(memory_space=pltpu.SMEM), pl.BlockSpec(memory_space=pl.ANY)
    steps = HEADS // EXTRACT_HEADS
    period = (2 * MID, 2, HALF)
    shapes = [
        ((2 * HEADS, PACK, WIDTH), BF16),
        ((4, HEADS, 2, COV, WIDTH), F32),
        ((2, HEADS, 2, COV, WIDTH), BF16),
        ((HEADS, SEG1, 4 * COV), BF16),
    ]
    return pl.pallas_call(
        extract_kernel,
        in_specs=[smem, smem] + [hbm] * 4,
        out_specs=[hbm] * 4,
        out_shape=[pltpu.HBM(*x) for x in shapes],
        scratch_shapes=[pltpu.VMEM((steps, *period, EXTRACT_HEADS * WIDTH), BF16)] * 4
        + [pltpu.VMEM(*x) for x in shapes]
        + [pltpu.SemaphoreType.DMA((steps, 4))] * 2,
        compiler_params=pltpu.CompilerParams(vmem_limit_bytes=63 * 2**20),
        cost_estimate=pl.CostEstimate(flops=2**32, bytes_accessed=12 * 2**20, transcendentals=2**18),
        name="extract",
    )(*offsets, *in_hbm([x.reshape(*period, HEADS * WIDTH) for x in (q, k, v, g)]))


def local_kernel(first, count, kept, off2_ref, off3_ref, *refs):
    sources, outs = refs[:4], refs[4 + kept : 8 + kept]
    held, done, (in_sems, out_sems) = refs[8 + kept : 12 + kept], refs[12 + kept : 16 + kept], refs[16 + kept :]
    position = iota((1, SEG1), 1)

    def place(c):
        head, t = (first + c) // 2, (first + c) % 2
        return head, t, pl.ds(pl.multiple_of(head * WIDTH, WIDTH), WIDTH), pl.ds(pl.multiple_of(t * SEG1, SEG1), SEG1)

    def loads(c):
        _, _, lane, rows = place(c)
        return [
            pltpu.make_async_copy(sources[at].at[rows, lane], held[at].at[c], in_sems.at[c, at]) for at in range(4)
        ]

    def stores(c):
        head, t, lane, rows = place(c)
        return [
            pltpu.make_async_copy(
                done[at].at[c], outs[at].at[t, :, :, :, lane] if at < 2 else outs[at].at[head, rows], out_sems.at[c, at]
            )
            for at in range(4)
        ]

    def start(c):
        for copy in loads(c):
            copy.start()

    start(0)
    start(1)

    @pl.loop(0, count)
    def _(c):
        @pl.when(c + 2 < count)
        def _():
            start(c + 2)

        head = (first + c) // 2
        covered = ((position & (DILATION_TWO - 1)) == off2_ref[head]) | (position == off3_ref[head])
        for copy in loads(c):
            copy.wait()
        q, k, v, g = (ref[c] for ref in held)
        scores = dot_nt(k, q) * (FACTOR * math.log2(math.e))
        grad = dot_nt(v, g)
        weight = jnp.exp2(scores - jnp.max(scores, axis=0, keepdims=True))
        inverse = 1.0 / jnp.sum(weight, axis=0, keepdims=True)
        att = (dot_nn(v.T, weight.astype(BF16)) * inverse).astype(BF16)
        delta = jnp.sum(g.T.astype(F32) * att.astype(F32), axis=0, keepdims=True)
        out = stores(c)
        done[0][c] = att.T.reshape(MID, 2, HALF, WIDTH)
        out[0].start()
        prob = weight * jnp.where(covered, 0.0, inverse)
        dscore = (prob * (grad - delta)).astype(BF16)
        done[1][c] = (dot_nn(k.T, dscore) * FACTOR).astype(BF16).T.reshape(MID, 2, HALF, WIDTH)
        out[1].start()
        done[2][c] = dot_nn(dscore, q).astype(BF16)
        out[2].start()
        done[3][c] = dot_nn(prob.astype(BF16), g).astype(BF16)
        out[3].start()

    @pl.loop(0, count)
    def _(c):
        for copy in stores(c):
            copy.wait()


def local(offsets, arrays, first, count, earlier):
    smem, hbm = pl.BlockSpec(memory_space=pltpu.SMEM), pl.BlockSpec(memory_space=pl.ANY)
    share = count / (2 * HEADS)
    period = (MID, 2, HALF)
    return pl.pallas_call(
        lambda *refs: local_kernel(first, count, len(earlier), *refs),
        in_specs=[smem, smem] + [hbm] * (4 + len(earlier)),
        out_specs=[hbm] * 4,
        out_shape=[pltpu.HBM((2, *period, HEADS * WIDTH), BF16)] * 2 + [pltpu.HBM((HEADS, 2 * SEG1, WIDTH), BF16)] * 2,
        input_output_aliases={6 + at: at for at in range(len(earlier))},
        scratch_shapes=[pltpu.VMEM((count, SEG1, WIDTH), BF16)] * 4
        + [pltpu.VMEM((count, *period, WIDTH), BF16)] * 2
        + [pltpu.VMEM((count, SEG1, WIDTH), BF16)] * 2
        + [pltpu.SemaphoreType.DMA((count, 4))] * 2,
        compiler_params=pltpu.CompilerParams(vmem_limit_bytes=VMEM),
        cost_estimate=pl.CostEstimate(
            flops=int(share * 12 * 2**30), bytes_accessed=int(share * 16 * 2**20), transcendentals=int(share * 2**22)
        ),
        name="local",
    )(*offsets, *in_hbm((*arrays, *earlier)))


def merge_lse(parts):
    top = parts[0]
    for part in parts[1:]:
        top = jnp.maximum(top, part)
    total = jnp.exp(parts[0] - top)
    for part in parts[1:]:
        total = total + jnp.exp(part - top)
    return top + jnp.log(total)


def part(ref, at, rows):
    return ref[:, at * MID : at * MID + rows, :].reshape(ref.shape[0] * rows, WIDTH)


def far_places(shape, dim, starts):
    j = iota(shape, dim)
    n = shape[dim] // 7
    place = jnp.zeros(shape, jnp.int32)
    for at, start in enumerate(starts):
        if at < 2:
            u = j - 2 * n * at
            place = jnp.where((u >= 0) & (u < 2 * n), MID * (u // 2) + u % 2 + start, place)
        else:
            u = j - n * (at + 2)
            place = jnp.where((u >= 0) & (u < n), MID * u + start, place)
    return place


def forward_kernel(off2_ref, off3_ref, in_ref, far_ref, out_ref, figures_ref):
    head = lax.axis_index("inner") // 2
    off_three = off3_ref[head]
    n = in_ref.shape[0]
    k, v, q, g = part(in_ref, 0, 2 * MID), part(in_ref, 2, 2 * MID), part(in_ref, 4, MID), part(in_ref, 5, MID)
    queries = n * MID
    scores = dot_nt(q, k) * FACTOR
    top = jnp.max(scores, axis=1, keepdims=True)
    weight = jnp.exp(scores - top)
    total = jnp.sum(weight, axis=1, keepdims=True)
    out = dot_nn(weight.astype(BF16), v) / total
    lse = jnp.broadcast_to(top + jnp.log(total), (queries, WIDTH))
    delta = jnp.broadcast_to(jnp.sum(g.astype(F32) * out, axis=1, keepdims=True), (queries, WIDTH))
    out_ref[...] = out.astype(BF16)
    figures_ref[...] = lanes([lse, delta], queries)
    pick = (iota((7 * n, queries), 1) == far_places((7 * n, 1), 0, (0, 2, 4, 5, 6))).astype(BF16)
    picked = dot_nn(pick, part(in_ref, 7, MID))
    stats = picked[6 * n :]
    same = ((off_three % DILATION_TWO) == off2_ref[head]) & (
        iota((n, MID, WIDTH), 1) == off_three // DILATION_TWO
    )
    lse1, delta1 = join3(stats, 0), join3(stats, 3)
    lse2 = jnp.max(jnp.where(same, lse.reshape(n, MID, WIDTH), NEG), axis=1)
    delta2 = jnp.sum(jnp.where(same, delta.reshape(n, MID, WIDTH), 0.0), axis=1)
    both = merge_lse([lse1, lse2])
    delta = jnp.exp(lse1 - both) * delta1 + jnp.exp(lse2 - both) * delta2
    rows = jnp.concatenate([picked[: 6 * n], lanes(split3(both) + split3(delta), n)], 0).astype(BF16)
    for o in range(far_ref.shape[0]):
        far_ref[o] = rows


def backward_kernel(off2_ref, off3_ref, in_ref, far_ref, out2_ref, figures_ref, out_ref, key_ref, query_ref):
    head, outer = lax.axis_index("inner") // 2, lax.axis_index("outer")
    off_three = off3_ref[head]
    n = in_ref.shape[0]
    queries = n * MID
    turn = (iota((8, WIDTH), 0) == iota((8, WIDTH), 1)).astype(BF16)
    kf, vf = part(far_ref, 0, 2 * MID), part(far_ref, 2, 2 * MID)
    qf, gf = part(far_ref, 4, MID), part(far_ref, 5, MID)
    figures = dot_nt(turn, part(far_ref, 6, MID))
    lse12 = figures[0:1] + figures[1:2] + figures[2:3]
    delta12 = figures[3:4] + figures[4:5] + figures[5:6]
    scores = dot_nt(kf, qf) * FACTOR
    grads = dot_nt(vf, gf)
    top = jnp.max(scores, axis=0, keepdims=True)
    weight = jnp.exp(scores - top)
    total = jnp.sum(weight, axis=0, keepdims=True)
    lse3 = top + jnp.log(total)
    share = weight / total
    delta3 = jnp.sum(share * grads, axis=0, keepdims=True)
    lse = merge_lse([lse12, lse3])
    delta = jnp.exp(lse12 - lse) * delta12 + jnp.exp(lse3 - lse) * delta3
    prob = jnp.exp(scores - lse)
    dscore = (prob * (grads - delta)).astype(BF16)
    key_ref[0] = dot_nn(dscore, qf)
    key_ref[1] = dot_nn(prob.astype(BF16), gf)
    query_ref[0] = dot_tn(dscore, kf)
    query_ref[1] = dot_tn(share.astype(BF16), vf)
    eight = iota((8, lse3.shape[1]), 0)
    figures = jnp.zeros(eight.shape, F32)
    for at, x in enumerate(split3(lse3) + split3(delta3)):
        figures = jnp.where(eight == at, x, figures)
    query_ref[2] = dot_tn(figures.astype(BF16), turn)
    own_keys = pl.ds(pl.multiple_of(outer * 2 * n, 2 * n), 2 * n)
    own_queries = pl.ds(pl.multiple_of(outer * n, n), n)
    own = [key_ref[0, own_keys, :], key_ref[1, own_keys, :]] + [query_ref[at, own_queries, :] for at in range(3)]
    unpick = (iota((queries, 7 * n), 0) == far_places((1, 7 * n), 1, (3, 5, 0, 1, 2))).astype(BF16)
    packed = dot_nn(unpick, jnp.concatenate(own, 0).astype(BF16))
    same = ((off_three % DILATION_TWO) == off2_ref[head]) & (
        iota((n, MID, WIDTH), 1) == off_three // DILATION_TWO
    )

    def expand(column, other):
        wide = jnp.broadcast_to(jnp.broadcast_to(column, (n, WIDTH)).reshape(n, 1, WIDTH), (n, MID, WIDTH))
        return jnp.where(same, wide, other).reshape(queries, WIDTH)[:, 0:1]

    lse3, delta3 = expand(join3(own[4], 0), NEG), expand(join3(own[4], 3), 0.0)
    stats = part(in_ref, 6, MID).astype(F32)
    lse1, delta1 = join3(stats, 0), join3(stats, 3)
    lse2, delta2 = figures_ref[:, 0:1], figures_ref[:, 1:2]
    lse = merge_lse([lse1, lse2, lse3])
    delta = jnp.exp(lse1 - lse) * delta1 + jnp.exp(lse2 - lse) * delta2 + jnp.exp(lse3 - lse) * delta3
    k, v, q, g = part(in_ref, 0, 2 * MID), part(in_ref, 2, 2 * MID), part(in_ref, 4, MID), part(in_ref, 5, MID)
    prob = jnp.exp(dot_nt(q, k) * FACTOR - lse)
    dscore = (prob * (dot_nt(g, v) - delta)).astype(BF16)

    def give(at, rows, value):
        out_ref[:, at * MID : at * MID + rows, :] = value.astype(BF16).reshape(n, rows, WIDTH)

    give(0, 2 * MID, dot_tn(dscore, q))
    give(2, 2 * MID, dot_tn(prob.astype(BF16), g))
    give(4, MID, dot_nn(dscore, k))
    give(5, MID, out2_ref[...])
    give(6, MID, lanes(split3(lse2), queries))
    give(7, MID, packed)


def remote_call(kernel, offsets, arrays, shapes, scratch, name):
    vmem, smem = pl.BlockSpec(memory_space=pltpu.VMEM), pl.BlockSpec(memory_space=pltpu.SMEM)
    return pl.pallas_call(
        kernel,
        in_specs=[smem, smem] + [vmem] * len(arrays),
        out_specs=[vmem] * len(shapes),
        out_shape=shapes,
        scratch_shapes=[pltpu.VMEM(*x) for x in scratch],
        compiler_params=pltpu.CompilerParams(vmem_limit_bytes=VMEM),
        cost_estimate=pl.CostEstimate(flops=2**31, bytes_accessed=2**21, transcendentals=2**19),
        name=name,
    )(*offsets, *arrays)


def remote_forward(offsets, received, outer):
    n = received.shape[0]
    rows = n * MID
    return remote_call(
        forward_kernel, offsets, (received,),
        [jax.ShapeDtypeStruct((outer, 7 * n, WIDTH), BF16), jax.ShapeDtypeStruct((rows, WIDTH), BF16),
         jax.ShapeDtypeStruct((rows, WIDTH), F32)],
        [], "remote_forward",
    )


def remote_backward(offsets, received, far, out, figures):
    n, outer = received.shape[0], far.shape[0]
    return remote_call(
        backward_kernel, offsets, (received, far, out, figures), [jax.ShapeDtypeStruct(received.shape, BF16)],
        [((2, outer * 2 * n, WIDTH), F32), ((3, outer * n, WIDTH), F32)], "remote_backward",
    )[0]


def prepare(off2_ref, off3_ref, cov_ref, low_ref, back_ref, right_ref, rows_ref):
    cells, rows = 2 * HEADS, 2 * HEADS * COV
    back = back_ref[...].astype(F32)

    def pad(x):
        return jnp.concatenate([x, jnp.zeros((cells, COV - MID, WIDTH), F32)], 1).reshape(rows, WIDTH)

    def own(at):
        return pad(back[:, at * MID : (at + 1) * MID])

    def both(at):
        x = back[:, at * MID : (at + 2) * MID].reshape(HEADS, 2, COV, WIDTH)
        return pad((x[:, 0] + x[:, 1]).reshape(cells, MID, WIDTH))

    def spread(x):
        return jnp.broadcast_to(x.reshape(cells, 1, WIDTH), (cells, COV, WIDTH)).reshape(rows, WIDTH)

    row = iota((COV, WIDTH), 0)
    is_far = []
    for head in range(HEADS):
        off_three = off3_ref[head]
        twice = (off_three % DILATION_TWO) == off2_ref[head]
        is_far += [(row == jnp.where(twice, off_three // DILATION_TWO, MID)).astype(F32)] * 2
    is_far = jnp.concatenate(is_far, 0) > 0.0
    is_mid = jnp.concatenate([row] * cells, 0) < MID
    ones = (iota((WIDTH, WIDTH), 0) < 3).astype(BF16)

    def joined(x):
        return dot_nn(x.astype(BF16), ones)

    q, g = (low_ref[at].reshape(rows, WIDTH).astype(F32) for at in range(2))
    out, dq_one, dq_two, figures = (cov_ref[at].reshape(rows, WIDTH) for at in range(4))
    lse1, delta1 = figures[:, 0:1], figures[:, 1:2]
    packed = back[:, 7 * MID : 8 * MID]
    far = packed[:, 3:7].reshape(HEADS, 2, 4, WIDTH)
    far = (far[:, 0] + far[:, 1]).reshape(HEADS, 2, 2, WIDTH)
    lse2 = jnp.where(is_mid, joined(own(6)), NEG)
    lse3 = jnp.where(is_far, joined(spread(packed[:, 2:3])), NEG)
    lse = merge_lse([lse1, lse2, lse3])
    share = jnp.exp(lse1 - lse)
    att = (
        share * out + jnp.exp(lse2 - lse) * own(5) + jnp.exp(lse3 - lse) * spread(packed[:, 1:2])
    ).astype(BF16)
    delta = jnp.sum(g * att.astype(F32), axis=1, keepdims=True)
    change = share * (delta - delta1)
    dq = share * dq_one - change * dq_two + own(4) + jnp.where(is_far, spread(packed[:, 0:1]), 0.0)
    dk = both(0) + jnp.where(is_far, spread(far[:, 0]), 0.0)
    dv = both(2) + jnp.where(is_far, spread(far[:, 1]), 0.0)

    def column(at):
        return slice(at * WIDTH, (at + 1) * WIDTH)

    def put(at, to, x):
        x = x.astype(BF16).reshape(HEADS, 2, COV, WIDTH)
        for t in range(2):
            start = (2 * t + at) * COV
            right_ref[:, t, start : start + COV, column(to)] = x[:, t]

    def put_rows(to, x):
        high = x.astype(BF16)
        for at, part_ in enumerate((high, (x - high.astype(F32)).astype(BF16))):
            start = (4 + at) * COV
            right_ref[:, :, start : start + COV, column(to)] = part_.reshape(HEADS, 2, COV, WIDTH)

    rows_ref[0] = att.astype(F32).reshape(HEADS, 2, COV, WIDTH)
    rows_ref[1] = (FACTOR * dq).reshape(HEADS, 2, COV, WIDTH)
    nothing = jnp.zeros((HEADS, 2 * COV, 2 * WIDTH), BF16)
    right_ref[:, 0, 2 * COV : 4 * COV, :] = nothing
    right_ref[:, 1, : 2 * COV, :] = nothing
    put(0, 0, share * q)
    put(1, 0, -change * q)
    put_rows(0, dk)
    put(0, 1, jnp.zeros((rows, WIDTH), F32))
    put(1, 1, share * g)
    put_rows(1, dv)


def patch(off_two, off_three, rows_ref, head, at, slab_ref, other_ref, wide_ref):
    size = 2 * MID * HALF
    twice = (off_three % DILATION_TWO) == off_two
    beside = ((off_three % DILATION_TWO) // HALF) == (off_two // HALF)
    far = rows_ref[at, head, :, MID : MID + 1]
    wide_ref[at, :size, :] = slab_ref[at, head].astype(F32).reshape(size, WIDTH)
    wide_ref[at, pl.ds(off_two % HALF, 2 * MID, stride=HALF), :] = rows_ref[at, head, :, :MID].reshape(2 * MID, WIDTH)
    for t in range(2):
        spot = (t * MID + off_three // DILATION_TWO) * HALF + off_three % HALF
        spot = jnp.where(beside & jnp.logical_not(twice), spot, size)
        wide_ref[at, pl.ds(spot, 1), :] = far[t]
    slab_ref[at, head] = wide_ref[at, :size, :].astype(BF16).reshape(2, MID, HALF, WIDTH)
    there = (iota((2, HALF, WIDTH), 1) == off_three % HALF) & jnp.logical_not(beside)
    other_ref[at, head] = jnp.where(there, far, other_ref[at, head].astype(F32)).astype(BF16)


def finish_kernel(
    off2_ref, off3_ref, cov_hbm, low_hbm, back_ref, left_hbm, att_hbm, dq_hbm, dk_hbm, dv_hbm,
    att_out, dq_out, dk_out, dv_out,
    cov_ref, low_ref, left_ref, right_ref, rows_ref, held, done_ref, slab_ref, other_ref, wide_ref,
    first_sems, in_sems, out_sems, slab_in, slab_out,
):
    first = [
        pltpu.make_async_copy(source, target, first_sems.at[at])
        for at, (source, target) in enumerate(((cov_hbm, cov_ref), (low_hbm, low_ref)))
    ]

    def slabs(head, arrays):
        half, period = off2_ref[head] // HALF, off3_ref[head] // DILATION_TWO
        lane = pl.ds(pl.multiple_of(head * WIDTH, WIDTH), WIDTH)
        pairs = []
        for at, array in enumerate(arrays):
            pairs.append((array.at[:, :, half, :, lane], slab_ref.at[at, head]))
            pairs.append((array.at[:, period, 1 - half, :, lane], other_ref.at[at, head]))
        return pairs

    def loads(head):
        pairs = slabs(head, (att_hbm, dq_hbm))
        copies = [pltpu.make_async_copy(*pair, slab_in.at[head, at]) for at, pair in enumerate(pairs)]
        pairs = [(dk_hbm.at[head], held.at[0, head]), (dv_hbm.at[head], held.at[1, head])]
        pairs.append((left_hbm.at[head], left_ref.at[head]))
        return copies + [pltpu.make_async_copy(*pair, in_sems.at[head, at]) for at, pair in enumerate(pairs)]

    def slab_stores(head):
        pairs = slabs(head, (att_out, dq_out))
        return [
            pltpu.make_async_copy(source, target, slab_out.at[head, at]) for at, (target, source) in enumerate(pairs)
        ]

    def stores(head):
        lane = pl.ds(pl.multiple_of(head * WIDTH, WIDTH), WIDTH)
        return [
            pltpu.make_async_copy(done_ref.at[at, head], out.at[:, lane], out_sems.at[head, at])
            for at, out in enumerate((dk_out, dv_out))
        ]

    for copy in first:
        copy.start()

    @pl.loop(0, HEADS)
    def _(head):
        for copy in loads(head):
            copy.start()

    for copy in first:
        copy.wait()
    prepare(off2_ref, off3_ref, cov_ref, low_ref, back_ref, right_ref, rows_ref)

    @pl.loop(0, HEADS)
    def _(head):
        for copy in loads(head):
            copy.wait()
        for at in range(2):
            patch(off2_ref[head], off3_ref[head], rows_ref, head, at, slab_ref, other_ref, wide_ref)
        for copy in slab_stores(head):
            copy.start()
        off_two, off_three = off2_ref[head], off3_ref[head]
        place = targets((1, 2 * COV), 1, off_two, off_three)
        twice = (off_three % DILATION_TWO) == off_two
        place = jnp.where(((iota((1, 2 * COV), 1) % COV) == MID) & twice, -1, place)
        select = (iota((SEG1, 2 * COV), 0) == place).astype(BF16)
        left = jnp.concatenate([left_ref[head], select], 1)
        for t in range(2):
            rows = slice(t * SEG1, (t + 1) * SEG1)
            x = dot_nn(left, right_ref[head, t])
            done_ref[0, head, rows, :] = (FACTOR * (held[0, head, rows, :].astype(F32) + x[:, :WIDTH])).astype(BF16)
            done_ref[1, head, rows, :] = (held[1, head, rows, :].astype(F32) + x[:, WIDTH:]).astype(BF16)
        for copy in stores(head):
            copy.start()

    @pl.loop(0, HEADS)
    def _(head):
        for copy in slab_stores(head) + stores(head):
            copy.wait()


def finish(offsets, cov, low, left, back, att, dq, dk, dv):
    smem, hbm = pl.BlockSpec(memory_space=pltpu.SMEM), pl.BlockSpec(memory_space=pl.ANY)
    kind = (2, HEADS, 2 * SEG1, WIDTH)
    whole = (2 * SEG1, HEADS * WIDTH)
    att, dq, dk, dv = pl.pallas_call(
        finish_kernel,
        in_specs=[smem, smem, hbm, hbm, pl.BlockSpec(memory_space=pltpu.VMEM)] + [hbm] * 5,
        out_specs=[hbm] * 4,
        out_shape=[pltpu.HBM(att.shape, BF16)] * 2 + [pltpu.HBM(whole, BF16)] * 2,
        input_output_aliases={6: 0, 7: 1},
        scratch_shapes=[pltpu.VMEM(x.shape, x.dtype) for x in (cov, low, left)]
        + [
            pltpu.VMEM((HEADS, 2, 6 * COV, 2 * WIDTH), BF16),
            pltpu.VMEM((2, HEADS, 2, COV, WIDTH), F32),
            pltpu.VMEM(kind, BF16),
            pltpu.VMEM(kind, BF16),
            pltpu.VMEM((2, HEADS, 2, MID, HALF, WIDTH), BF16),
            pltpu.VMEM((2, HEADS, 2, HALF, WIDTH), BF16),
            pltpu.VMEM((2, 2 * MID * HALF + HALF, WIDTH), F32),
            pltpu.SemaphoreType.DMA((2,)),
            pltpu.SemaphoreType.DMA((HEADS, 3)),
            pltpu.SemaphoreType.DMA((HEADS, 2)),
            pltpu.SemaphoreType.DMA((HEADS, 4)),
            pltpu.SemaphoreType.DMA((HEADS, 4)),
        ],
        compiler_params=pltpu.CompilerParams(vmem_limit_bytes=VMEM),
        cost_estimate=pl.CostEstimate(flops=2**30, bytes_accessed=17 * 2**20, transcendentals=2**18),
        name="finish",
    )(*offsets, *in_hbm((cov, low)), back, *in_hbm((left, att, dq, dk, dv)))
    return att.reshape(whole), dq.reshape(whole), dk, dv


def solution(mesh):
    outer = mesh.shape["outer"]
    split = P(("outer", "inner"), None)

    def body(queries, keys, values, out_grad, middle_head_offsets, distant_head_offsets):
        offsets = (middle_head_offsets, distant_head_offsets)
        arrays = (queries, keys, values, out_grad)
        send, cov, low, left = extract(offsets, *arrays)
        got = lax.all_to_all(send, "inner", 0, 0)
        parts = local(offsets, arrays, 0, SHARES[0], ())
        got, *parts = lax.optimization_barrier((got, *parts))
        far, out, figures = remote_forward(offsets, got, outer)
        far, *parts = lax.optimization_barrier((far, *parts))
        far = lax.all_to_all(far, "outer", 0, 0)
        parts = local(offsets, arrays, SHARES[0], SHARES[1], parts)
        far, *parts = lax.optimization_barrier((far, *parts))
        back = remote_backward(offsets, got, far, out, figures)
        back, *parts = lax.optimization_barrier((back, *parts))
        back = lax.all_to_all(back, "inner", 0, 0)
        parts = local(offsets, arrays, SHARES[0] + SHARES[1], SHARES[2], parts)
        back, *parts = lax.optimization_barrier((back, *parts))
        return finish(offsets, cov, low, left, back, *parts)

    return jax.shard_map(
        body, mesh=mesh, in_specs=(split,) * 4 + (P(), P()), out_specs=(split,) * 4, check_vma=False
    )
```
